32 devices in a mesh: gx: 8 (over y, x, core), yz: 4 (over z).
Axes of the slice: x: 2, y: 2, z: 4, core: 2. Of those that a mesh axis runs over, the one named last changes fastest.
Arguments:
- volume: bfloat16 [64, 16, 32, 128], P('gx', None, 'yz'), may hold values from -6 to 6
- weight_one: bfloat16 [32, 432], replicated, may hold values from -0.875 to 0.875
- weight_two: bfloat16 [64, 864], replicated, may hold values from -0.625 to 0.625
- weight_three: bfloat16 [128, 1728], replicated, may hold values from -0.21875 to 0.21875
Outputs:
- features: bfloat16 [128, 16, 256], P('yz', 'gx')
The draws below stay inside these ranges and needn't reach their ends.
All inputs are finite; a program needn't handle non-finite values.
Results may differ from the reference program's by a relative error of at most 0.0053.
Values may be sent and summed in bfloat16 or wider, within the bound.
No kernel may reach another device: no remote copies, remote signals or barrier semaphores. Data moves between devices by JAX's collectives and lax.ppermute only.
A program may use at most 64 MiB of HBM per device.

```python
import jax
import jax.numpy as jnp
from jax import lax

C1 = 16
C2 = 32
C3 = 64
C4 = 128
NZ = 128
NX = 64
NY = 32


def block_scale(rng, dims, pieces, smallest, top_value):
    factor_of = 1.0
    for position, parts in pieces:
        heights = jax.random.uniform(jax.random.fold_in(jax.random.fold_in(rng, 6), position), (parts,), jnp.float32, smallest / len(pieces), top_value / len(pieces))
        factor_of = factor_of * jnp.repeat(jnp.exp(heights), dims[position] // parts).reshape((-1,) + (1,) * (len(dims) - 1 - position))
    return factor_of


def scatter_about(own_key, extent, spread, bound, cuts=(), kind=jnp.bfloat16):
    drawn = jax.random.normal(own_key, extent, jnp.float32) * spread
    if len(cuts) > 0:
        drawn = block_scale(own_key, extent, cuts, -0.22, 0.18) * drawn
    return jnp.clip(drawn, min=-bound, max=bound).astype(kind)


def setup_inputs(seed: int = 0) -> dict:
    key_of = jax.random.split(jax.random.key(seed), 5)
    return {
        "volume": scatter_about(key_of[0], (NX, C1, NY, NZ), 1.0, 6.0, ((0, 8), (2, 4))),
        "weight_one": scatter_about(key_of[1], (C2, 27 * C1), (27 * C1 // 8) ** -0.5, 0.875),
        "weight_two": scatter_about(key_of[2], (C3, 27 * C2), (27 * C2 // 8) ** -0.5, 0.625),
        "weight_three": scatter_about(key_of[3], (C4, 27 * C3), (27 * C3 // 2) ** -0.5, 0.21875),
    }


def plane_conv(planes, weight):
    height = planes.shape[2] - 2
    breadth = planes.shape[3] - 2
    shifted = [planes[a, :, b:b + height, c:c + breadth] for a in range(3) for b in range(3) for c in range(3)]
    patches = jnp.stack(shifted).reshape(27 * planes.shape[1], height * breadth)
    return jnp.dot(weight, patches, preferred_element_type=jnp.float32)


def conv_pool(padded, weight):
    out_planes = padded.shape[0] - 2
    height = padded.shape[2] - 2
    breadth = padded.shape[3] - 2

    def pair_step(plane_index):
        planes = lax.dynamic_slice_in_dim(padded, 2 * plane_index, 4, 0)
        lower_plane = jax.nn.relu(plane_conv(planes[0:3], weight))
        upper_plane = jax.nn.relu(plane_conv(planes[1:4], weight))
        summed = (lower_plane + upper_plane).reshape(weight.shape[0], height // 2, 2, breadth // 2, 2)
        return (jnp.sum(summed, axis=(2, 4)) * 0.125).astype(jnp.bfloat16)

    return lax.map(pair_step, jnp.arange(out_planes // 2, dtype=jnp.int32))


def conv_planes(padded, weight):
    out_planes = padded.shape[0] - 2

    def one_plane(plane_index):
        return plane_conv(lax.dynamic_slice_in_dim(padded, plane_index, 3, 0), weight)

    return lax.map(one_plane, jnp.arange(out_planes, dtype=jnp.int32))


def pad_all(block):
    return jnp.pad(block, ((1, 1), (0, 0), (1, 1), (1, 1)))


def reference(volume, weight_one, weight_two, weight_three):
    pooled_one = conv_pool(pad_all(volume), weight_one)
    pooled_two = conv_pool(pad_all(pooled_one), weight_two)
    result = jax.nn.relu(conv_planes(pad_all(pooled_two), weight_three))
    return jnp.moveaxis(result, 0, 1).astype(jnp.bfloat16)
```

```python
import functools

import jax
import jax.numpy as jnp
import numpy as np
from jax import lax
from jax.experimental import pallas as pl
from jax.experimental.pallas import tpu as pltpu
from jax.sharding import PartitionSpec as P

BF = jnp.bfloat16
F32 = jnp.float32
WHOLE = pl.BlockSpec(memory_space=pltpu.VMEM)
HALO = 3


def mat(a, b):
    return jnp.dot(a, b, preferred_element_type=F32)


def relu(a):
    return jnp.maximum(a, 0.0)


def iota(shape, dim):
    return lax.broadcasted_iota(jnp.int32, shape, dim)


def call(body, outs, *args, scratch=(), flops=0, name=None):
    moved = sum(a.size * a.dtype.itemsize for a in args)
    return pl.pallas_call(
        body,
        out_shape=[jax.ShapeDtypeStruct(s, d) for s, d in outs],
        in_specs=[WHOLE] * len(args),
        out_specs=[WHOLE] * len(outs),
        scratch_shapes=list(scratch),
        compiler_params=pltpu.CompilerParams(vmem_limit_bytes=40 * 1024 * 1024),
        cost_estimate=pl.CostEstimate(flops=flops, bytes_accessed=moved, transcendentals=0),
        name=name,
    )(*args)


def turn_kernel(vol, turned, send_a, send_b):
    planes, chans, height, breadth = vol.shape
    rows = chans * height
    dest = iota((rows, rows), 0)
    source = (dest & (chans - 1)) * height + dest // chans
    swap = (iota((rows, rows), 1) == source).astype(F32).astype(BF)
    even = lax.rem(lax.axis_index("yz"), 2) == 0
    edge = HALO * chans
    for x in range(planes):
        t = mat(swap, vol[x].reshape(rows, breadth)).astype(BF)
        turned[x] = t
        low, high = t[:edge], t[rows - edge :]
        send_a[x] = jnp.where(even, high, low)
        send_b[x] = jnp.where(even, low, high)


def yz_pairs(gx, yz, second):
    pairs = []
    for g in range(gx):
        for k in range(yz):
            if not second:
                pairs.append((g * yz + k, g * yz + (k ^ 1)))
            elif k in (0, yz - 1):
                pairs.append((g * yz + k, (g ^ 1) * yz + k))
            else:
                pairs.append((g * yz + k, g * yz + (k + 1 if k % 2 else k - 1)))
    return pairs


def ring(x, step):
    count = lax.axis_size("gx")
    return lax.ppermute(x, "gx", [(i, (i + step) % count) for i in range(count)])


def y_sides(got_a, got_b, x):
    k = lax.axis_index("yz")
    last = lax.axis_size("yz") - 1
    even = lax.rem(k, 2) == 0
    a, b = got_a[x], got_b[x]
    zero = jnp.zeros_like(a)
    low = jnp.where(k == 0, zero, jnp.where(even, b, a))
    high = jnp.where(k == last, zero, jnp.where(even, a, b))
    return low, high


def extend_kernel(turned, got_a, got_b, send_low, send_high):
    planes, rows, _ = turned.shape
    edge = got_a.shape[1]
    for out, first in ((send_low, 0), (send_high, planes - HALO)):
        for x in range(HALO):
            low, high = y_sides(got_a, got_b, first + x)
            out[x, :edge] = low
            out[x, edge : edge + rows] = turned[first + x]
            out[x, edge + rows :] = high


def weights_kernel(w1, w2, src1, src2, band1, band2, z_sel, p_sel):
    def spread(w, src, chans):
        sel = (iota((w.shape[1], src.shape[1]), 0) == src[...]).astype(F32).astype(BF)
        return mat(w[...], sel)

    for w, src, band, chans in ((w1, src1, band1, 16), (w2, src2, band2, 32)):
        base = spread(w, src, chans)
        out_rows, columns = base.shape
        wide = -(-columns // 128) * 128
        base = jnp.pad(base, ((0, 0), (0, wide - columns)))
        for y in range(4):
            moved = base if y == 0 else pltpu.roll(base, y * chans, 1)
            band[out_rows * y : out_rows * (y + 1)] = moved[:, :columns].astype(BF)

    rows, columns = z_sel.shape
    breadth = rows // 2
    r, c = iota(z_sel.shape, 0), iota(z_sel.shape, 1)
    tap = c // breadth
    within = c - tap * breadth
    same = (r // breadth) == (within // (breadth // 2))
    cell = (r & (breadth - 1)) // 2 == (within & (breadth // 2 - 1)) + tap - 1
    z_sel[...] = jnp.where(same & cell, 0.125, 0.0).astype(BF)

    rows, columns = p_sel.shape
    z = rows // 8
    r, c = iota(p_sel.shape, 0), iota(p_sel.shape, 1)
    hit = (r // (4 * z) == (c // (z // 2)) % 2) & ((r // (2 * z)) % 2 == c // z)
    hit = hit & ((r & (z - 1)) // 2 == (c & (z // 2 - 1)))
    p_sel[...] = jnp.where(hit, 0.125, 0.0).astype(BF)


def band_sources(chans):
    out = []
    for a in range(3):
        for c in range(3):
            for y in range(6):
                for i in range(chans):
                    out.append(((3 * a + y) * 3 + c) * chans + i if y < 3 else -1)
    return np.asarray(out, np.int32)[None]


def convs_kernel(turned, got_a, got_b, got_low, got_high, band1, band2, z_sel, p_sel, out, taps, pooled, taps2):
    planes, rows, breadth = turned.shape
    edge = got_a.shape[1]
    chans = edge // HALO
    window = 6 * chans
    lane = iota((1, breadth), 1)
    g, k = lax.axis_index("gx"), lax.axis_index("yz")
    g_last, k_last = lax.axis_size("gx") - 1, lax.axis_size("yz") - 1

    def put(e, t):
        wide = t.astype(F32)
        before = jnp.where(lane == 0, 0.0, pltpu.roll(wide, 1, 1)).astype(BF)
        after = jnp.where(lane == breadth - 1, 0.0, pltpu.roll(wide, breadth - 1, 1)).astype(BF)
        for tap, value in enumerate((before, t, after)):
            for part in range(3):
                first = part * 4 * chans
                taps[part, e, tap * window : (tap + 1) * window] = value[first : first + window]

    for x in range(HALO):
        t = got_low[x]
        put(x, jnp.where(g == 0, jnp.zeros_like(t), t))
        t = got_high[x]
        put(HALO + planes + x, jnp.where(g == g_last, jnp.zeros_like(t), t))
    for x in range(planes):
        low, high = y_sides(got_a, got_b, x)
        put(HALO + x, jnp.concatenate([low, turned[x], high], 0))

    pairs = pooled.shape[0]
    w1 = band1[...]
    width = w1.shape[0] // 4
    for j in range(pairs):
        for part in range(3):
            left = taps[part, 2 * j : 2 * j + 3].reshape(-1, breadth)
            right = taps[part, 2 * j + 1 : 2 * j + 4].reshape(-1, breadth)
            r = relu(mat(w1, jnp.concatenate([left, right], 1)))
            s = r[:, :breadth] + r[:, breadth:]
            lower = s[:width] + s[width : 2 * width]
            upper = s[2 * width : 3 * width] + s[3 * width :]
            if part == 0:
                lower = jnp.where(k == 0, 0.0, lower)
            if part == 2:
                upper = jnp.where(k == k_last, 0.0, upper)
            if j == 0:
                lower, upper = jnp.where(g == 0, 0.0, lower), jnp.where(g == 0, 0.0, upper)
            if j == pairs - 1:
                lower, upper = jnp.where(g == g_last, 0.0, lower), jnp.where(g == g_last, 0.0, upper)
            first = 2 * part * width
            pooled[j, first : first + width] = lower.astype(BF)
            pooled[j, first + width : first + 2 * width] = upper.astype(BF)

    window2 = pooled.shape[1]
    for j in range(pairs - 1):
        q = mat(jnp.concatenate([pooled[j], pooled[j + 1]], 1), z_sel[...]).astype(BF)
        for tap in range(3):
            taps2[j, tap * window2 : (tap + 1) * window2] = q[:, tap * breadth : (tap + 1) * breadth]
    left = taps2[0:3].reshape(-1, breadth)
    right = taps2[2:5].reshape(-1, breadth)
    r = relu(mat(band2[...], jnp.concatenate([left, right], 1)))
    width = r.shape[0] // 4
    lower = (r[:width] + r[width : 2 * width]).astype(BF)
    upper = (r[2 * width : 3 * width] + r[3 * width :]).astype(BF)
    out[...] = mat(jnp.concatenate([lower, upper], 1), p_sel[...]).astype(BF)


def lay_kernel(*refs):
    tiles, (low, high) = refs[:-2], refs[-2:]
    k = lax.axis_index("yz")
    even = lax.rem(k, 2) == 0
    half = tiles[0].shape[1] // 2
    lane = iota((1, 2 * half), 1)
    for m in range(len(tiles) // 2):
        a, b = tiles[2 * m][...].astype(F32), tiles[2 * m + 1][...].astype(F32)
        first, second = jnp.where(even, a, b), jnp.where(even, b, a)
        place = pl.ds(pl.multiple_of((lax.div(k, 2) ^ m) * 2 * half, 2 * half), 2 * half)
        low[:, place] = jnp.where(lane < half, first, pltpu.roll(second, half, 1)).astype(BF)
        high[:, place] = jnp.where(lane < half, pltpu.roll(first, half, 1), second).astype(BF)


def last_kernel(z, low, high, before, after, w3, out, taps):
    chans, cells = low.shape
    g = lax.axis_index("gx")
    g_last = lax.axis_size("gx") - 1
    lane = iota((1, cells), 1)
    depth = lane & (z - 1)
    for x, ref in enumerate((before, low, high, after)):
        t = ref[...].astype(F32)
        if x == 0:
            t = jnp.where(g == 0, 0.0, t)
        if x == 3:
            t = jnp.where(g == g_last, 0.0, t)
        for b in range(3):
            for c in range(3):
                step = (b - 1) * z + c - 1
                moved = t if step == 0 else pltpu.roll(t, (-step) % cells, 1)
                inside = (lane + step >= 0) & (lane + step < cells)
                inside = inside & (depth + (c - 1) >= 0) & (depth + (c - 1) < z)
                row = (3 * b + c) * chans
                taps[x, row : row + chans] = jnp.where(inside, moved, 0.0).astype(BF)
    w = w3[...]
    for x in range(2):
        acc = mat(w, taps[x : x + 3].reshape(-1, cells))
        out[:, x * cells : (x + 1) * cells] = relu(acc).astype(BF)


def per_device(volume, weight_one, weight_two, weight_three):
    gx, yz = lax.axis_size("gx"), lax.axis_size("yz")
    planes, chans, height, breadth = volume.shape
    rows = chans * height
    edge = HALO * chans
    c2, c3 = weight_one.shape[0], weight_two.shape[0]

    turned, send_a, send_b = call(
        turn_kernel,
        [((planes, rows, breadth), BF), ((planes, edge, breadth), BF), ((planes, edge, breadth), BF)],
        volume,
    )
    got_a = lax.ppermute(send_a, ("gx", "yz"), yz_pairs(gx, yz, False))
    got_b = lax.ppermute(send_b, ("gx", "yz"), yz_pairs(gx, yz, True))
    k1, k2 = 54 * chans, 54 * c2
    band1, band2, z_sel, p_sel = call(
        weights_kernel,
        [((4 * c2, k1), BF), ((4 * c3, k2), BF), ((2 * breadth, 3 * breadth), BF), ((4 * breadth, breadth), BF)],
        weight_one,
        weight_two,
        jnp.asarray(band_sources(chans)),
        jnp.asarray(band_sources(c2)),
        flops=2 * 64 * 864 * 1728,
    )
    ext = rows + 2 * edge
    send_low, send_high = call(
        extend_kernel, [((HALO, ext, breadth), BF), ((HALO, ext, breadth), BF)], turned, got_a, got_b
    )
    got_high = ring(send_low, -1)
    got_low = ring(send_high, 1)
    pairs = planes // 2 + 2
    (tile,) = call(
        convs_kernel,
        [((c3, breadth), BF)],
        turned,
        got_a,
        got_b,
        got_low,
        got_high,
        band1,
        band2,
        z_sel,
        p_sel,
        scratch=[
            pltpu.VMEM((3, planes + 2 * HALO, 18 * chans, breadth), BF),
            pltpu.VMEM((pairs, 6 * c2, breadth), BF),
            pltpu.VMEM((pairs - 1, 18 * c2, breadth), BF),
        ],
        flops=2 * 600_000_000,
    )
    tiles = [tile] + [lax.ppermute(tile, "yz", [(i, i ^ d) for i in range(yz)]) for d in range(1, yz)]
    cells = yz * (height // 4) * (breadth // 4)
    low, high = call(lay_kernel, [((c3, cells), BF), ((c3, cells), BF)], *tiles)
    after = ring(low, -1)
    before = ring(high, 1)
    out_rows = weight_three.shape[0] // yz
    picked = lax.dynamic_slice_in_dim(weight_three, lax.axis_index("yz") * out_rows, out_rows, 0)
    (out,) = call(
        functools.partial(last_kernel, breadth // 4),
        [((out_rows, 2 * cells), BF)],
        low,
        high,
        before,
        after,
        picked,
        scratch=[pltpu.VMEM((4, 9 * c3, cells), BF)],
        flops=2 * 32 * 1728 * 512,
    )
    return out.reshape(out_rows, 2, cells)


def solution(mesh):
    placed = (P("gx", None, "yz", None), P(), P(), P())
    return jax.shard_map(
        per_device, mesh=mesh, in_specs=placed, out_specs=P("yz", "gx", None), check_vma=False
    )
```

```python
import functools

import jax
import jax.numpy as jnp
from jax import lax
from jax.experimental import pallas as pl
from jax.experimental.pallas import tpu as pltpu
from jax.sharding import PartitionSpec as P

BF = jnp.bfloat16
F32 = jnp.float32
WHOLE = pl.BlockSpec(memory_space=pltpu.VMEM)
HALO = 3


def mat(a, b):
    return jnp.dot(a, b, preferred_element_type=F32)


def relu(a):
    return jnp.maximum(a, 0.0)


def iota(shape, dim):
    return lax.broadcasted_iota(jnp.int32, shape, dim)


def call(body, outs, *args, scratch=(), flops=0, space=pltpu.VMEM):
    moved = sum(a.size * a.dtype.itemsize for a in args)
    return pl.pallas_call(
        body,
        out_shape=[jax.ShapeDtypeStruct(s, d) for s, d in outs],
        in_specs=[pl.BlockSpec(memory_space=space)] * len(args),
        out_specs=[WHOLE] * len(outs),
        scratch_shapes=list(scratch),
        compiler_params=pltpu.CompilerParams(vmem_limit_bytes=40 * 1024 * 1024),
        cost_estimate=pl.CostEstimate(flops=flops, bytes_accessed=moved, transcendentals=0),
    )(*args)


def turn_kernel(vol, turned, send_a, send_b):
    planes, chans, height, breadth = vol.shape
    rows = chans * height
    dest = iota((rows, rows), 0)
    source = (dest & (chans - 1)) * height + dest // chans
    swap = (iota((rows, rows), 1) == source).astype(F32).astype(BF)
    even = lax.rem(lax.axis_index("yz"), 2) == 0
    edge = HALO * chans
    for x in range(planes):
        t = mat(swap, vol[x].reshape(rows, breadth)).astype(BF)
        turned[x] = t
        low, high = t[:edge], t[rows - edge :]
        send_a[x] = jnp.where(even, high, low)
        send_b[x] = jnp.where(even, low, high)


def yz_pairs(gx, yz, second):
    pairs = []
    for g in range(gx):
        for k in range(yz):
            if not second:
                pairs.append((g * yz + k, g * yz + (k ^ 1)))
            elif k in (0, yz - 1):
                pairs.append((g * yz + k, (g ^ 1) * yz + k))
            else:
                pairs.append((g * yz + k, g * yz + (k + 1 if k % 2 else k - 1)))
    return pairs


def gx_pairs(gx, yz, far):
    pairs = []
    for g in range(gx):
        for k in range(yz):
            if not far:
                pairs.append((g * yz + k, (g ^ 1) * yz + k))
            elif g in (0, gx - 1):
                pairs.append((g * yz + k, g * yz + (k ^ 1)))
            else:
                pairs.append((g * yz + k, (g + 1 if g % 2 else g - 1) * yz + k))
    return pairs


def is_even(axis):
    return lax.rem(lax.axis_index(axis), 2) == 0


def y_sides(got_a, got_b, x):
    k = lax.axis_index("yz")
    last = lax.axis_size("yz") - 1
    even = lax.rem(k, 2) == 0
    a, b = got_a[x], got_b[x]
    zero = jnp.zeros_like(a)
    low = jnp.where(k == 0, zero, jnp.where(even, b, a))
    high = jnp.where(k == last, zero, jnp.where(even, a, b))
    return low, high


def extend_kernel(turned, got_a, got_b, _, send_mate, send_far):
    planes, rows, _ = turned.shape
    edge = got_a.shape[1]
    even = is_even("gx")
    for out, first in (
        (send_mate, jnp.where(even, planes - HALO, 0)),
        (send_far, jnp.where(even, 0, planes - HALO)),
    ):
        for x in range(HALO):
            low, high = y_sides(got_a, got_b, first + x)
            out[x, :edge] = low
            out[x, edge : edge + rows] = turned[first + x]
            out[x, edge + rows :] = high


def weights_kernel(w1_hbm, w2_hbm, band1, band1_last, band2, z_sel, p_sel, w1, w2, sems):
    loads = [pltpu.make_async_copy(a, b, sems.at[i]) for i, (a, b) in enumerate(((w1_hbm, w1), (w2_hbm, w2)))]
    for load in loads:
        load.start()

    rows, columns = z_sel.shape
    breadth = rows // 2
    r, c = iota(z_sel.shape, 0), iota(z_sel.shape, 1)
    tap = c // breadth
    within = c - tap * breadth
    same = (r // breadth) == (within // (breadth // 2))
    cell = (r & (breadth - 1)) == 2 * ((within & (breadth // 2 - 1)) + tap - 1)
    z_sel[...] = jnp.where(same & cell, 1.0, 0.0).astype(BF)

    rows, columns = p_sel.shape
    z = rows // 8
    r, c = iota(p_sel.shape, 0), iota(p_sel.shape, 1)
    hit = (r // (4 * z) == (c // (z // 2)) % 2) & ((r // z) % 4 == 2 * (c // z))
    hit = hit & ((r & (z - 1)) == 2 * (c & (z // 2 - 1)))
    p_sel[...] = jnp.where(hit, 1.0, 0.0).astype(BF)

    for load in loads:
        load.wait()
    for w, band, last in ((w1, band1, band1_last), (w2, band2, None)):
        out_rows, columns = w.shape[0], band.shape[1]
        chans = w.shape[1] // 27
        col = iota((1, columns), 1)
        block = col // chans
        row, group = block % 6, block // 6
        source = ((group // 3 * 3 + row) * 3 + group % 3) * chans + col % chans
        source = jnp.where(row < 3, source, -1)
        sel = (iota((w.shape[1], columns), 0) == source).astype(F32).astype(BF)
        base = mat(w[...], sel)
        wide = -(-columns // 128) * 128
        base = jnp.pad(base, ((0, 0), (0, wide - columns)))
        for y in range(4):
            moved = base if y == 0 else pltpu.roll(base, y * chans, 1)
            rows = slice(out_rows * y, out_rows * (y + 1))
            band[rows] = moved[:, :columns].astype(BF)
            if last is not None:
                last[rows] = moved[:, columns // 3 * 2 : columns].astype(BF)


def put_taps(dest, t, chans):
    breadth = t.shape[1]
    window = 6 * chans
    lane = iota((1, breadth), 1)
    wide = t.astype(F32)
    before = jnp.where(lane == 0, 0.0, pltpu.roll(wide, 1, 1)).astype(BF)
    after = jnp.where(lane == breadth - 1, 0.0, pltpu.roll(wide, breadth - 1, 1)).astype(BF)
    for tap, value in enumerate((before, t, after)):
        for part in range(3):
            first = part * 4 * chans
            dest(part)[tap * window : (tap + 1) * window] = value[first : first + window]


def pool_first(acc, part, outside):
    k = lax.axis_index("yz")
    breadth = acc.shape[1] // 2
    width = acc.shape[0] // 4
    r = relu(acc)
    s = r[:, :breadth] + r[:, breadth:]
    halves = []
    for y in range(2):
        t = s[2 * y * width : (2 * y + 1) * width] + s[(2 * y + 1) * width : (2 * y + 2) * width]
        t = (t + pltpu.roll(t, breadth - 1, 1)) * 0.125
        drop = outside
        if part == 0 and y == 0:
            drop = drop | (k == 0)
        if part == 2 and y == 1:
            drop = drop | (k == lax.axis_size("yz") - 1)
        halves.append(jnp.where(drop, 0.0, t))
    return jnp.concatenate(halves, 0).astype(BF)


def inner_kernel(turned, got_a, got_b, band1, taps, pooled, partial):
    planes, rows, breadth = turned.shape
    chans = got_a.shape[1] // HALO
    for x in range(planes):
        low, high = y_sides(got_a, got_b, x)
        put_taps(lambda part: taps.at[part, x], jnp.concatenate([low, turned[x], high], 0), chans)
    w = band1[...]
    zero = jnp.zeros((taps.shape[2], breadth), BF)
    pairs = planes // 2
    for p in range(pairs):
        for part in range(3):
            if p == 0:
                left = jnp.concatenate([zero, taps[part, 0:2].reshape(-1, breadth)], 0)
            else:
                left = taps[part, 2 * p - 1 : 2 * p + 2].reshape(-1, breadth)
            if p == pairs - 1:
                right = jnp.concatenate([taps[part, planes - 2 : planes].reshape(-1, breadth), zero], 0)
            else:
                right = taps[part, 2 * p : 2 * p + 3].reshape(-1, breadth)
            acc = mat(w, jnp.concatenate([left, right], 1))
            if p == 0:
                partial[0, part] = acc
            elif p == pairs - 1:
                partial[1, part] = acc
            else:
                half = pooled.shape[1] // 3
                pooled[p - 1, part * half : (part + 1) * half] = pool_first(acc, part, False)


def outer_kernel(
    taps, pooled_in, partial, got_mate, got_far, band1, band1_last, band2, z_sel, p_sel, out, taps_low, taps_high, pooled, taps2
):
    _, planes, depth, breadth = taps.shape
    chans = depth // 18
    even = is_even("gx")
    g, g_last = lax.axis_index("gx"), lax.axis_size("gx") - 1
    for x in range(HALO):
        mate, far = got_mate[x], got_far[x]
        zero = jnp.zeros_like(mate)
        low = jnp.where(g == 0, zero, jnp.where(even, far, mate))
        high = jnp.where(g == g_last, zero, jnp.where(even, mate, far))
        put_taps(lambda part: taps_low.at[part, x], low, chans)
        put_taps(lambda part: taps_high.at[part, x], high, chans)

    pairs = pooled.shape[0]
    half = pooled.shape[1] // 3
    w = band1[...]
    for part in range(3):
        rows = slice(part * half, (part + 1) * half)
        left = taps_low[part].reshape(-1, breadth)
        right = jnp.concatenate([taps_low[part, 1:3].reshape(-1, breadth), taps[part, 0]], 0)
        pooled[0, rows] = pool_first(mat(w, jnp.concatenate([left, right], 1)), part, g == 0)
        left = jnp.concatenate([taps[part, planes - 1], taps_high[part, 0:2].reshape(-1, breadth)], 0)
        right = taps_high[part].reshape(-1, breadth)
        pooled[pairs - 1, rows] = pool_first(mat(w, jnp.concatenate([left, right], 1)), part, g == g_last)
        acc = partial[0, part]
        left = acc[:, :breadth] + mat(w[:, :depth], taps_low[part, 2])
        pooled[1, rows] = pool_first(jnp.concatenate([left, acc[:, breadth:]], 1), part, False)
        acc = partial[1, part]
        right = acc[:, breadth:] + mat(band1_last[...], taps_high[part, 0])
        pooled[pairs - 2, rows] = pool_first(jnp.concatenate([acc[:, :breadth], right], 1), part, False)
    for j in range(pairs - 4):
        pooled[2 + j] = pooled_in[j]

    window = pooled.shape[1]
    for j in range(pairs - 1):
        q = mat(jnp.concatenate([pooled[j], pooled[j + 1]], 1), z_sel[...]).astype(BF)
        for tap in range(3):
            taps2[j, tap * window : (tap + 1) * window] = q[:, tap * breadth : (tap + 1) * breadth]
    left = taps2[0:3].reshape(-1, breadth)
    right = taps2[2:5].reshape(-1, breadth)
    r = relu(mat(band2[...], jnp.concatenate([left, right], 1)))
    width = r.shape[0] // 4
    halves = []
    for y in range(2):
        t = r[2 * y * width : (2 * y + 1) * width] + r[(2 * y + 1) * width : (2 * y + 2) * width]
        t = t + pltpu.roll(t, 2 * breadth - breadth // 2, 1)
        t = (t + pltpu.roll(t, 2 * breadth - 1, 1)) * 0.125
        halves.append(t.astype(BF))
    out[...] = mat(jnp.concatenate(halves, 1), p_sel[...]).astype(BF)


def lay_kernel(*refs):
    tiles, (mate, far) = refs[:-2], refs[-2:]
    k = lax.axis_index("yz")
    even = is_even("yz")
    half = tiles[0].shape[1] // 2
    lane = iota((1, 2 * half), 1)
    for m in range(len(tiles) // 2):
        a, b = tiles[2 * m][...].astype(F32), tiles[2 * m + 1][...].astype(F32)
        first, second = jnp.where(even, a, b), jnp.where(even, b, a)
        place = pl.ds(pl.multiple_of((lax.div(k, 2) ^ m) * 2 * half, 2 * half), 2 * half)
        low = jnp.where(lane < half, first, pltpu.roll(second, half, 1))
        high = jnp.where(lane < half, pltpu.roll(first, half, 1), second)
        mate[:, place] = jnp.where(is_even("gx"), high, low).astype(BF)
        far[:, place] = jnp.where(is_even("gx"), low, high).astype(BF)


def plane_taps(dest, t, z):
    chans, cells = t.shape
    lane = iota((1, cells), 1)
    depth = lane & (z - 1)
    for b in range(3):
        for c in range(3):
            step = (b - 1) * z + c - 1
            moved = t if step == 0 else pltpu.roll(t, (-step) % cells, 1)
            inside = (lane + step >= 0) & (lane + step < cells)
            inside = inside & (depth + (c - 1) >= 0) & (depth + (c - 1) < z)
            row = (3 * b + c) * chans
            dest[row : row + chans] = jnp.where(inside, moved, 0.0).astype(BF)


def middle_kernel(z, mate, far, w3, partial, taps):
    chans, cells = mate.shape
    even = is_even("gx")
    a, b = mate[...].astype(F32), far[...].astype(F32)
    plane_taps(taps.at[0], jnp.where(even, b, a), z)
    plane_taps(taps.at[1], jnp.where(even, a, b), z)
    w = w3[...]
    depth = 9 * chans
    both = taps[...].reshape(2 * depth, cells)
    partial[0] = mat(w[:, depth:], both)
    partial[1] = mat(w[:, : 2 * depth], both)


def last_kernel(z, partial, got_mate, got_far, w3, out, taps):
    chans, cells = got_mate.shape
    g, g_last = lax.axis_index("gx"), lax.axis_size("gx") - 1
    even = is_even("gx")
    mate, far = got_mate[...].astype(F32), got_far[...].astype(F32)
    plane_taps(taps.at[0], jnp.where(g == 0, 0.0, jnp.where(even, far, mate)), z)
    plane_taps(taps.at[1], jnp.where(g == g_last, 0.0, jnp.where(even, mate, far)), z)
    w = w3[...]
    depth = 9 * chans
    first = relu(partial[0] + mat(w[:, :depth], taps[0]))
    second = relu(partial[1] + mat(w[:, 2 * depth :], taps[1]))
    out[...] = jnp.stack([first, second], 1).astype(BF)


def per_device(volume, weight_one, weight_two, weight_three):
    gx, yz = lax.axis_size("gx"), lax.axis_size("yz")
    planes, chans, height, breadth = volume.shape
    rows = chans * height
    edge = HALO * chans
    c2, c3 = weight_one.shape[0], weight_two.shape[0]

    turned, send_a, send_b = call(
        turn_kernel,
        [((planes, rows, breadth), BF), ((planes, edge, breadth), BF), ((planes, edge, breadth), BF)],
        volume,
    )
    got_b = lax.ppermute(send_b, ("gx", "yz"), yz_pairs(gx, yz, True))
    got_a = lax.ppermute(send_a, ("gx", "yz"), yz_pairs(gx, yz, False))
    k1, k2 = 54 * chans, 54 * c2
    band1, band1_last, band2, z_sel, p_sel = call(
        weights_kernel,
        [
            ((4 * c2, k1), BF),
            ((4 * c2, k1 // 3), BF),
            ((4 * c3, k2), BF),
            ((2 * breadth, 3 * breadth), BF),
            ((4 * breadth, breadth), BF),
        ],
        weight_one,
        weight_two,
        scratch=[
            pltpu.VMEM(weight_one.shape, BF),
            pltpu.VMEM(weight_two.shape, BF),
            pltpu.SemaphoreType.DMA((2,)),
        ],
        flops=2 * 64 * 864 * 1728,
        space=pltpu.HBM,
    )
    ext = rows + 2 * edge
    send_mate, send_far = call(
        extend_kernel,
        [((HALO, ext, breadth), BF), ((HALO, ext, breadth), BF)],
        turned,
        got_a,
        got_b,
        p_sel,
    )
    near, away = gx_pairs(gx, yz, False), gx_pairs(gx, yz, True)
    got_far = lax.ppermute(send_far, ("gx", "yz"), away)
    got_mate = lax.ppermute(send_mate, ("gx", "yz"), near)
    pairs = planes // 2 + 2
    taps, pooled, partial = call(
        inner_kernel,
        [
            ((3, planes, 18 * chans, breadth), BF),
            ((pairs - 4, 6 * c2, breadth), BF),
            ((2, 3, 4 * c2, 2 * breadth), F32),
        ],
        turned,
        got_a,
        got_b,
        band1,
        flops=2 * 300_000_000,
    )
    (tile,) = call(
        outer_kernel,
        [((c3, breadth), BF)],
        taps,
        pooled,
        partial,
        got_mate,
        got_far,
        band1,
        band1_last,
        band2,
        z_sel,
        p_sel,
        scratch=[
            pltpu.VMEM((3, HALO, 18 * chans, breadth), BF),
            pltpu.VMEM((3, HALO, 18 * chans, breadth), BF),
            pltpu.VMEM((pairs, 6 * c2, breadth), BF),
            pltpu.VMEM((pairs - 1, 18 * c2, breadth), BF),
        ],
        flops=2 * 400_000_000,
    )
    tiles = [tile] + [lax.ppermute(tile, "yz", [(i, i ^ d) for i in range(yz)]) for d in range(1, yz)]
    cells = yz * (height // 4) * (breadth // 4)
    z = breadth // 4
    mate, far = call(lay_kernel, [((c3, cells), BF), ((c3, cells), BF)], *tiles)
    got_far = lax.ppermute(far, ("gx", "yz"), away)
    got_mate = lax.ppermute(mate, ("gx", "yz"), near)
    out_rows = weight_three.shape[0] // yz
    picked = lax.dynamic_slice_in_dim(weight_three, lax.axis_index("yz") * out_rows, out_rows, 0)
    (partial,) = call(
        functools.partial(middle_kernel, z),
        [((2, out_rows, cells), F32)],
        mate,
        far,
        picked,
        scratch=[pltpu.VMEM((2, 9 * c3, cells), BF)],
        flops=2 * 32 * 1152 * 512,
    )
    (out,) = call(
        functools.partial(last_kernel, z),
        [((out_rows, 2, cells), BF)],
        partial,
        got_mate,
        got_far,
        picked,
        scratch=[pltpu.VMEM((2, 9 * c3, cells), BF)],
        flops=2 * 32 * 576 * 512,
    )
    return out


def solution(mesh):
    placed = (P("gx", None, "yz", None), P(), P(), P())
    return jax.shard_map(
        per_device, mesh=mesh, in_specs=placed, out_specs=P("yz", "gx", None), check_vma=False
    )
```

```python
import functools

import jax
import jax.numpy as jnp
from jax import lax
from jax.experimental import pallas as pl
from jax.experimental.pallas import tpu as pltpu
from jax.sharding import PartitionSpec as P

BF = jnp.bfloat16
F32 = jnp.float32
WHOLE = pl.BlockSpec(memory_space=pltpu.VMEM)
HALO = 3


def mat(a, b):
    return jnp.dot(a, b, preferred_element_type=F32)


def relu(a):
    return jnp.maximum(a, 0.0)


def iota(shape, dim):
    return lax.broadcasted_iota(jnp.int32, shape, dim)


def call(body, outs, *args, scratch=(), flops=0, hbm=()):
    moved = sum(a.size * a.dtype.itemsize for a in args)
    args = [pltpu.with_memory_space_constraint(a, pltpu.HBM) if i in hbm else a for i, a in enumerate(args)]
    return pl.pallas_call(
        body,
        out_shape=[jax.ShapeDtypeStruct(s, d) for s, d in outs],
        in_specs=[pl.BlockSpec(memory_space=pltpu.HBM if i in hbm else pltpu.VMEM) for i in range(len(args))],
        out_specs=[WHOLE] * len(outs),
        scratch_shapes=list(scratch),
        compiler_params=pltpu.CompilerParams(vmem_limit_bytes=40 * 1024 * 1024),
        cost_estimate=pl.CostEstimate(flops=flops, bytes_accessed=moved, transcendentals=0),
    )(*args)


def turn_kernel(vol, turned, send_a, send_b):
    planes, chans, height, breadth = vol.shape
    rows = chans * height
    dest = iota((rows, rows), 0)
    source = (dest & (chans - 1)) * height + dest // chans
    swap = (iota((rows, rows), 1) == source).astype(F32).astype(BF)
    even = lax.rem(lax.axis_index("yz"), 2) == 0
    edge = HALO * chans
    for x in range(planes):
        t = mat(swap, vol[x].reshape(rows, breadth)).astype(BF)
        turned[x] = t
        low, high = t[:edge], t[rows - edge :]
        send_a[x] = jnp.where(even, high, low)
        send_b[x] = jnp.where(even, low, high)


def yz_pairs(gx, yz, second):
    pairs = []
    for g in range(gx):
        for k in range(yz):
            if not second:
                pairs.append((g * yz + k, g * yz + (k ^ 1)))
            elif k in (0, yz - 1):
                pairs.append((g * yz + k, (g ^ 1) * yz + k))
            else:
                pairs.append((g * yz + k, g * yz + (k + 1 if k % 2 else k - 1)))
    return pairs


def gx_pairs(gx, yz, far):
    pairs = []
    for g in range(gx):
        for k in range(yz):
            if not far:
                pairs.append((g * yz + k, (g ^ 1) * yz + k))
            elif g in (0, gx - 1):
                pairs.append((g * yz + k, g * yz + (k ^ 1)))
            else:
                pairs.append((g * yz + k, (g + 1 if g % 2 else g - 1) * yz + k))
    return pairs


def is_even(axis):
    return lax.rem(lax.axis_index(axis), 2) == 0


def y_sides(got_a, got_b, x):
    k = lax.axis_index("yz")
    last = lax.axis_size("yz") - 1
    even = lax.rem(k, 2) == 0
    a, b = got_a[x], got_b[x]
    zero = jnp.zeros_like(a)
    low = jnp.where(k == 0, zero, jnp.where(even, b, a))
    high = jnp.where(k == last, zero, jnp.where(even, a, b))
    return low, high


def extend_kernel(turned, got_a, got_b, _, send_mate, send_far):
    planes, rows, _ = turned.shape
    edge = got_a.shape[1]
    even = is_even("gx")
    for out, first in (
        (send_mate, jnp.where(even, planes - HALO, 0)),
        (send_far, jnp.where(even, 0, planes - HALO)),
    ):
        for x in range(HALO):
            low, high = y_sides(got_a, got_b, first + x)
            out[x, :edge] = low
            out[x, edge : edge + rows] = turned[first + x]
            out[x, edge + rows :] = high


def weights_kernel(w1_hbm, w2_hbm, band1, band1_last, band2, z_sel, p_sel, w1, w2, sems):
    loads = [pltpu.make_async_copy(a, b, sems.at[i]) for i, (a, b) in enumerate(((w1_hbm, w1), (w2_hbm, w2)))]
    for load in loads:
        load.start()
    rows, columns = z_sel.shape
    breadth = rows // 2
    r, c = iota(z_sel.shape, 0), iota(z_sel.shape, 1)
    tap = c // breadth
    within = c - tap * breadth
    same = (r // breadth) == (within // (breadth // 2))
    cell = (r & (breadth - 1)) == 2 * ((within & (breadth // 2 - 1)) + tap - 1)
    z_sel[...] = jnp.where(same & cell, 1.0, 0.0).astype(BF)

    rows, columns = p_sel.shape
    z = rows // 8
    r, c = iota(p_sel.shape, 0), iota(p_sel.shape, 1)
    hit = (r // (4 * z) == (c // (z // 2)) % 2) & ((r // z) % 4 == 2 * (c // z))
    hit = hit & ((r & (z - 1)) == 2 * (c & (z // 2 - 1)))
    p_sel[...] = jnp.where(hit, 1.0, 0.0).astype(BF)

    for load in loads:
        load.wait()
    for w, band, last in ((w1, band1, band1_last), (w2, band2, None)):
        out_rows, columns = w.shape[0], band.shape[1]
        chans = w.shape[1] // 27
        col = iota((1, columns // 3), 1)
        block = col // chans
        row, tap = block % 6, block // 6
        source = jnp.where(row < 3, (row * 3 + tap) * chans + col % chans, -1)
        sel = (iota((9 * chans, columns // 3), 0) == source).astype(F32).astype(BF)
        taps = w[...]
        base = [mat(taps[:, a * 9 * chans : (a + 1) * 9 * chans], sel) for a in range(3)]
        wide = -(-columns // 128) * 128
        base = jnp.concatenate(base + [jnp.zeros((out_rows, wide - columns), F32)], 1)
        for y in range(4):
            moved = base if y == 0 else pltpu.roll(base, y * chans, 1)
            rows = slice(out_rows * y, out_rows * (y + 1))
            band[rows] = moved[:, :columns].astype(BF)
            if last is not None:
                last[rows] = moved[:, columns // 3 * 2 : columns].astype(BF)


def put_taps(dest, t, chans):
    breadth = t.shape[1]
    window = 6 * chans
    lane = iota((1, breadth), 1)
    wide = t.astype(F32)
    before = jnp.where(lane == 0, 0.0, pltpu.roll(wide, 1, 1)).astype(BF)
    after = jnp.where(lane == breadth - 1, 0.0, pltpu.roll(wide, breadth - 1, 1)).astype(BF)
    for tap, value in enumerate((before, t, after)):
        for part in range(3):
            first = part * 4 * chans
            dest(part)[tap * window : (tap + 1) * window] = value[first : first + window]


def pool_first(acc, part, outside):
    k = lax.axis_index("yz")
    breadth = acc.shape[1] // 2
    width = acc.shape[0] // 4
    r = relu(acc)
    s = r[:, :breadth] + r[:, breadth:]
    halves = []
    for y in range(2):
        t = s[2 * y * width : (2 * y + 1) * width] + s[(2 * y + 1) * width : (2 * y + 2) * width]
        t = (t + pltpu.roll(t, breadth - 1, 1)) * 0.125
        drop = outside
        if part == 0 and y == 0:
            drop = drop | (k == 0)
        if part == 2 and y == 1:
            drop = drop | (k == lax.axis_size("yz") - 1)
        halves.append(jnp.where(drop, 0.0, t))
    return jnp.concatenate(halves, 0).astype(BF)


def inner_kernel(turned, got_a, got_b, band1, w3_hbm, taps, pooled, partial, picked, w3, sem):
    load = pltpu.make_async_copy(w3_hbm, w3, sem)
    load.start()
    planes, rows, breadth = turned.shape
    chans = got_a.shape[1] // HALO
    for x in range(planes):
        low, high = y_sides(got_a, got_b, x)
        put_taps(lambda part: taps.at[part, x], jnp.concatenate([low, turned[x], high], 0), chans)
    w = band1[...]
    zero = jnp.zeros((taps.shape[2], breadth), BF)
    pairs = planes // 2
    for p in range(pairs):
        for part in range(3):
            if p == 0:
                left = jnp.concatenate([zero, taps[part, 0:2].reshape(-1, breadth)], 0)
            else:
                left = taps[part, 2 * p - 1 : 2 * p + 2].reshape(-1, breadth)
            if p == pairs - 1:
                right = jnp.concatenate([taps[part, planes - 2 : planes].reshape(-1, breadth), zero], 0)
            else:
                right = taps[part, 2 * p : 2 * p + 3].reshape(-1, breadth)
            acc = mat(w, jnp.concatenate([left, right], 1))
            if p == 0:
                partial[0, part] = acc
            elif p == pairs - 1:
                partial[1, part] = acc
            else:
                half = pooled.shape[1] // 3
                pooled[p - 1, part * half : (part + 1) * half] = pool_first(acc, part, False)
    load.wait()
    own = (picked.shape[0], w3.shape[1])
    first = lax.axis_index("yz") * own[0]
    pick = (iota(own, 1) == iota(own, 0) + first).astype(F32).astype(BF)
    picked[...] = lax.dot_general(pick, w3[...], (((1,), (1,)), ((), ())), preferred_element_type=F32).astype(BF)


def outer_kernel(
    taps, pooled_in, partial, got_mate, got_far, band1, band1_last, band2, z_sel, p_sel, out, taps_low, taps_high, pooled, taps2
):
    _, planes, depth, breadth = taps.shape
    chans = depth // 18
    even = is_even("gx")
    g, g_last = lax.axis_index("gx"), lax.axis_size("gx") - 1
    for x in range(HALO):
        mate, far = got_mate[x], got_far[x]
        zero = jnp.zeros_like(mate)
        low = jnp.where(g == 0, zero, jnp.where(even, far, mate))
        high = jnp.where(g == g_last, zero, jnp.where(even, mate, far))
        put_taps(lambda part: taps_low.at[part, x], low, chans)
        put_taps(lambda part: taps_high.at[part, x], high, chans)

    pairs = pooled.shape[0]
    half = pooled.shape[1] // 3
    w = band1[...]
    for part in range(3):
        rows = slice(part * half, (part + 1) * half)
        left = taps_low[part].reshape(-1, breadth)
        right = jnp.concatenate([taps_low[part, 1:3].reshape(-1, breadth), taps[part, 0]], 0)
        pooled[0, rows] = pool_first(mat(w, jnp.concatenate([left, right], 1)), part, g == 0)
        left = jnp.concatenate([taps[part, planes - 1], taps_high[part, 0:2].reshape(-1, breadth)], 0)
        right = taps_high[part].reshape(-1, breadth)
        pooled[pairs - 1, rows] = pool_first(mat(w, jnp.concatenate([left, right], 1)), part, g == g_last)
        acc = partial[0, part]
        left = acc[:, :breadth] + mat(w[:, :depth], taps_low[part, 2])
        pooled[1, rows] = pool_first(jnp.concatenate([left, acc[:, breadth:]], 1), part, False)
        acc = partial[1, part]
        right = acc[:, breadth:] + mat(band1_last[...], taps_high[part, 0])
        pooled[pairs - 2, rows] = pool_first(jnp.concatenate([acc[:, :breadth], right], 1), part, False)
    for j in range(pairs - 4):
        pooled[2 + j] = pooled_in[j]

    window = pooled.shape[1]
    for j in range(pairs - 1):
        q = mat(jnp.concatenate([pooled[j], pooled[j + 1]], 1), z_sel[...]).astype(BF)
        for tap in range(3):
            taps2[j, tap * window : (tap + 1) * window] = q[:, tap * breadth : (tap + 1) * breadth]
    left = taps2[0:3].reshape(-1, breadth)
    right = taps2[2:5].reshape(-1, breadth)
    r = relu(mat(band2[...], jnp.concatenate([left, right], 1)))
    width = r.shape[0] // 4
    halves = []
    for y in range(2):
        t = r[2 * y * width : (2 * y + 1) * width] + r[(2 * y + 1) * width : (2 * y + 2) * width]
        t = t + pltpu.roll(t, 2 * breadth - breadth // 2, 1)
        t = (t + pltpu.roll(t, 2 * breadth - 1, 1)) * 0.125
        halves.append(t.astype(BF))
    out[...] = mat(jnp.concatenate(halves, 1), p_sel[...]).astype(BF)


def lay_kernel(*refs):
    tiles, (mate, far) = refs[:-2], refs[-2:]
    k = lax.axis_index("yz")
    even = is_even("yz")
    half = tiles[0].shape[1] // 2
    lane = iota((1, 2 * half), 1)
    for m in range(len(tiles) // 2):
        a, b = tiles[2 * m][...].astype(F32), tiles[2 * m + 1][...].astype(F32)
        first, second = jnp.where(even, a, b), jnp.where(even, b, a)
        place = pl.ds(pl.multiple_of((lax.div(k, 2) ^ m) * 2 * half, 2 * half), 2 * half)
        low = jnp.where(lane < half, first, pltpu.roll(second, half, 1))
        high = jnp.where(lane < half, pltpu.roll(first, half, 1), second)
        mate[:, place] = jnp.where(is_even("gx"), high, low).astype(BF)
        far[:, place] = jnp.where(is_even("gx"), low, high).astype(BF)


def plane_taps(dest, t, z):
    chans, cells = t.shape
    lane = iota((1, cells), 1)
    depth = lane & (z - 1)
    for b in range(3):
        for c in range(3):
            step = (b - 1) * z + c - 1
            moved = t if step == 0 else pltpu.roll(t, (-step) % cells, 1)
            inside = (lane + step >= 0) & (lane + step < cells)
            inside = inside & (depth + (c - 1) >= 0) & (depth + (c - 1) < z)
            row = (3 * b + c) * chans
            dest[row : row + chans] = jnp.where(inside, moved, 0.0).astype(BF)


def middle_kernel(z, mate, far, w3, partial, taps):
    chans, cells = mate.shape
    even = is_even("gx")
    a, b = mate[...].astype(F32), far[...].astype(F32)
    plane_taps(taps.at[0], jnp.where(even, b, a), z)
    plane_taps(taps.at[1], jnp.where(even, a, b), z)
    w = w3[...]
    depth = 9 * chans
    both = taps[...].reshape(2 * depth, cells)
    partial[0] = mat(w[:, depth:], both)
    partial[1] = mat(w[:, : 2 * depth], both)


def last_kernel(z, partial, got_mate, got_far, w3, out, taps):
    chans, cells = got_mate.shape
    g, g_last = lax.axis_index("gx"), lax.axis_size("gx") - 1
    even = is_even("gx")
    mate, far = got_mate[...].astype(F32), got_far[...].astype(F32)
    plane_taps(taps.at[0], jnp.where(g == 0, 0.0, jnp.where(even, far, mate)), z)
    plane_taps(taps.at[1], jnp.where(g == g_last, 0.0, jnp.where(even, mate, far)), z)
    w = w3[...]
    depth = 9 * chans
    first = relu(partial[0] + mat(w[:, :depth], taps[0]))
    second = relu(partial[1] + mat(w[:, 2 * depth :], taps[1]))
    out[...] = jnp.stack([first, second], 1).astype(BF)


def per_device(volume, weight_one, weight_two, weight_three):
    gx, yz = lax.axis_size("gx"), lax.axis_size("yz")
    planes, chans, height, breadth = volume.shape
    rows = chans * height
    edge = HALO * chans
    c2, c3 = weight_one.shape[0], weight_two.shape[0]

    turned, send_a, send_b = call(
        turn_kernel,
        [((planes, rows, breadth), BF), ((planes, edge, breadth), BF), ((planes, edge, breadth), BF)],
        volume,
    )
    got_b = lax.ppermute(send_b, ("gx", "yz"), yz_pairs(gx, yz, True))
    got_a = lax.ppermute(send_a, ("gx", "yz"), yz_pairs(gx, yz, False))
    k1, k2 = 54 * chans, 54 * c2
    band1, band1_last, band2, z_sel, p_sel = call(
        weights_kernel,
        [
            ((4 * c2, k1), BF),
            ((4 * c2, k1 // 3), BF),
            ((4 * c3, k2), BF),
            ((2 * breadth, 3 * breadth), BF),
            ((4 * breadth, breadth), BF),
        ],
        weight_one,
        weight_two,
        scratch=[
            pltpu.VMEM(weight_one.shape, BF),
            pltpu.VMEM(weight_two.shape, BF),
            pltpu.SemaphoreType.DMA((2,)),
        ],
        hbm=(0, 1),
        flops=2 * 64 * 864 * 1728,
    )
    ext = rows + 2 * edge
    send_mate, send_far = call(
        extend_kernel,
        [((HALO, ext, breadth), BF), ((HALO, ext, breadth), BF)],
        turned,
        got_a,
        got_b,
        p_sel,
    )
    near, away = gx_pairs(gx, yz, False), gx_pairs(gx, yz, True)
    got_far = lax.ppermute(send_far, ("gx", "yz"), away)
    got_mate = lax.ppermute(send_mate, ("gx", "yz"), near)
    pairs = planes // 2 + 2
    out_rows = weight_three.shape[0] // yz
    taps, pooled, partial, picked = call(
        inner_kernel,
        [
            ((3, planes, 18 * chans, breadth), BF),
            ((pairs - 4, 6 * c2, breadth), BF),
            ((2, 3, 4 * c2, 2 * breadth), F32),
            ((out_rows, weight_three.shape[1]), BF),
        ],
        turned,
        got_a,
        got_b,
        band1,
        weight_three.T,
        scratch=[pltpu.VMEM(weight_three.shape[::-1], BF), pltpu.SemaphoreType.DMA],
        hbm=(4,),
        flops=2 * 300_000_000,
    )
    (tile,) = call(
        outer_kernel,
        [((c3, breadth), BF)],
        taps,
        pooled,
        partial,
        got_mate,
        got_far,
        band1,
        band1_last,
        band2,
        z_sel,
        p_sel,
        scratch=[
            pltpu.VMEM((3, HALO, 18 * chans, breadth), BF),
            pltpu.VMEM((3, HALO, 18 * chans, breadth), BF),
            pltpu.VMEM((pairs, 6 * c2, breadth), BF),
            pltpu.VMEM((pairs - 1, 18 * c2, breadth), BF),
        ],
        flops=2 * 400_000_000,
    )
    tiles = [tile] + [lax.ppermute(tile, "yz", [(i, i ^ d) for i in range(yz)]) for d in range(1, yz)]
    cells = yz * (height // 4) * (breadth // 4)
    z = breadth // 4
    mate, far = call(lay_kernel, [((c3, cells), BF), ((c3, cells), BF)], *tiles)
    got_far = lax.ppermute(far, ("gx", "yz"), away)
    got_mate = lax.ppermute(mate, ("gx", "yz"), near)
    (partial,) = call(
        functools.partial(middle_kernel, z),
        [((2, out_rows, cells), F32)],
        mate,
        far,
        picked,
        scratch=[pltpu.VMEM((2, 9 * c3, cells), BF)],
        flops=2 * 32 * 1152 * 512,
    )
    (out,) = call(
        functools.partial(last_kernel, z),
        [((out_rows, 2, cells), BF)],
        partial,
        got_mate,
        got_far,
        picked,
        scratch=[pltpu.VMEM((2, 9 * c3, cells), BF)],
        flops=2 * 32 * 576 * 512,
    )
    return out


def solution(mesh):
    placed = (P("gx", None, "yz", None), P(), P(), P())
    return jax.shard_map(
        per_device, mesh=mesh, in_specs=placed, out_specs=P("yz", "gx", None), check_vma=False
    )
```

```python
import functools

import jax
import jax.numpy as jnp
from jax import lax
from jax.experimental import pallas as pl
from jax.experimental.pallas import tpu as pltpu
from jax.sharding import PartitionSpec as P

BF = jnp.bfloat16
F32 = jnp.float32
WHOLE = pl.BlockSpec(memory_space=pltpu.VMEM)
PLANES = 2
HALO = 2 * PLANES - 1
EDGE = 3


def mat(a, b):
    return jnp.dot(a, b, preferred_element_type=F32)


def relu(a):
    return jnp.maximum(a, 0.0)


def iota(shape, dim):
    return lax.broadcasted_iota(jnp.int32, shape, dim)


def call(body, outs, *args, scratch=(), flops=0, hbm=()):
    moved = sum(a.size * a.dtype.itemsize for a in args)
    args = [pltpu.with_memory_space_constraint(a, pltpu.HBM) if i in hbm else a for i, a in enumerate(args)]
    return pl.pallas_call(
        body,
        out_shape=[jax.ShapeDtypeStruct(s, d) for s, d in outs],
        in_specs=[pl.BlockSpec(memory_space=pltpu.HBM if i in hbm else pltpu.VMEM) for i in range(len(args))],
        out_specs=[WHOLE] * len(outs),
        scratch_shapes=list(scratch),
        compiler_params=pltpu.CompilerParams(vmem_limit_bytes=40 * 1024 * 1024),
        cost_estimate=pl.CostEstimate(flops=flops, bytes_accessed=moved, transcendentals=0),
    )(*args)


def turn_kernel(vol, turned, send_mate, send_far):
    planes, chans, height, breadth = vol.shape
    rows = chans * height
    dest = iota((rows, rows), 0)
    source = (dest & (chans - 1)) * height + dest // chans
    swap = (iota((rows, rows), 1) == source).astype(F32).astype(BF)
    for x in range(planes):
        turned[x] = mat(swap, vol[x].reshape(rows, breadth)).astype(BF)
    even = is_even("gx")
    for out, first in (
        (send_mate, jnp.where(even, planes - HALO, 0)),
        (send_far, jnp.where(even, 0, planes - HALO)),
    ):
        for x in range(HALO):
            out[x] = turned[first + x]


def yz_pairs(gx, yz, second):
    pairs = []
    for g in range(gx):
        for k in range(yz):
            if not second:
                pairs.append((g * yz + k, g * yz + (k ^ 1)))
            elif k in (0, yz - 1):
                pairs.append((g * yz + k, (g ^ 1) * yz + k))
            else:
                pairs.append((g * yz + k, g * yz + (k + 1 if k % 2 else k - 1)))
    return pairs


def gx_pairs(gx, yz, far):
    pairs = []
    for g in range(gx):
        for k in range(yz):
            if not far:
                pairs.append((g * yz + k, (g ^ 1) * yz + k))
            elif g in (0, gx - 1):
                pairs.append((g * yz + k, g * yz + (k ^ 1)))
            else:
                pairs.append((g * yz + k, (g + 1 if g % 2 else g - 1) * yz + k))
    return pairs


def is_even(axis):
    return lax.rem(lax.axis_index(axis), 2) == 0


def from_sides(mate, far, even, no_low, no_high):
    zero = jnp.zeros_like(mate)
    low = jnp.where(no_low, zero, jnp.where(even, far, mate))
    high = jnp.where(no_high, zero, jnp.where(even, mate, far))
    return low, high


def all_planes(turned, got_mate, got_far):
    g = lax.axis_index("gx")
    even, first, last = is_even("gx"), g == 0, g == lax.axis_size("gx") - 1
    sides = [from_sides(got_mate[x], got_far[x], even, first, last) for x in range(HALO)]
    return [low for low, _ in sides] + [turned[x] for x in range(turned.shape[0])] + [high for _, high in sides]


def edge_kernel(turned, got_far, got_mate, _, send_a, send_b):
    edge = send_a.shape[1]
    even = is_even("yz")
    for x, t in enumerate(all_planes(turned, got_mate, got_far)):
        low, high = t[:edge], t[t.shape[0] - edge :]
        send_a[x] = jnp.where(even, high, low)
        send_b[x] = jnp.where(even, low, high)


def weights_kernel(w1_hbm, w2_hbm, lower1, upper1, middle2, outer2, z_sel, p_sel, w1, w2, sems):
    loads = [pltpu.make_async_copy(a, b, sems.at[i]) for i, (a, b) in enumerate(((w1_hbm, w1), (w2_hbm, w2)))]
    for load in loads:
        load.start()

    rows, columns = z_sel.shape
    breadth = rows // 2
    r, c = iota(z_sel.shape, 0), iota(z_sel.shape, 1)
    tap = c // breadth
    within = c - tap * breadth
    same = (r // breadth) == (within // (breadth // 2))
    cell = (r & (breadth - 1)) == 2 * ((within & (breadth // 2 - 1)) + tap - 1)
    z_sel[...] = jnp.where(same & cell, 1.0, 0.0).astype(BF)

    rows, columns = p_sel.shape
    z = rows // 8
    r, c = iota(p_sel.shape, 0), iota(p_sel.shape, 1)
    hit = (r // (4 * z) == (c // (z // 2)) % 2) & ((r // z) % 4 == 2 * (c // z))
    hit = hit & ((r & (z - 1)) == 2 * (c & (z // 2 - 1)))
    p_sel[...] = jnp.where(hit, 1.0, 0.0).astype(BF)

    for load in loads:
        load.wait()
    for w, bands in (
        (w1, ((lower1, lambda y: (0, 1, 2)), (upper1, lambda y: (3, 4, 5)))),
        (w2, ((middle2, lambda y: (2, 3)), (outer2, lambda y: (0, 1) if y < 2 else (4, 5)))),
    ):
        out_rows, width = w.shape[0], w.shape[1] // 9
        taps = w[...].astype(F32)
        zero = jnp.zeros((out_rows, width), F32)
        for band, window in bands:
            for y in range(4):
                pieces = []
                for a in range(3):
                    for row in window(y):
                        first = (3 * a + row - y) * width
                        pieces.append(taps[:, first : first + width] if 0 <= row - y < 3 else zero)
                band[out_rows * y : out_rows * (y + 1)] = jnp.concatenate(pieces, 1).astype(BF)


def put_taps(dest, t, chans):
    breadth = t.shape[1]
    lane = iota((1, breadth), 1)
    wide = t.astype(F32)
    before = jnp.where(lane == 0, 0.0, pltpu.roll(wide, 1, 1)).astype(BF)
    after = jnp.where(lane == breadth - 1, 0.0, pltpu.roll(wide, breadth - 1, 1)).astype(BF)
    for y in range(t.shape[0] // chans):
        for tap, value in enumerate((before, t, after)):
            row = (3 * y + tap) * chans
            dest[row : row + chans] = value[y * chans : (y + 1) * chans]


def three(taps, e, first, rows):
    return jnp.concatenate([taps[e + a, first : first + rows] for a in range(3)], 0)


def two_cells(taps, j, first, rows):
    return jnp.concatenate([three(taps, 2 * j, first, rows), three(taps, 2 * j + 1, first, rows)], 1)


def pool_first(acc, j, pairs, no_low, no_high):
    g = lax.axis_index("gx")
    breadth = acc.shape[1] // 2
    width = acc.shape[0] // 4
    r = relu(acc)
    s = r[:, :breadth] + r[:, breadth:]
    halves = []
    for y, drop in enumerate((no_low, no_high)):
        t = s[2 * y * width : (2 * y + 1) * width] + s[(2 * y + 1) * width : (2 * y + 2) * width]
        t = (t + pltpu.roll(t, breadth - 1, 1)) * 0.125
        if j < PLANES - 1:
            drop = drop | (g == 0)
        if j > pairs - PLANES:
            drop = drop | (g == lax.axis_size("gx") - 1)
        halves.append(t if drop is False else jnp.where(drop, 0.0, t))
    return jnp.concatenate(halves, 0).astype(BF)


def second_taps(pooled, z_sel):
    beside = [jnp.concatenate([a, b], 1) for a, b in zip(pooled[:-1], pooled[1:])]
    q = mat(jnp.concatenate(beside, 0), z_sel)
    breadth = q.shape[1] // 2
    before, here = q[:, :breadth], q[:, breadth:]
    lane = iota((1, breadth), 1)
    last = (lane & (breadth // 2 - 1)) == breadth // 2 - 1
    after = jnp.where(last, 0.0, pltpu.roll(here, breadth - 1, 1))
    taps = [t.astype(BF) for t in (before, here, after)]
    chans = pooled[0].shape[0] // 2
    planes = []
    for j in range(len(beside)):
        rows = [slice((2 * j + y) * chans, (2 * j + y + 1) * chans) for y in range(2)]
        planes.append([t[r] for r in rows for t in taps])
    columns = [jnp.concatenate(planes[j] + planes[j + 1] + planes[j + 2], 0) for j in range(0, len(planes) - 2, 2)]
    return jnp.concatenate(columns, 1)


def inner_kernel(
    turned, got_mate, got_far, lower1, upper1, middle2, z_sel, w3_hbm, partial1, partial2, picked, taps, w3, sem
):
    load = pltpu.make_async_copy(w3_hbm, w3, sem)
    load.start()
    chans = lower1.shape[1] // 27
    for e, t in enumerate(all_planes(turned, got_mate, got_far)):
        put_taps(taps.at[e], t, chans)
    pairs = partial1.shape[1]
    width = lower1.shape[0] // 4
    lower, upper = lower1[: 3 * width], upper1[width:]
    step = 3 * chans
    pooled = []
    zero = jnp.zeros((width, partial1.shape[3]), F32)
    for j in range(pairs):
        partial1[0, j, :width] = zero
        partial1[0, j, width:] = mat(upper, two_cells(taps, j, 0, 3 * step))
        partial1[1, j, : 3 * width] = mat(lower, two_cells(taps, j, 5 * step, 3 * step))
        partial1[1, j, 3 * width :] = zero
        a = mat(lower, two_cells(taps, j, step, 3 * step))
        b = mat(upper, two_cells(taps, j, 4 * step, 3 * step))
        acc = jnp.concatenate([a[:width], a[width:] + b[: 2 * width], b[2 * width :]], 0)
        pooled.append(pool_first(acc, j, pairs, False, False))
    partial2[...] = mat(middle2[...], second_taps(pooled, z_sel[...]))
    load.wait()
    out_rows = picked.shape[0] // 9
    own = (out_rows, w3.shape[1])
    first = lax.axis_index("yz") * out_rows
    pick = (iota(own, 1) == iota(own, 0) + first).astype(F32).astype(BF)
    own3 = lax.dot_general(pick, w3[...], (((1,), (1,)), ((), ())), preferred_element_type=F32)
    depth = picked.shape[1] // 3
    for tap in range(9):
        pieces = [own3[:, (9 * a + tap) * depth : (9 * a + tap + 1) * depth] for a in range(3)]
        picked[tap * out_rows : (tap + 1) * out_rows] = jnp.concatenate(pieces, 1)


def outer_kernel(got_a, got_b, partial1, partial2, lower1, upper1, outer2, z_sel, p_sel, out, low_taps, high_taps):
    planes, edge, breadth = got_a.shape
    chans = edge // EDGE
    k = lax.axis_index("yz")
    even, first, last = is_even("yz"), k == 0, k == lax.axis_size("yz") - 1
    for e in range(planes):
        low, high = from_sides(got_a[e], got_b[e], even, first, last)
        put_taps(low_taps.at[e], low, chans)
        put_taps(high_taps.at[e], high, chans)
    pairs = partial1.shape[1]
    width = lower1.shape[0] // 4
    lower, upper = lower1[: 3 * width], upper1[width:]
    rows = 3 * edge
    below, above = [], []
    for j in range(pairs):
        p = partial1[0, j]
        a = p[: 3 * width] + mat(lower, two_cells(low_taps, j, 0, rows))
        below.append(pool_first(jnp.concatenate([a, p[3 * width :]], 0), j, pairs, first, False))
        p = partial1[1, j]
        b = p[width:] + mat(upper, two_cells(high_taps, j, 0, rows))
        above.append(pool_first(jnp.concatenate([p[:width], b], 0), j, pairs, False, last))
    width = outer2.shape[0] // 4
    halves = []
    for y, pooled in enumerate((below, above)):
        part = slice(2 * y * width, 2 * (y + 1) * width)
        r = relu(partial2[part] + mat(outer2[part], second_taps(pooled, z_sel[...])))
        t = r[:width] + r[width:]
        cells = t.shape[1]
        t = t + pltpu.roll(t, cells - breadth // 2, 1)
        t = (t + pltpu.roll(t, cells - 1, 1)) * 0.125
        halves.append(t.astype(BF))
    for x in range(0, PLANES, 2):
        both = [t[:, x * breadth : (x + 2) * breadth] for t in halves]
        out[x // 2 * width : (x // 2 + 1) * width] = mat(jnp.concatenate(both, 1), p_sel[...]).astype(BF)


def lay(tiles, rows):
    even = is_even("yz")
    half = tiles[0].shape[1] // 2
    lane = iota((1, 2 * half), 1)
    tiles = [tiles[i] for i in [0, 3, 2, 1]]
    low, high = [], []
    for m in range(len(tiles) // 2):
        a, b = tiles[2 * m][rows].astype(F32), tiles[2 * m + 1][rows].astype(F32)
        first, second = jnp.where(even, a, b), jnp.where(even, b, a)
        low.append(jnp.where(lane < half, first, pltpu.roll(second, half, 1)))
        high.append(jnp.where(lane < half, pltpu.roll(first, half, 1), second))
    return low, high


def put_plane(dest, blocks):
    wide = blocks[0].shape[1]
    k = lax.axis_index("yz")
    for m, block in enumerate(blocks):
        dest[:, pl.ds(pl.multiple_of((lax.div(k, 2) ^ m) * wide, wide), wide)] = block.astype(BF)


def lay_kernel(*refs):
    tiles, (mate, far) = refs[:-2], refs[-2:]
    low, high = lay(tiles, slice(None))
    even = is_even("gx")
    put_plane(mate, [jnp.where(even, b, a) for a, b in zip(low, high)])
    put_plane(far, [jnp.where(even, a, b) for a, b in zip(low, high)])


def shift_taps(products, z):
    rows, cells = products.shape[0] // 9, products.shape[1]
    lane = iota((1, cells), 1)
    depth = lane & (z - 1)
    total = None
    for b in range(3):
        one = [products[(3 * b + c) * rows : (3 * b + c + 1) * rows] for c in range(3)]
        t = one[1] + jnp.where(depth == 0, 0.0, pltpu.roll(one[0], 1, 1))
        t = t + jnp.where(depth == z - 1, 0.0, pltpu.roll(one[2], cells - 1, 1))
        if b == 0:
            t = jnp.where(lane < z, 0.0, pltpu.roll(t, z, 1))
        if b == 2:
            t = jnp.where(lane >= cells - z, 0.0, pltpu.roll(t, cells - z, 1))
        total = t if total is None else total + t
    return total


def middle_kernel(z, mate, far, w3, partial):
    depth = mate.shape[0]
    even = is_even("gx")
    a, b = mate[...], far[...]
    both = jnp.concatenate([jnp.where(even, b, a), jnp.where(even, a, b)], 0)
    w = w3[...].astype(BF)
    partial[0] = shift_taps(mat(w[:, depth:], both), z)
    partial[1] = shift_taps(mat(w[:, : 2 * depth], both), z)


def last_kernel(z, partial, got_far, got_mate, w3, out):
    depth = got_mate.shape[0]
    g, g_last = lax.axis_index("gx"), lax.axis_size("gx") - 1
    low, high = from_sides(got_mate[...], got_far[...], is_even("gx"), g == 0, g == g_last)
    w = w3[...].astype(BF)
    first = relu(partial[0] + shift_taps(mat(w[:, :depth], low), z))
    second = relu(partial[1] + shift_taps(mat(w[:, 2 * depth :], high), z))
    out[...] = jnp.stack([first, second], 1).astype(BF)


def all_kernel(z, *refs):
    tiles, (w3, out, planes) = refs[:-3], refs[-3:]
    depth = planes.shape[1]
    for x in range(2):
        low, high = lay(tiles, slice(x * depth, (x + 1) * depth))
        put_plane(planes.at[2 * x], low)
        put_plane(planes.at[2 * x + 1], high)
    g, g_last = lax.axis_index("gx"), lax.axis_size("gx") - 1
    t = [planes[x] for x in range(4)]
    t[0] = jnp.where(g == 0, jnp.zeros_like(t[0]), t[0])
    t[3] = jnp.where(g == g_last, jnp.zeros_like(t[3]), t[3])
    w = w3[...].astype(BF)
    results = [relu(shift_taps(mat(w, jnp.concatenate(t[x : x + 3], 0)), z)) for x in range(2)]
    out[...] = jnp.stack(results, 1).astype(BF)


def per_device(volume, weight_one, weight_two, weight_three):
    gx, yz = lax.axis_size("gx"), lax.axis_size("yz")
    planes, chans, height, breadth = volume.shape
    rows = chans * height
    edge = EDGE * chans
    c2, c3 = weight_one.shape[0], weight_two.shape[0]

    turned, send_mate, send_far = call(
        turn_kernel,
        [((planes, rows, breadth), BF), ((HALO, rows, breadth), BF), ((HALO, rows, breadth), BF)],
        volume,
    )
    near, away = gx_pairs(gx, yz, False), gx_pairs(gx, yz, True)
    got_mate = lax.ppermute(send_mate, ("gx", "yz"), near)
    got_far = lax.ppermute(send_far, ("gx", "yz"), away)
    k1, k2 = 27 * chans, 27 * c2
    lower1, upper1, middle2, outer2, z_sel, p_sel = call(
        weights_kernel,
        [
            ((4 * c2, k1), BF),
            ((4 * c2, k1), BF),
            ((4 * c3, 2 * k2 // 3), BF),
            ((4 * c3, 2 * k2 // 3), BF),
            ((2 * breadth, 2 * breadth), BF),
            ((4 * breadth, breadth), BF),
        ],
        weight_one,
        weight_two,
        scratch=[
            pltpu.VMEM(weight_one.shape, BF),
            pltpu.VMEM(weight_two.shape, BF),
            pltpu.SemaphoreType.DMA((2,)),
        ],
        hbm=(0, 1),
        flops=2 * 64 * 864 * 1728,
    )
    wide = planes + 2 * HALO
    send_a, send_b = call(
        edge_kernel,
        [((wide, edge, breadth), BF), ((wide, edge, breadth), BF)],
        turned,
        got_far,
        got_mate,
        p_sel,
    )
    got_b = lax.ppermute(send_b, ("gx", "yz"), yz_pairs(gx, yz, True))
    got_a = lax.ppermute(send_a, ("gx", "yz"), yz_pairs(gx, yz, False))
    pairs = 2 * PLANES + 2
    out_rows = weight_three.shape[0] // yz
    partial1, partial2, picked = call(
        inner_kernel,
        [
            ((2, pairs, 4 * c2, 2 * breadth), F32),
            ((4 * c3, PLANES * breadth), F32),
            ((9 * out_rows, 3 * c3), F32),
        ],
        turned,
        got_mate,
        got_far,
        lower1,
        upper1,
        middle2,
        z_sel,
        weight_three.T,
        scratch=[
            pltpu.VMEM((wide, 3 * rows, breadth), BF),
            pltpu.VMEM(weight_three.shape[::-1], BF),
            pltpu.SemaphoreType.DMA,
        ],
        hbm=(7,),
        flops=2 * 300_000_000,
    )
    (tile,) = call(
        outer_kernel,
        [((PLANES // 2 * c3, breadth), BF)],
        got_a,
        got_b,
        partial1,
        partial2,
        lower1,
        upper1,
        outer2,
        z_sel,
        p_sel,
        scratch=[pltpu.VMEM((wide, 3 * edge, breadth), BF), pltpu.VMEM((wide, 3 * edge, breadth), BF)],
        flops=2 * 400_000_000,
    )
    tiles = [tile] + [lax.ppermute(tile, "yz", [(i, i ^ d) for i in range(yz)]) for d in range(1, yz)]
    cells = yz * (height // 4) * (breadth // 4)
    z = breadth // 4
    if PLANES == 4:
        (out,) = call(
            functools.partial(all_kernel, z),
            [((out_rows, 2, cells), BF)],
            *tiles[::-1],
            picked,
            scratch=[pltpu.VMEM((4, c3, cells), BF)],
            flops=2 * 32 * 1728 * 512,
        )
        return out
    mate, far = call(lay_kernel, [((c3, cells), BF), ((c3, cells), BF)], tiles[0], *[tiles[d] for d in [3, 2, 1]])
    got_far = lax.ppermute(far, ("gx", "yz"), away)
    got_mate = lax.ppermute(mate, ("gx", "yz"), near)
    (partial,) = call(
        functools.partial(middle_kernel, z),
        [((2, out_rows, cells), F32)],
        mate,
        far,
        picked,
        flops=2 * 32 * 1152 * 512,
    )
    (out,) = call(
        functools.partial(last_kernel, z),
        [((out_rows, 2, cells), BF)],
        partial,
        got_far,
        got_mate,
        picked,
        flops=2 * 32 * 576 * 512,
    )
    return out


def solution(mesh):
    placed = (P("gx", None, "yz", None), P(), P(), P())
    return jax.shard_map(
        per_device, mesh=mesh, in_specs=placed, out_specs=P("yz", "gx", None), check_vma=False
    )
```

```python
import functools

import jax
import jax.numpy as jnp
from jax import lax
from jax.experimental import pallas as pl
from jax.experimental.pallas import tpu as pltpu
from jax.sharding import PartitionSpec as P

BF = jnp.bfloat16
F32 = jnp.float32
WHOLE = pl.BlockSpec(memory_space=pltpu.VMEM)
PLANES = 2
HALO = 2 * PLANES - 1
EDGE = 3


def mat(a, b):
    return jnp.dot(a, b, preferred_element_type=F32)


def relu(a):
    return jnp.maximum(a, 0.0)


def iota(shape, dim):
    return lax.broadcasted_iota(jnp.int32, shape, dim)


def call(body, outs, *args, scratch=(), flops=0, hbm=(), hbm_out=False, aliases={}):
    moved = sum(a.size * a.dtype.itemsize for a in args)
    args = [pltpu.with_memory_space_constraint(a, pltpu.HBM) if i in hbm else a for i, a in enumerate(args)]
    return pl.pallas_call(
        body,
        out_shape=[jax.ShapeDtypeStruct(s, d) for s, d in outs],
        in_specs=[pl.BlockSpec(memory_space=pltpu.HBM if i in hbm else pltpu.VMEM) for i in range(len(args))],
        out_specs=[pl.BlockSpec(memory_space=pltpu.HBM) if hbm_out else WHOLE] * len(outs),
        scratch_shapes=list(scratch),
        input_output_aliases=aliases,
        compiler_params=pltpu.CompilerParams(vmem_limit_bytes=40 * 1024 * 1024),
        cost_estimate=pl.CostEstimate(flops=flops, bytes_accessed=moved, transcendentals=0),
    )(*args)


def turn_kernel(vol, turned, send_mate, send_far):
    planes, chans, height, breadth = vol.shape
    rows = chans * height
    dest = iota((rows, rows), 0)
    source = (dest & (chans - 1)) * height + dest // chans
    swap = (iota((rows, rows), 1) == source).astype(F32).astype(BF)
    for x in range(planes):
        turned[x] = mat(swap, vol[x].reshape(rows, breadth)).astype(BF)
    even = is_even("gx")
    for out, first in (
        (send_mate, jnp.where(even, planes - HALO, 0)),
        (send_far, jnp.where(even, 0, planes - HALO)),
    ):
        for x in range(HALO):
            out[x] = turned[first + x]


def yz_pairs(gx, yz, second):
    pairs = []
    for g in range(gx):
        for k in range(yz):
            if not second:
                pairs.append((g * yz + k, g * yz + (k ^ 1)))
            elif k in (0, yz - 1):
                pairs.append((g * yz + k, (g ^ 1) * yz + k))
            else:
                pairs.append((g * yz + k, g * yz + (k + 1 if k % 2 else k - 1)))
    return pairs


def gx_pairs(gx, yz, far):
    pairs = []
    for g in range(gx):
        for k in range(yz):
            if not far:
                pairs.append((g * yz + k, (g ^ 1) * yz + k))
            elif g in (0, gx - 1):
                pairs.append((g * yz + k, g * yz + (k ^ 1)))
            else:
                pairs.append((g * yz + k, (g + 1 if g % 2 else g - 1) * yz + k))
    return pairs


def is_even(axis):
    return lax.rem(lax.axis_index(axis), 2) == 0


def from_sides(mate, far, even, no_low, no_high):
    zero = jnp.zeros_like(mate)
    low = jnp.where(no_low, zero, jnp.where(even, far, mate))
    high = jnp.where(no_high, zero, jnp.where(even, mate, far))
    return low, high


def all_planes(turned, got_mate, got_far):
    g = lax.axis_index("gx")
    even, first, last = is_even("gx"), g == 0, g == lax.axis_size("gx") - 1
    sides = [from_sides(got_mate[x], got_far[x], even, first, last) for x in range(HALO)]
    return [low for low, _ in sides] + [turned[x] for x in range(turned.shape[0])] + [high for _, high in sides]


def edge_kernel(turned, got_far, got_mate, _, send_a, send_b):
    edge = send_a.shape[1]
    even = is_even("yz")
    for x, t in enumerate(all_planes(turned, got_mate, got_far)):
        low, high = t[:edge], t[t.shape[0] - edge :]
        send_a[x] = jnp.where(even, high, low)
        send_b[x] = jnp.where(even, low, high)


def weights_kernel(w1_hbm, w2_hbm, lower1, upper1, middle2, outer2, z_sel, p_sel, w1, w2, sems):
    loads = [pltpu.make_async_copy(a, b, sems.at[i]) for i, (a, b) in enumerate(((w1_hbm, w1), (w2_hbm, w2)))]
    for load in loads:
        load.start()

    rows, columns = z_sel.shape
    breadth = rows // 2
    r, c = iota(z_sel.shape, 0), iota(z_sel.shape, 1)
    tap = c // breadth
    within = c - tap * breadth
    same = (r // breadth) == (within // (breadth // 2))
    cell = (r & (breadth - 1)) == 2 * ((within & (breadth // 2 - 1)) + tap - 1)
    z_sel[...] = jnp.where(same & cell, 1.0, 0.0).astype(BF)

    rows, columns = p_sel.shape
    z = rows // 8
    r, c = iota(p_sel.shape, 0), iota(p_sel.shape, 1)
    hit = (r // (4 * z) == (c // (z // 2)) % 2) & ((r // z) % 4 == 2 * (c // z))
    hit = hit & ((r & (z - 1)) == 2 * (c & (z // 2 - 1)))
    p_sel[...] = jnp.where(hit, 1.0, 0.0).astype(BF)

    for load in loads:
        load.wait()
    for w, bands in (
        (w1, ((lower1, lambda y: (0, 1, 2)), (upper1, lambda y: (3, 4, 5)))),
        (w2, ((middle2, lambda y: (2, 3)), (outer2, lambda y: (0, 1) if y < 2 else (4, 5)))),
    ):
        out_rows, width = w.shape[0], w.shape[1] // 9
        taps = w[...].astype(F32)
        zero = jnp.zeros((out_rows, width), F32)
        for band, window in bands:
            for y in range(4):
                pieces = []
                for a in range(3):
                    for row in window(y):
                        first = (3 * a + row - y) * width
                        pieces.append(taps[:, first : first + width] if 0 <= row - y < 3 else zero)
                band[out_rows * y : out_rows * (y + 1)] = jnp.concatenate(pieces, 1).astype(BF)


def put_taps(dest, t, chans):
    breadth = t.shape[1]
    lane = iota((1, breadth), 1)
    wide = t.astype(F32)
    before = jnp.where(lane == 0, 0.0, pltpu.roll(wide, 1, 1)).astype(BF)
    after = jnp.where(lane == breadth - 1, 0.0, pltpu.roll(wide, breadth - 1, 1)).astype(BF)
    for y in range(t.shape[0] // chans):
        for tap, value in enumerate((before, t, after)):
            row = (3 * y + tap) * chans
            dest[row : row + chans] = value[y * chans : (y + 1) * chans]


def three(taps, e, first, rows):
    return jnp.concatenate([taps[e + a, first : first + rows] for a in range(3)], 0)


def two_cells(taps, j, first, rows):
    return jnp.concatenate([three(taps, 2 * j, first, rows), three(taps, 2 * j + 1, first, rows)], 1)


def pool_first(acc, j, pairs, no_low, no_high):
    g = lax.axis_index("gx")
    breadth = acc.shape[1] // 2
    width = acc.shape[0] // 4
    r = relu(acc)
    s = r[:, :breadth] + r[:, breadth:]
    halves = []
    for y, drop in enumerate((no_low, no_high)):
        t = s[2 * y * width : (2 * y + 1) * width] + s[(2 * y + 1) * width : (2 * y + 2) * width]
        t = (t + pltpu.roll(t, breadth - 1, 1)) * 0.125
        if j < PLANES - 1:
            drop = drop | (g == 0)
        if j > pairs - PLANES:
            drop = drop | (g == lax.axis_size("gx") - 1)
        halves.append(t if drop is False else jnp.where(drop, 0.0, t))
    return jnp.concatenate(halves, 0).astype(BF)


def second_taps(pooled, z_sel):
    beside = [jnp.concatenate([a, b], 1) for a, b in zip(pooled[:-1], pooled[1:])]
    q = mat(jnp.concatenate(beside, 0), z_sel)
    breadth = q.shape[1] // 2
    before, here = q[:, :breadth], q[:, breadth:]
    lane = iota((1, breadth), 1)
    last = (lane & (breadth // 2 - 1)) == breadth // 2 - 1
    after = jnp.where(last, 0.0, pltpu.roll(here, breadth - 1, 1))
    taps = [t.astype(BF) for t in (before, here, after)]
    chans = pooled[0].shape[0] // 2
    planes = []
    for j in range(len(beside)):
        rows = [slice((2 * j + y) * chans, (2 * j + y + 1) * chans) for y in range(2)]
        planes.append([t[r] for r in rows for t in taps])
    columns = [jnp.concatenate(planes[j] + planes[j + 1] + planes[j + 2], 0) for j in range(0, len(planes) - 2, 2)]
    return jnp.concatenate(columns, 1)


def inner_kernel(
    turned, got_mate, got_far, lower1, upper1, middle2, z_sel, w3_hbm, partial1, partial2, picked, taps, w3, sem
):
    load = pltpu.make_async_copy(w3_hbm, w3, sem)
    load.start()
    chans = lower1.shape[1] // 27
    for e, t in enumerate(all_planes(turned, got_mate, got_far)):
        put_taps(taps.at[e], t, chans)
    pairs = partial1.shape[1]
    width = lower1.shape[0] // 4
    lower, upper = lower1[: 3 * width], upper1[width:]
    step = 3 * chans
    pooled = []
    zero = jnp.zeros((width, partial1.shape[3]), F32)
    for j in range(pairs):
        partial1[0, j, :width] = zero
        partial1[0, j, width:] = mat(upper, two_cells(taps, j, 0, 3 * step))
        partial1[1, j, : 3 * width] = mat(lower, two_cells(taps, j, 5 * step, 3 * step))
        partial1[1, j, 3 * width :] = zero
        a = mat(lower, two_cells(taps, j, step, 3 * step))
        b = mat(upper, two_cells(taps, j, 4 * step, 3 * step))
        acc = jnp.concatenate([a[:width], a[width:] + b[: 2 * width], b[2 * width :]], 0)
        pooled.append(pool_first(acc, j, pairs, False, False))
    partial2[...] = mat(middle2[...], second_taps(pooled, z_sel[...]))
    load.wait()
    out_rows = picked.shape[0] // 9
    own = (out_rows, w3.shape[1])
    first = lax.axis_index("yz") * out_rows
    pick = (iota(own, 1) == iota(own, 0) + first).astype(F32).astype(BF)
    own3 = lax.dot_general(pick, w3[...], (((1,), (1,)), ((), ())), preferred_element_type=F32)
    depth = picked.shape[1] // 3
    for tap in range(9):
        pieces = [own3[:, (9 * a + tap) * depth : (9 * a + tap + 1) * depth] for a in range(3)]
        picked[tap * out_rows : (tap + 1) * out_rows] = jnp.concatenate(pieces, 1)


def outer_kernel(got_a, got_b, partial1, partial2, lower1, upper1, outer2, z_sel, p_sel, out, low_taps, high_taps):
    planes, edge, breadth = got_a.shape
    chans = edge // EDGE
    k = lax.axis_index("yz")
    even, first, last = is_even("yz"), k == 0, k == lax.axis_size("yz") - 1
    for e in range(planes):
        low, high = from_sides(got_a[e], got_b[e], even, first, last)
        put_taps(low_taps.at[e], low, chans)
        put_taps(high_taps.at[e], high, chans)
    pairs = partial1.shape[1]
    width = lower1.shape[0] // 4
    lower, upper = lower1[: 3 * width], upper1[width:]
    rows = 3 * edge
    below, above = [], []
    for j in range(pairs):
        p = partial1[0, j]
        a = p[: 3 * width] + mat(lower, two_cells(low_taps, j, 0, rows))
        below.append(pool_first(jnp.concatenate([a, p[3 * width :]], 0), j, pairs, first, False))
        p = partial1[1, j]
        b = p[width:] + mat(upper, two_cells(high_taps, j, 0, rows))
        above.append(pool_first(jnp.concatenate([p[:width], b], 0), j, pairs, False, last))
    width = outer2.shape[0] // 4
    halves = []
    for y, pooled in enumerate((below, above)):
        part = slice(2 * y * width, 2 * (y + 1) * width)
        r = relu(partial2[part] + mat(outer2[part], second_taps(pooled, z_sel[...])))
        t = r[:width] + r[width:]
        cells = t.shape[1]
        t = t + pltpu.roll(t, cells - breadth // 2, 1)
        t = (t + pltpu.roll(t, cells - 1, 1)) * 0.125
        halves.append(t.astype(BF))
    for x in range(0, PLANES, 2):
        both = [t[:, x * breadth : (x + 2) * breadth] for t in halves]
        out[x // 2 * width : (x // 2 + 1) * width] = mat(jnp.concatenate(both, 1), p_sel[...]).astype(BF)


def lay(tiles, rows):
    even = is_even("yz")
    half = tiles[0].shape[1] // 2
    lane = iota((1, 2 * half), 1)
    tiles = [tiles[i] for i in [0, 3, 2, 1]]
    low, high = [], []
    for m in range(len(tiles) // 2):
        a, b = tiles[2 * m][rows].astype(F32), tiles[2 * m + 1][rows].astype(F32)
        first, second = jnp.where(even, a, b), jnp.where(even, b, a)
        low.append(jnp.where(lane < half, first, pltpu.roll(second, half, 1)))
        high.append(jnp.where(lane < half, pltpu.roll(first, half, 1), second))
    return low, high


def put_plane(dest, blocks):
    wide = blocks[0].shape[1]
    k = lax.axis_index("yz")
    for m, block in enumerate(blocks):
        dest[:, pl.ds(pl.multiple_of((lax.div(k, 2) ^ m) * wide, wide), wide)] = block.astype(BF)


def lay_kernel(*refs):
    tiles, (mate, far) = refs[:-2], refs[-2:]
    low, high = lay(tiles, slice(None))
    even = is_even("gx")
    put_plane(mate, [jnp.where(even, b, a) for a, b in zip(low, high)])
    put_plane(far, [jnp.where(even, a, b) for a, b in zip(low, high)])


def shift_taps(products, z):
    rows, cells = products.shape[0] // 9, products.shape[1]
    lane = iota((1, cells), 1)
    depth = lane & (z - 1)
    total = None
    for b in range(3):
        one = [products[(3 * b + c) * rows : (3 * b + c + 1) * rows] for c in range(3)]
        t = one[1] + jnp.where(depth == 0, 0.0, pltpu.roll(one[0], 1, 1))
        t = t + jnp.where(depth == z - 1, 0.0, pltpu.roll(one[2], cells - 1, 1))
        if b == 0:
            t = jnp.where(lane < z, 0.0, pltpu.roll(t, z, 1))
        if b == 2:
            t = jnp.where(lane >= cells - z, 0.0, pltpu.roll(t, cells - z, 1))
        total = t if total is None else total + t
    return total


def near_kernel(z, mate, far, got_mate, w3, out, ready, pending):
    depth = mate.shape[0]
    even = is_even("gx")
    a, b = mate[...], far[...]
    both = jnp.concatenate([jnp.where(even, b, a), jnp.where(even, a, b)], 0)
    w = w3[...].astype(BF)
    first, second = w[:, depth:], w[:, : 2 * depth]
    beside = jnp.where(even, w[:, 2 * depth :], w[:, :depth])
    t = mat(jnp.where(even, second, first), both) + mat(beside, got_mate[...])
    done = relu(shift_taps(t, z))
    part = shift_taps(mat(jnp.where(even, first, second), both), z)
    ready[...] = done
    pending[...] = part
    part = relu(part)
    out[...] = jnp.stack([jnp.where(even, part, done), jnp.where(even, done, part)], 1).astype(BF)


def far_kernel(z, got_far, w3, ready, pending, _, out, block, sem):
    depth = got_far.shape[0]
    g = lax.axis_index("gx")

    @pl.when((g > 0) & (g < lax.axis_size("gx") - 1))
    def _():
        even = is_even("gx")
        w = w3[...].astype(BF)
        beside = jnp.where(even, w[:, :depth], w[:, 2 * depth :])
        part = relu(pending[...] + shift_taps(mat(beside, got_far[...]), z))
        done = ready[...]
        block[...] = jnp.stack([jnp.where(even, part, done), jnp.where(even, done, part)], 1).astype(BF)
        copy = pltpu.make_async_copy(block, out, sem)
        copy.start()
        copy.wait()


def per_device(volume, weight_one, weight_two, weight_three):
    gx, yz = lax.axis_size("gx"), lax.axis_size("yz")
    planes, chans, height, breadth = volume.shape
    rows = chans * height
    edge = EDGE * chans
    c2, c3 = weight_one.shape[0], weight_two.shape[0]

    turned, send_mate, send_far = call(
        turn_kernel,
        [((planes, rows, breadth), BF), ((HALO, rows, breadth), BF), ((HALO, rows, breadth), BF)],
        volume,
    )
    near, away = gx_pairs(gx, yz, False), gx_pairs(gx, yz, True)
    got_mate = lax.ppermute(send_mate, ("gx", "yz"), near)
    got_far = lax.ppermute(send_far, ("gx", "yz"), away)
    k1, k2 = 27 * chans, 27 * c2
    lower1, upper1, middle2, outer2, z_sel, p_sel = call(
        weights_kernel,
        [
            ((4 * c2, k1), BF),
            ((4 * c2, k1), BF),
            ((4 * c3, 2 * k2 // 3), BF),
            ((4 * c3, 2 * k2 // 3), BF),
            ((2 * breadth, 2 * breadth), BF),
            ((4 * breadth, breadth), BF),
        ],
        weight_one,
        weight_two,
        scratch=[
            pltpu.VMEM(weight_one.shape, BF),
            pltpu.VMEM(weight_two.shape, BF),
            pltpu.SemaphoreType.DMA((2,)),
        ],
        hbm=(0, 1),
        flops=2 * 64 * 864 * 1728,
    )
    wide = planes + 2 * HALO
    send_a, send_b = call(
        edge_kernel,
        [((wide, edge, breadth), BF), ((wide, edge, breadth), BF)],
        turned,
        got_far,
        got_mate,
        p_sel,
    )
    got_b = lax.ppermute(send_b, ("gx", "yz"), yz_pairs(gx, yz, True))
    got_a = lax.ppermute(send_a, ("gx", "yz"), yz_pairs(gx, yz, False))
    pairs = 2 * PLANES + 2
    out_rows = weight_three.shape[0] // yz
    partial1, partial2, picked = call(
        inner_kernel,
        [
            ((2, pairs, 4 * c2, 2 * breadth), F32),
            ((4 * c3, PLANES * breadth), F32),
            ((9 * out_rows, 3 * c3), F32),
        ],
        turned,
        got_mate,
        got_far,
        lower1,
        upper1,
        middle2,
        z_sel,
        weight_three.T,
        scratch=[
            pltpu.VMEM((wide, 3 * rows, breadth), BF),
            pltpu.VMEM(weight_three.shape[::-1], BF),
            pltpu.SemaphoreType.DMA,
        ],
        hbm=(7,),
        flops=2 * 300_000_000,
    )
    (tile,) = call(
        outer_kernel,
        [((PLANES // 2 * c3, breadth), BF)],
        got_a,
        got_b,
        partial1,
        partial2,
        lower1,
        upper1,
        outer2,
        z_sel,
        p_sel,
        scratch=[pltpu.VMEM((wide, 3 * edge, breadth), BF), pltpu.VMEM((wide, 3 * edge, breadth), BF)],
        flops=2 * 400_000_000,
    )
    tiles = [tile] + [lax.ppermute(tile, "yz", [(i, i ^ d) for i in range(yz)]) for d in range(1, yz)]
    cells = yz * (height // 4) * (breadth // 4)
    z = breadth // 4
    mate, far = call(lay_kernel, [((c3, cells), BF), ((c3, cells), BF)], tiles[0], *[tiles[d] for d in [3, 2, 1]])
    got_far = lax.ppermute(far, ("gx", "yz"), away)
    got_mate = lax.ppermute(mate, ("gx", "yz"), near)
    shape = (out_rows, 2, cells)
    out, ready, pending = call(
        functools.partial(near_kernel, z),
        [(shape, BF), ((out_rows, cells), F32), ((out_rows, cells), F32)],
        mate,
        far,
        got_mate,
        picked,
        flops=2 * 32 * 1728 * 512,
    )
    (out,) = call(
        functools.partial(far_kernel, z),
        [(shape, BF)],
        got_far,
        picked,
        ready,
        pending,
        out,
        scratch=[pltpu.VMEM(shape, BF), pltpu.SemaphoreType.DMA],
        hbm=(4,),
        hbm_out=True,
        aliases={4: 0},
        flops=2 * 32 * 576 * 256,
    )
    return out


def solution(mesh):
    placed = (P("gx", None, "yz", None), P(), P(), P())
    return jax.shard_map(
        per_device, mesh=mesh, in_specs=placed, out_specs=P("yz", "gx", None), check_vma=False
    )
```

```python
import functools

import jax
import jax.numpy as jnp
from jax import lax
from jax.experimental import pallas as pl
from jax.experimental.pallas import tpu as pltpu
from jax.sharding import PartitionSpec as P

BF = jnp.bfloat16
F32 = jnp.float32
PLANES = 2
HALO = 2 * PLANES - 1
EDGE = 3


def mat(a, b):
    return jnp.dot(a, b, preferred_element_type=F32)


def relu(a):
    return jnp.maximum(a, 0.0)


def iota(shape, dim):
    return lax.broadcasted_iota(jnp.int32, shape, dim)


def call(body, outs, *args, scratch=(), flops=0, free=False, hbm=(), hbm_out=False, aliases={}):
    moved = 0 if free else sum(a.size * a.dtype.itemsize for a in args)
    args = [pltpu.with_memory_space_constraint(a, pltpu.HBM) if i in hbm else a for i, a in enumerate(args)]
    return pl.pallas_call(
        body,
        out_shape=[jax.ShapeDtypeStruct(s, d) for s, d in outs],
        in_specs=[pl.BlockSpec(memory_space=pltpu.HBM if i in hbm else pltpu.VMEM) for i in range(len(args))],
        out_specs=[pl.BlockSpec(memory_space=pltpu.HBM if hbm_out and i == 0 else pltpu.VMEM) for i in range(len(outs))],
        scratch_shapes=list(scratch),
        input_output_aliases=aliases,
        compiler_params=pltpu.CompilerParams(vmem_limit_bytes=40 * 1024 * 1024),
        cost_estimate=pl.CostEstimate(flops=flops, bytes_accessed=moved, transcendentals=0),
    )(*args)


def turn_kernel(vol, turned, send_mate, send_far):
    planes, chans, height, breadth = vol.shape
    rows = chans * height
    dest = iota((rows, rows), 0)
    source = (dest & (chans - 1)) * height + dest // chans
    swap = (iota((rows, rows), 1) == source).astype(F32).astype(BF)
    for x in range(planes):
        turned[x] = mat(swap, vol[x].reshape(rows, breadth)).astype(BF)
    even = is_even("gx")
    for out, first in (
        (send_mate, jnp.where(even, planes - HALO, 0)),
        (send_far, jnp.where(even, 0, planes - HALO)),
    ):
        for x in range(HALO):
            out[x] = turned[first + x]


def yz_pairs(gx, yz, second):
    pairs = []
    for g in range(gx):
        for k in range(yz):
            if not second:
                pairs.append((g * yz + k, g * yz + (k ^ 1)))
            elif k in (0, yz - 1):
                pairs.append((g * yz + k, (g ^ 1) * yz + k))
            else:
                pairs.append((g * yz + k, g * yz + (k + 1 if k % 2 else k - 1)))
    return pairs


def gx_pairs(gx, yz, far):
    pairs = []
    for g in range(gx):
        for k in range(yz):
            if not far:
                pairs.append((g * yz + k, (g ^ 1) * yz + k))
            elif g in (0, gx - 1):
                pairs.append((g * yz + k, g * yz + (k ^ 1)))
            else:
                pairs.append((g * yz + k, (g + 1 if g % 2 else g - 1) * yz + k))
    return pairs


def is_even(axis):
    return lax.rem(lax.axis_index(axis), 2) == 0


def from_sides(mate, far, even, no_low, no_high):
    zero = jnp.zeros_like(mate)
    low = jnp.where(no_low, zero, jnp.where(even, far, mate))
    high = jnp.where(no_high, zero, jnp.where(even, mate, far))
    return low, high


def all_planes(turned, got_mate, got_far):
    g = lax.axis_index("gx")
    even, first, last = is_even("gx"), g == 0, g == lax.axis_size("gx") - 1
    sides = [from_sides(got_mate[x], got_far[x], even, first, last) for x in range(HALO)]
    return [low for low, _ in sides] + [turned[x] for x in range(turned.shape[0])] + [high for _, high in sides]


def edge_kernel(turned, got_far, got_mate, _, send_a, send_b):
    edge = send_a.shape[1]
    even = is_even("yz")
    for x, t in enumerate(all_planes(turned, got_mate, got_far)):
        low, high = t[:edge], t[t.shape[0] - edge :]
        send_a[x] = jnp.where(even, high, low)
        send_b[x] = jnp.where(even, low, high)


def weights_kernel(w1_hbm, w2_hbm, lower1, upper1, middle2, outer2, p_sel, w1, w2, sems):
    loads = [pltpu.make_async_copy(a, b, sems.at[i]) for i, (a, b) in enumerate(((w1_hbm, w1), (w2_hbm, w2)))]
    for load in loads:
        load.start()

    rows, columns = p_sel.shape
    z = rows // 4
    r, c = iota(p_sel.shape, 0), iota(p_sel.shape, 1)
    hit = (r // (2 * z) == (c // (z // 4)) % 2) & ((r // z) % 2 == c // (z // 2))
    hit = hit & ((r & (z - 1)) == 4 * (c & (z // 4 - 1)))
    p_sel[...] = jnp.where(hit, 1.0, 0.0).astype(BF)

    for load in loads:
        load.wait()
    for w, bands in (
        (w1, ((lower1, lambda y: (0, 1, 2)), (upper1, lambda y: (3, 4, 5)))),
        (w2, ((middle2, lambda y: (2, 3)), (outer2, lambda y: (0, 1) if y < 2 else (4, 5)))),
    ):
        out_rows, width = w.shape[0], w.shape[1] // 9
        taps = w[...].astype(F32)
        zero = jnp.zeros((out_rows, width), F32)
        for band, window in bands:
            for y in range(4):
                pieces = []
                for a in range(3):
                    for row in window(y):
                        first = (3 * a + row - y) * width
                        pieces.append(taps[:, first : first + width] if 0 <= row - y < 3 else zero)
                band[out_rows * y : out_rows * (y + 1)] = jnp.concatenate(pieces, 1).astype(BF)


def put_taps(dest, t, chans):
    breadth = t.shape[1]
    lane = iota((1, breadth), 1)
    wide = t.astype(F32)
    before = jnp.where(lane == 0, 0.0, pltpu.roll(wide, 1, 1)).astype(BF)
    after = jnp.where(lane == breadth - 1, 0.0, pltpu.roll(wide, breadth - 1, 1)).astype(BF)
    for y in range(t.shape[0] // chans):
        for tap, value in enumerate((before, t, after)):
            row = (3 * y + tap) * chans
            dest[row : row + chans] = value[y * chans : (y + 1) * chans]


def three(taps, e, first, rows):
    return jnp.concatenate([taps[e + a, first : first + rows] for a in range(3)], 0)


def two_cells(taps, j, first, rows):
    return jnp.concatenate([three(taps, 2 * j, first, rows), three(taps, 2 * j + 1, first, rows)], 1)


def pool_first(acc, j, pairs, no_low, no_high):
    g = lax.axis_index("gx")
    breadth = acc.shape[1] // 2
    width = acc.shape[0] // 4
    r = relu(acc)
    s = r[:, :breadth] + r[:, breadth:]
    halves = []
    for y, drop in enumerate((no_low, no_high)):
        t = s[2 * y * width : (2 * y + 1) * width] + s[(2 * y + 1) * width : (2 * y + 2) * width]
        t = (t + pltpu.roll(t, breadth - 1, 1)) * 0.125
        if j < PLANES - 1:
            drop = drop | (g == 0)
        if j > pairs - PLANES:
            drop = drop | (g == lax.axis_size("gx") - 1)
        halves.append(t if drop is False else jnp.where(drop, 0.0, t))
    return pooled_taps(jnp.concatenate(halves, 0))


def pooled_taps(t):
    breadth = t.shape[1]
    lane = iota((1, breadth), 1)
    before = jnp.where(lane < 2, 0.0, pltpu.roll(t, 2, 1)).astype(BF)
    after = jnp.where(lane >= breadth - 2, 0.0, pltpu.roll(t, breadth - 2, 1)).astype(BF)
    chans = t.shape[0] // 2
    rows = [slice(y * chans, (y + 1) * chans) for y in range(2)]
    return jnp.concatenate([u[r] for r in rows for u in (before, t.astype(BF), after)], 0)


def second_taps(planes):
    return jnp.concatenate([jnp.concatenate(planes[x : x + 3], 0) for x in range(len(planes) - 2)], 1)


def inner_kernel(
    turned, got_mate, got_far, lower1, upper1, middle2, w3_hbm, partial1, partial2, picked, taps, w3, sem
):
    load = pltpu.make_async_copy(w3_hbm, w3, sem)
    load.start()
    chans = lower1.shape[1] // 27
    for e, t in enumerate(all_planes(turned, got_mate, got_far)):
        put_taps(taps.at[e], t, chans)
    pairs = partial1.shape[1]
    width = lower1.shape[0] // 4
    lower, upper = lower1[: 3 * width], upper1[width:]
    step = 3 * chans
    pooled = []
    zero = jnp.zeros((width, partial1.shape[3]), F32)
    for j in range(pairs):
        partial1[0, j, :width] = zero
        partial1[0, j, width:] = mat(upper, two_cells(taps, j, 0, 3 * step))
        partial1[1, j, : 3 * width] = mat(lower, two_cells(taps, j, 5 * step, 3 * step))
        partial1[1, j, 3 * width :] = zero
        a = mat(lower, two_cells(taps, j, step, 3 * step))
        b = mat(upper, two_cells(taps, j, 4 * step, 3 * step))
        acc = jnp.concatenate([a[:width], a[width:] + b[: 2 * width], b[2 * width :]], 0)
        pooled.append(pool_first(acc, j, pairs, False, False))
    partial2[...] = mat(middle2[...], second_taps(pooled))
    load.wait()
    out_rows = picked.shape[0] // 9
    own = (out_rows, w3.shape[1])
    first = lax.axis_index("yz") * out_rows
    pick = (iota(own, 1) == iota(own, 0) + first).astype(F32).astype(BF)
    own3 = lax.dot_general(pick, w3[...], (((1,), (1,)), ((), ())), preferred_element_type=F32)
    depth = picked.shape[1] // 3
    for tap in range(9):
        pieces = [own3[:, (9 * a + tap) * depth : (9 * a + tap + 1) * depth] for a in range(3)]
        picked[tap * out_rows : (tap + 1) * out_rows] = jnp.concatenate(pieces, 1)


def outer_kernel(got_a, got_b, partial1, partial2, lower1, upper1, outer2, p_sel, out, low_taps, high_taps):
    planes, edge, breadth = got_a.shape
    chans = edge // EDGE
    k = lax.axis_index("yz")
    even, first, last = is_even("yz"), k == 0, k == lax.axis_size("yz") - 1
    for e in range(planes):
        low, high = from_sides(got_a[e], got_b[e], even, first, last)
        put_taps(low_taps.at[e], low, chans)
        put_taps(high_taps.at[e], high, chans)
    pairs = partial1.shape[1]
    width = lower1.shape[0] // 4
    lower, upper = lower1[: 3 * width], upper1[width:]
    rows = 3 * edge
    below, above = [], []
    for j in range(pairs):
        p = partial1[0, j]
        a = p[: 3 * width] + mat(lower, two_cells(low_taps, j, 0, rows))
        below.append(pool_first(jnp.concatenate([a, p[3 * width :]], 0), j, pairs, first, False))
        p = partial1[1, j]
        b = p[width:] + mat(upper, two_cells(high_taps, j, 0, rows))
        above.append(pool_first(jnp.concatenate([p[:width], b], 0), j, pairs, False, last))
    width = outer2.shape[0] // 4
    halves = []
    for y, pooled in enumerate((below, above)):
        part = slice(2 * y * width, 2 * (y + 1) * width)
        r = relu(partial2[part] + mat(outer2[part], second_taps(pooled)))
        t = r[:width] + r[width:]
        t = [t[:, 2 * x * breadth : (2 * x + 1) * breadth] + t[:, (2 * x + 1) * breadth : 2 * (x + 1) * breadth] for x in range(PLANES)]
        halves.append([((u + pltpu.roll(u, breadth - 2, 1)) * 0.125).astype(BF) for u in t])
    out[...] = mat(jnp.concatenate(halves[0] + halves[1], 1), p_sel[...]).astype(BF)


def lay(tiles, rows):
    even = is_even("yz")
    half = tiles[0].shape[1] // 2
    lane = iota((1, 2 * half), 1)
    tiles = [tiles[i] for i in [0, 3, 2, 1]]
    low, high = [], []
    for m in range(len(tiles) // 2):
        a, b = tiles[2 * m][rows].astype(F32), tiles[2 * m + 1][rows].astype(F32)
        first, second = jnp.where(even, a, b), jnp.where(even, b, a)
        low.append(jnp.where(lane < half, first, pltpu.roll(second, half, 1)))
        high.append(jnp.where(lane < half, pltpu.roll(first, half, 1), second))
    return low, high


def put_plane(dest, blocks):
    wide = blocks[0].shape[1]
    k = lax.axis_index("yz")
    for m, block in enumerate(blocks):
        dest[: block.shape[0], pl.ds(pl.multiple_of((lax.div(k, 2) ^ m) * wide, wide), wide)] = block.astype(BF)


def lay_kernel(*refs):
    tiles, (mate, far) = refs[:-2], refs[-2:]
    low, high = lay(tiles, slice(None))
    even = is_even("gx")
    put_plane(mate, [jnp.where(even, b, a) for a, b in zip(low, high)])
    put_plane(far, [jnp.where(even, a, b) for a, b in zip(low, high)])
    depth = mate.shape[0]
    far[depth:] = jnp.zeros((far.shape[0] - depth, far.shape[1]), BF)


def shift_taps(products, z):
    rows, cells = products.shape[0] // 9, products.shape[1]
    lane = iota((1, cells), 1)
    depth = lane & (z - 1)
    total = None
    for b in range(3):
        one = [products[(3 * b + c) * rows : (3 * b + c + 1) * rows] for c in range(3)]
        t = one[1] + jnp.where(depth == 0, 0.0, pltpu.roll(one[0], 1, 1))
        t = t + jnp.where(depth == z - 1, 0.0, pltpu.roll(one[2], cells - 1, 1))
        if b == 0:
            t = jnp.where(lane < z, 0.0, pltpu.roll(t, z, 1))
        if b == 2:
            t = jnp.where(lane >= cells - z, 0.0, pltpu.roll(t, cells - z, 1))
        total = t if total is None else total + t
    return total


def middle_kernel(z, mate, far, w3, beside_mate, beside_far, w_mate, w_far):
    depth = mate.shape[0]
    even = is_even("gx")
    a, b = mate[...], far[:depth]
    both = jnp.concatenate([jnp.where(even, b, a), jnp.where(even, a, b)], 0)
    w = w3[...].astype(BF)
    first, second = w[:, depth:], w[:, : 2 * depth]
    beside_mate[...] = shift_taps(mat(jnp.where(even, second, first), both), z)
    beside_far[...] = shift_taps(mat(jnp.where(even, first, second), both), z)
    w_mate[...] = jnp.where(even, w[:, 2 * depth :], w[:, :depth])
    w_far[...] = jnp.where(even, w[:, :depth], w[:, 2 * depth :])


def is_end():
    g = lax.axis_index("gx")
    return (g == 0) | (g == lax.axis_size("gx") - 1)


def write_planes(beside_mate, beside_far, out, block, sem):
    even = is_even("gx")
    a, b = relu(beside_mate), relu(beside_far)
    block[...] = jnp.stack([jnp.where(even, b, a), jnp.where(even, a, b)], 1).astype(BF)
    copy = pltpu.make_async_copy(block, out, sem)
    copy.start()
    copy.wait()


def near_kernel(z, beside_mate, beside_far, w_mate, got_mate, out, ready, block, sem):
    ready[...] = beside_mate[...] + shift_taps(mat(w_mate[...], got_mate[...]), z)

    @pl.when(is_end())
    def _():
        write_planes(ready[...], beside_far[...], out, block, sem)


def far_kernel(z, got_far, w_far, ready, beside_far, _, out, block, sem):
    @pl.when(jnp.logical_not(is_end()))
    def _():
        part = beside_far[...] + shift_taps(mat(w_far[...], got_far[: w_far.shape[1]]), z)
        write_planes(ready[...], part, out, block, sem)


def per_device(volume, weight_one, weight_two, weight_three):
    gx, yz = lax.axis_size("gx"), lax.axis_size("yz")
    planes, chans, height, breadth = volume.shape
    rows = chans * height
    edge = EDGE * chans
    c2, c3 = weight_one.shape[0], weight_two.shape[0]

    turned, send_mate, send_far = call(
        turn_kernel,
        [((planes, rows, breadth), BF), ((HALO, rows, breadth), BF), ((HALO, rows, breadth), BF)],
        volume,
    )
    near, away = gx_pairs(gx, yz, False), gx_pairs(gx, yz, True)
    got_mate = lax.ppermute(send_mate, ("gx", "yz"), near)
    got_far = lax.ppermute(send_far, ("gx", "yz"), away)
    k1, k2 = 27 * chans, 27 * c2
    lower1, upper1, middle2, outer2, p_sel = call(
        weights_kernel,
        [
            ((4 * c2, k1), BF),
            ((4 * c2, k1), BF),
            ((4 * c3, 2 * k2 // 3), BF),
            ((4 * c3, 2 * k2 // 3), BF),
            ((4 * breadth, breadth), BF),
        ],
        weight_one,
        weight_two,
        scratch=[
            pltpu.VMEM(weight_one.shape, BF),
            pltpu.VMEM(weight_two.shape, BF),
            pltpu.SemaphoreType.DMA((2,)),
        ],
        hbm=(0, 1),
        flops=2 * 64 * 864 * 1728,
    )
    wide = planes + 2 * HALO
    send_a, send_b = call(
        edge_kernel,
        [((wide, edge, breadth), BF), ((wide, edge, breadth), BF)],
        turned,
        got_far,
        got_mate,
        p_sel,
    )
    got_b = lax.ppermute(send_b, ("gx", "yz"), yz_pairs(gx, yz, True))
    got_a = lax.ppermute(send_a, ("gx", "yz"), yz_pairs(gx, yz, False))
    pairs = 2 * PLANES + 2
    out_rows = weight_three.shape[0] // yz
    partial1, partial2, picked = call(
        inner_kernel,
        [
            ((2, pairs, 4 * c2, 2 * breadth), F32),
            ((4 * c3, 2 * PLANES * breadth), F32),
            ((9 * out_rows, 3 * c3), F32),
        ],
        turned,
        got_mate,
        got_far,
        lower1,
        upper1,
        middle2,
        weight_three.T,
        scratch=[
            pltpu.VMEM((wide, 3 * rows, breadth), BF),
            pltpu.VMEM(weight_three.shape[::-1], BF),
            pltpu.SemaphoreType.DMA,
        ],
        hbm=(6,),
        flops=2 * 300_000_000,
    )
    (tile,) = call(
        outer_kernel,
        [((c3, breadth), BF)],
        got_a,
        got_b,
        partial1,
        partial2,
        lower1,
        upper1,
        outer2,
        p_sel,
        scratch=[pltpu.VMEM((wide, 3 * edge, breadth), BF), pltpu.VMEM((wide, 3 * edge, breadth), BF)],
        flops=2 * 400_000_000,
    )
    tiles = [tile] + [lax.ppermute(tile, "yz", [(i, i ^ d) for i in range(yz)]) for d in range(1, yz)]
    cells = yz * (height // 4) * (breadth // 4)
    z = breadth // 4
    mate, far = call(lay_kernel, [((c3, cells), BF), ((c3 + 16, cells), BF)], tiles[0], *[tiles[d] for d in [3, 2, 1]])
    got_far = lax.ppermute(far, ("gx", "yz"), away)
    got_mate = lax.ppermute(mate, ("gx", "yz"), near)
    shape = (out_rows, 2, cells)
    plane, weights = ((out_rows, cells), F32), ((9 * out_rows, c3), BF)
    beside_mate, beside_far, w_mate, w_far = call(
        functools.partial(middle_kernel, z),
        [plane, plane, weights, weights],
        mate,
        far,
        picked,
        flops=2 * 32 * 1152 * 512,
    )
    block = [pltpu.VMEM(shape, BF), pltpu.SemaphoreType.DMA]
    out, ready = call(
        functools.partial(near_kernel, z),
        [(shape, BF), plane],
        beside_mate,
        beside_far,
        w_mate,
        got_mate,
        scratch=block,
        hbm_out=True,
        free=True,
    )
    (out,) = call(
        functools.partial(far_kernel, z),
        [(shape, BF)],
        got_far,
        w_far,
        ready,
        beside_far,
        out,
        scratch=block,
        hbm=(4,),
        hbm_out=True,
        aliases={4: 0},
        flops=2 * 32 * 576 * 256,
    )
    return out


def solution(mesh):
    placed = (P("gx", None, "yz", None), P(), P(), P())
    return jax.shard_map(
        per_device, mesh=mesh, in_specs=placed, out_specs=P("yz", "gx", None), check_vma=False
    )
```

```python
import functools

import jax
import jax.numpy as jnp
from jax import lax
from jax.experimental import pallas as pl
from jax.experimental.pallas import tpu as pltpu
from jax.sharding import PartitionSpec as P

BF = jnp.bfloat16
F32 = jnp.float32
PLANES = 2
HALO = 2 * PLANES - 1
EDGE = 3


def mat(a, b):
    return jnp.dot(a, b, preferred_element_type=F32)


def relu(a):
    return jnp.maximum(a, 0.0)


def iota(shape, dim):
    return lax.broadcasted_iota(jnp.int32, shape, dim)


def call(body, outs, *args, scratch=(), flops=0, free=False, hbm=(), hbm_out=False, aliases={}):
    moved = 0 if free else sum(a.size * a.dtype.itemsize for a in args)
    args = [pltpu.with_memory_space_constraint(a, pltpu.HBM) if i in hbm else a for i, a in enumerate(args)]
    return pl.pallas_call(
        body,
        out_shape=[jax.ShapeDtypeStruct(s, d) for s, d in outs],
        in_specs=[pl.BlockSpec(memory_space=pltpu.HBM if i in hbm else pltpu.VMEM) for i in range(len(args))],
        out_specs=[pl.BlockSpec(memory_space=pltpu.HBM if hbm_out and i == 0 else pltpu.VMEM) for i in range(len(outs))],
        scratch_shapes=list(scratch),
        input_output_aliases=aliases,
        compiler_params=pltpu.CompilerParams(vmem_limit_bytes=40 * 1024 * 1024),
        cost_estimate=pl.CostEstimate(flops=flops, bytes_accessed=moved, transcendentals=0),
    )(*args)


def turn_kernel(vol, turned, send_mate, send_far):
    planes, chans, height, breadth = vol.shape
    rows = chans * height
    dest = iota((rows, rows), 0)
    source = (dest & (chans - 1)) * height + dest // chans
    swap = (iota((rows, rows), 1) == source).astype(F32).astype(BF)
    for x in range(planes):
        turned[x] = mat(swap, vol[x].reshape(rows, breadth)).astype(BF)
    even = is_even("gx")
    for out, first in (
        (send_mate, jnp.where(even, planes - HALO, 0)),
        (send_far, jnp.where(even, 0, planes - HALO)),
    ):
        for x in range(HALO):
            out[x] = turned[first + x]


def yz_pairs(gx, yz, second):
    pairs = []
    for g in range(gx):
        for k in range(yz):
            if not second:
                pairs.append((g * yz + k, g * yz + (k ^ 1)))
            elif k in (0, yz - 1):
                pairs.append((g * yz + k, (g ^ 1) * yz + k))
            else:
                pairs.append((g * yz + k, g * yz + (k + 1 if k % 2 else k - 1)))
    return pairs


def gx_pairs(gx, yz, far):
    pairs = []
    for g in range(gx):
        for k in range(yz):
            if not far:
                pairs.append((g * yz + k, (g ^ 1) * yz + k))
            elif g in (0, gx - 1):
                pairs.append((g * yz + k, g * yz + (k ^ 1)))
            else:
                pairs.append((g * yz + k, (g + 1 if g % 2 else g - 1) * yz + k))
    return pairs


def is_even(axis):
    return lax.rem(lax.axis_index(axis), 2) == 0


def from_sides(mate, far, even, no_low, no_high):
    zero = jnp.zeros_like(mate)
    low = jnp.where(no_low, zero, jnp.where(even, far, mate))
    high = jnp.where(no_high, zero, jnp.where(even, mate, far))
    return low, high


def all_planes(turned, got_mate, got_far):
    g = lax.axis_index("gx")
    even, first, last = is_even("gx"), g == 0, g == lax.axis_size("gx") - 1
    sides = [from_sides(got_mate[x], got_far[x], even, first, last) for x in range(HALO)]
    return [low for low, _ in sides] + [turned[x] for x in range(turned.shape[0])] + [high for _, high in sides]


def edge_kernel(turned, got_far, got_mate, _, send_a, send_b):
    edge = send_a.shape[1]
    even = is_even("yz")
    for x, t in enumerate(all_planes(turned, got_mate, got_far)):
        low, high = t[:edge], t[t.shape[0] - edge :]
        send_a[x] = jnp.where(even, high, low)
        send_b[x] = jnp.where(even, low, high)


def weights_kernel(w1_hbm, w2_hbm, lower1, upper1, middle2, outer2, p_sel, w1, w2, sems):
    loads = [pltpu.make_async_copy(a, b, sems.at[i]) for i, (a, b) in enumerate(((w1_hbm, w1), (w2_hbm, w2)))]
    for load in loads:
        load.start()

    rows, columns = p_sel.shape
    z = rows // 4
    r, c = iota(p_sel.shape, 0), iota(p_sel.shape, 1)
    hit = (r // (2 * z) == (c // (z // 4)) % 2) & ((r // z) % 2 == c // (z // 2))
    hit = hit & ((r & (z - 1)) == 4 * (c & (z // 4 - 1)))
    p_sel[...] = jnp.where(hit, 1.0, 0.0).astype(BF)

    for load in loads:
        load.wait()
    for w, bands in (
        (w1, ((lower1, lambda y: (0, 1, 2)), (upper1, lambda y: (3, 4, 5)))),
        (w2, ((middle2, lambda y: (2, 3)), (outer2, lambda y: (0, 1) if y < 2 else (4, 5)))),
    ):
        out_rows, width = w.shape[0], w.shape[1] // 9
        taps = w[...].astype(F32)
        zero = jnp.zeros((out_rows, width), F32)
        for band, window in bands:
            for y in range(4):
                pieces = []
                for a in range(3):
                    for row in window(y):
                        first = (3 * a + row - y) * width
                        pieces.append(taps[:, first : first + width] if 0 <= row - y < 3 else zero)
                band[out_rows * y : out_rows * (y + 1)] = jnp.concatenate(pieces, 1).astype(BF)


def put_taps(dest, t, chans):
    breadth = t.shape[1]
    lane = iota((1, breadth), 1)
    wide = t.astype(F32)
    before = jnp.where(lane == 0, 0.0, pltpu.roll(wide, 1, 1)).astype(BF)
    after = jnp.where(lane == breadth - 1, 0.0, pltpu.roll(wide, breadth - 1, 1)).astype(BF)
    for y in range(t.shape[0] // chans):
        for tap, value in enumerate((before, t, after)):
            row = (3 * y + tap) * chans
            dest[row : row + chans] = value[y * chans : (y + 1) * chans]


def three(taps, e, first, rows):
    return jnp.concatenate([taps[e + a, first : first + rows] for a in range(3)], 0)


def two_cells(taps, j, first, rows):
    return jnp.concatenate([three(taps, 2 * j, first, rows), three(taps, 2 * j + 1, first, rows)], 1)


def pool_first(acc, j, pairs, no_low, no_high):
    g = lax.axis_index("gx")
    breadth = acc.shape[1] // 2
    width = acc.shape[0] // 4
    r = relu(acc)
    s = r[:, :breadth] + r[:, breadth:]
    halves = []
    for y, drop in enumerate((no_low, no_high)):
        t = s[2 * y * width : (2 * y + 1) * width] + s[(2 * y + 1) * width : (2 * y + 2) * width]
        t = (t + pltpu.roll(t, breadth - 1, 1)) * 0.125
        if j < PLANES - 1:
            drop = drop | (g == 0)
        if j > pairs - PLANES:
            drop = drop | (g == lax.axis_size("gx") - 1)
        halves.append(t if drop is False else jnp.where(drop, 0.0, t))
    return pooled_taps(jnp.concatenate(halves, 0))


def pooled_taps(t):
    breadth = t.shape[1]
    lane = iota((1, breadth), 1)
    before = jnp.where(lane < 2, 0.0, pltpu.roll(t, 2, 1)).astype(BF)
    after = jnp.where(lane >= breadth - 2, 0.0, pltpu.roll(t, breadth - 2, 1)).astype(BF)
    chans = t.shape[0] // 2
    rows = [slice(y * chans, (y + 1) * chans) for y in range(2)]
    return jnp.concatenate([u[r] for r in rows for u in (before, t.astype(BF), after)], 0)


def second_taps(planes):
    return jnp.concatenate([jnp.concatenate(planes[x : x + 3], 0) for x in range(len(planes) - 2)], 1)


def inner_kernel(
    turned, got_mate, got_far, lower1, upper1, middle2, w3_hbm, partial1, partial2, picked, taps, w3, sem
):
    load = pltpu.make_async_copy(w3_hbm, w3, sem)
    load.start()
    chans = lower1.shape[1] // 27
    for e, t in enumerate(all_planes(turned, got_mate, got_far)):
        put_taps(taps.at[e], t, chans)
    pairs = partial1.shape[1]
    width = lower1.shape[0] // 4
    lower, upper = lower1[: 3 * width], upper1[width:]
    step = 3 * chans
    pooled = []
    zero = jnp.zeros((width, partial1.shape[3]), F32)
    for j in range(pairs):
        partial1[0, j, :width] = zero
        partial1[0, j, width:] = mat(upper, two_cells(taps, j, 0, 3 * step))
        partial1[1, j, : 3 * width] = mat(lower, two_cells(taps, j, 5 * step, 3 * step))
        partial1[1, j, 3 * width :] = zero
        a = mat(lower, two_cells(taps, j, step, 3 * step))
        b = mat(upper, two_cells(taps, j, 4 * step, 3 * step))
        acc = jnp.concatenate([a[:width], a[width:] + b[: 2 * width], b[2 * width :]], 0)
        pooled.append(pool_first(acc, j, pairs, False, False))
    partial2[...] = mat(middle2[...], second_taps(pooled))
    load.wait()
    out_rows = picked.shape[0] // 9
    own = (out_rows, w3.shape[1])
    first = lax.axis_index("yz") * out_rows
    pick = (iota(own, 1) == iota(own, 0) + first).astype(F32).astype(BF)
    own3 = lax.dot_general(pick, w3[...], (((1,), (1,)), ((), ())), preferred_element_type=F32)
    depth = picked.shape[1] // 3
    for tap in range(9):
        pieces = [own3[:, (9 * a + tap) * depth : (9 * a + tap + 1) * depth] for a in range(3)]
        picked[tap * out_rows : (tap + 1) * out_rows] = jnp.concatenate(pieces, 1)


def outer_kernel(got_a, got_b, partial1, partial2, lower1, upper1, outer2, p_sel, out, low_taps, high_taps):
    planes, edge, breadth = got_a.shape
    chans = edge // EDGE
    k = lax.axis_index("yz")
    even, first, last = is_even("yz"), k == 0, k == lax.axis_size("yz") - 1
    for e in range(planes):
        low, high = from_sides(got_a[e], got_b[e], even, first, last)
        put_taps(low_taps.at[e], low, chans)
        put_taps(high_taps.at[e], high, chans)
    pairs = partial1.shape[1]
    width = lower1.shape[0] // 4
    lower, upper = lower1[: 3 * width], upper1[width:]
    rows = 3 * edge
    below, above = [], []
    lows = [mat(lower, two_cells(low_taps, j, 0, rows)) for j in range(pairs)]
    highs = [mat(upper, two_cells(high_taps, j, 0, rows)) for j in range(pairs)]
    for j in range(pairs):
        p = partial1[0, j]
        below.append(pool_first(jnp.concatenate([p[: 3 * width] + lows[j], p[3 * width :]], 0), j, pairs, first, False))
        p = partial1[1, j]
        above.append(pool_first(jnp.concatenate([p[:width], p[width:] + highs[j]], 0), j, pairs, False, last))
    width = outer2.shape[0] // 4
    sums = [mat(outer2[2 * y * width : 2 * (y + 1) * width], second_taps(p)) for y, p in enumerate((below, above))]
    halves = []
    for y in range(2):
        r = relu(partial2[2 * y * width : 2 * (y + 1) * width] + sums[y])
        t = r[:width] + r[width:]
        t = [t[:, 2 * x * breadth : (2 * x + 1) * breadth] + t[:, (2 * x + 1) * breadth : 2 * (x + 1) * breadth] for x in range(PLANES)]
        halves.append([((u + pltpu.roll(u, breadth - 2, 1)) * 0.125).astype(BF) for u in t])
    out[...] = mat(jnp.concatenate(halves[0] + halves[1], 1), p_sel[...]).astype(BF)


def lay(tiles, rows):
    even = is_even("yz")
    half = tiles[0].shape[1] // 2
    lane = iota((1, 2 * half), 1)
    tiles = [tiles[i] for i in [0, 3, 2, 1]]
    low, high = [], []
    for m in range(len(tiles) // 2):
        a, b = tiles[2 * m][rows].astype(F32), tiles[2 * m + 1][rows].astype(F32)
        first, second = jnp.where(even, a, b), jnp.where(even, b, a)
        low.append(jnp.where(lane < half, first, pltpu.roll(second, half, 1)))
        high.append(jnp.where(lane < half, pltpu.roll(first, half, 1), second))
    return low, high


def put_plane(dest, blocks):
    wide = blocks[0].shape[1]
    k = lax.axis_index("yz")
    for m, block in enumerate(blocks):
        dest[: block.shape[0], pl.ds(pl.multiple_of((lax.div(k, 2) ^ m) * wide, wide), wide)] = block.astype(BF)


def lay_kernel(*refs):
    tiles, (mate, far) = refs[:-2], refs[-2:]
    low, high = lay(tiles, slice(None))
    even = is_even("gx")
    put_plane(mate, [jnp.where(even, b, a) for a, b in zip(low, high)])
    put_plane(far, [jnp.where(even, a, b) for a, b in zip(low, high)])
    depth = mate.shape[0]
    far[depth:] = jnp.zeros((far.shape[0] - depth, far.shape[1]), BF)


def shift_taps(products, z):
    rows, cells = products.shape[0] // 9, products.shape[1]
    lane = iota((1, cells), 1)
    depth = lane & (z - 1)
    total = None
    for b in range(3):
        one = [products[(3 * b + c) * rows : (3 * b + c + 1) * rows] for c in range(3)]
        t = one[1] + jnp.where(depth == 0, 0.0, pltpu.roll(one[0], 1, 1))
        t = t + jnp.where(depth == z - 1, 0.0, pltpu.roll(one[2], cells - 1, 1))
        if b == 0:
            t = jnp.where(lane < z, 0.0, pltpu.roll(t, z, 1))
        if b == 2:
            t = jnp.where(lane >= cells - z, 0.0, pltpu.roll(t, cells - z, 1))
        total = t if total is None else total + t
    return total


def middle_kernel(z, mate, far, w3, beside_mate, beside_far, w_mate, w_far):
    depth = mate.shape[0]
    even = is_even("gx")
    a, b = mate[...], far[:depth]
    both = jnp.concatenate([jnp.where(even, b, a), jnp.where(even, a, b)], 0)
    w = w3[...].astype(BF)
    first, second = w[:, depth:], w[:, : 2 * depth]
    beside_mate[...] = shift_taps(mat(jnp.where(even, second, first), both), z)
    beside_far[...] = shift_taps(mat(jnp.where(even, first, second), both), z)
    w_mate[...] = jnp.where(even, w[:, 2 * depth :], w[:, :depth])
    w_far[...] = jnp.where(even, w[:, :depth], w[:, 2 * depth :])


def is_end():
    g = lax.axis_index("gx")
    return (g == 0) | (g == lax.axis_size("gx") - 1)


def write_planes(beside_mate, beside_far, out, block, sem):
    even = is_even("gx")
    a, b = relu(beside_mate), relu(beside_far)
    rows, cells = a.shape
    pair = jnp.concatenate([jnp.where(even, b, a), jnp.where(even, a, b)], 1)
    block[...] = pair.astype(BF).reshape(rows, 2, cells)
    copy = pltpu.make_async_copy(block, out, sem)
    copy.start()
    copy.wait()


def near_kernel(z, beside_mate, beside_far, w_mate, got_mate, out, ready, block, sem):
    ready[...] = beside_mate[...] + shift_taps(mat(w_mate[...], got_mate[...]), z)

    @pl.when(is_end())
    def _():
        write_planes(ready[...], beside_far[...], out, block, sem)


def far_kernel(z, got_far, w_far, ready, beside_far, _, out, block, sem):
    @pl.when(jnp.logical_not(is_end()))
    def _():
        part = beside_far[...] + shift_taps(mat(w_far[...], got_far[: w_far.shape[1]]), z)
        write_planes(ready[...], part, out, block, sem)


def per_device(volume, weight_one, weight_two, weight_three):
    gx, yz = lax.axis_size("gx"), lax.axis_size("yz")
    planes, chans, height, breadth = volume.shape
    rows = chans * height
    edge = EDGE * chans
    c2, c3 = weight_one.shape[0], weight_two.shape[0]

    turned, send_mate, send_far = call(
        turn_kernel,
        [((planes, rows, breadth), BF), ((HALO, rows, breadth), BF), ((HALO, rows, breadth), BF)],
        volume,
    )
    near, away = gx_pairs(gx, yz, False), gx_pairs(gx, yz, True)
    got_mate = lax.ppermute(send_mate, ("gx", "yz"), near)
    got_far = lax.ppermute(send_far, ("gx", "yz"), away)
    k1, k2 = 27 * chans, 27 * c2
    lower1, upper1, middle2, outer2, p_sel = call(
        weights_kernel,
        [
            ((4 * c2, k1), BF),
            ((4 * c2, k1), BF),
            ((4 * c3, 2 * k2 // 3), BF),
            ((4 * c3, 2 * k2 // 3), BF),
            ((4 * breadth, breadth), BF),
        ],
        weight_one,
        weight_two,
        scratch=[
            pltpu.VMEM(weight_one.shape, BF),
            pltpu.VMEM(weight_two.shape, BF),
            pltpu.SemaphoreType.DMA((2,)),
        ],
        hbm=(0, 1),
        flops=2 * 64 * 864 * 1728,
    )
    wide = planes + 2 * HALO
    send_a, send_b = call(
        edge_kernel,
        [((wide, edge, breadth), BF), ((wide, edge, breadth), BF)],
        turned,
        got_far,
        got_mate,
        p_sel,
    )
    got_b = lax.ppermute(send_b, ("gx", "yz"), yz_pairs(gx, yz, True))
    got_a = lax.ppermute(send_a, ("gx", "yz"), yz_pairs(gx, yz, False))
    pairs = 2 * PLANES + 2
    out_rows = weight_three.shape[0] // yz
    partial1, partial2, picked = call(
        inner_kernel,
        [
            ((2, pairs, 4 * c2, 2 * breadth), F32),
            ((4 * c3, 2 * PLANES * breadth), F32),
            ((9 * out_rows, 3 * c3), F32),
        ],
        turned,
        got_mate,
        got_far,
        lower1,
        upper1,
        middle2,
        weight_three.T,
        scratch=[
            pltpu.VMEM((wide, 3 * rows, breadth), BF),
            pltpu.VMEM(weight_three.shape[::-1], BF),
            pltpu.SemaphoreType.DMA,
        ],
        hbm=(6,),
        flops=2 * 300_000_000,
    )
    (tile,) = call(
        outer_kernel,
        [((c3, breadth), BF)],
        got_a,
        got_b,
        partial1,
        partial2,
        lower1,
        upper1,
        outer2,
        p_sel,
        scratch=[pltpu.VMEM((wide, 3 * edge, breadth), BF), pltpu.VMEM((wide, 3 * edge, breadth), BF)],
        flops=2 * 400_000_000,
    )
    tiles = [tile] + [lax.ppermute(tile, "yz", [(i, i ^ d) for i in range(yz)]) for d in range(1, yz)]
    cells = yz * (height // 4) * (breadth // 4)
    z = breadth // 4
    mate, far = call(lay_kernel, [((c3, cells), BF), ((c3 + 16, cells), BF)], tiles[0], *[tiles[d] for d in [3, 2, 1]])
    got_far = lax.ppermute(far, ("gx", "yz"), away)
    got_mate = lax.ppermute(mate, ("gx", "yz"), near)
    shape = (out_rows, 2, cells)
    plane, weights = ((out_rows, cells), F32), ((9 * out_rows, c3), BF)
    beside_mate, beside_far, w_mate, w_far = call(
        functools.partial(middle_kernel, z),
        [plane, plane, weights, weights],
        mate,
        far,
        picked,
        flops=2 * 32 * 1152 * 512,
    )
    block = [pltpu.VMEM(shape, BF), pltpu.SemaphoreType.DMA]
    out, ready = call(
        functools.partial(near_kernel, z),
        [(shape, BF), plane],
        beside_mate,
        beside_far,
        w_mate,
        got_mate,
        scratch=block,
        hbm_out=True,
        free=True,
    )
    (out,) = call(
        functools.partial(far_kernel, z),
        [(shape, BF)],
        got_far,
        w_far,
        ready,
        beside_far,
        out,
        scratch=block,
        hbm=(4,),
        hbm_out=True,
        aliases={4: 0},
        flops=2 * 32 * 576 * 256,
    )
    return out


def solution(mesh):
    placed = (P("gx", None, "yz", None), P(), P(), P())
    return jax.shard_map(
        per_device, mesh=mesh, in_specs=placed, out_specs=P("yz", "gx", None), check_vma=False
    )
```

```python
import functools

import jax
import jax.numpy as jnp
from jax import lax
from jax.experimental import pallas as pl
from jax.experimental.pallas import tpu as pltpu
from jax.sharding import PartitionSpec as P

BF = jnp.bfloat16
F32 = jnp.float32
PLANES = 2
HALO = 2 * PLANES - 1
EDGE = 3


def mat(a, b):
    return jnp.dot(a, b, preferred_element_type=F32)


def relu(a):
    return jnp.maximum(a, 0.0)


def iota(shape, dim):
    return lax.broadcasted_iota(jnp.int32, shape, dim)


def call(body, outs, *args, scratch=(), flops=0, free=False, hbm=(), hbm_out=False, aliases={}):
    moved = 0 if free else sum(a.size * a.dtype.itemsize for a in args)
    args = [pltpu.with_memory_space_constraint(a, pltpu.HBM) if i in hbm else a for i, a in enumerate(args)]
    return pl.pallas_call(
        body,
        out_shape=[jax.ShapeDtypeStruct(s, d) for s, d in outs],
        in_specs=[pl.BlockSpec(memory_space=pltpu.HBM if i in hbm else pltpu.VMEM) for i in range(len(args))],
        out_specs=[pl.BlockSpec(memory_space=pltpu.HBM if hbm_out and i == 0 else pltpu.VMEM) for i in range(len(outs))],
        scratch_shapes=list(scratch),
        input_output_aliases=aliases,
        compiler_params=pltpu.CompilerParams(vmem_limit_bytes=40 * 1024 * 1024),
        cost_estimate=pl.CostEstimate(flops=flops, bytes_accessed=moved, transcendentals=0),
    )(*args)


def planes_kernel(volume, send_mate, send_far, sems):
    planes = volume.shape[0]
    even = is_even("gx")
    copies = []
    for i, (out, first) in enumerate(
        ((send_far, jnp.where(even, 0, planes - HALO)), (send_mate, jnp.where(even, planes - HALO, 0)))
    ):
        copies.append(pltpu.make_async_copy(volume.at[pl.ds(first, HALO)], out, sems.at[i]))
    for copy in copies:
        copy.start()
    for copy in copies:
        copy.wait()


def turn(swap, plane):
    rows, breadth = swap.shape[0], plane.shape[-1]
    return mat(swap, plane.reshape(rows, breadth)).astype(BF)


def yz_pairs(gx, yz, second):
    pairs = []
    for g in range(gx):
        for k in range(yz):
            if not second:
                pairs.append((g * yz + k, g * yz + (k ^ 1)))
            elif k in (0, yz - 1):
                pairs.append((g * yz + k, (g ^ 1) * yz + k))
            else:
                pairs.append((g * yz + k, g * yz + (k + 1 if k % 2 else k - 1)))
    return pairs


def gx_pairs(gx, yz, far):
    pairs = []
    for g in range(gx):
        for k in range(yz):
            if not far:
                pairs.append((g * yz + k, (g ^ 1) * yz + k))
            elif g in (0, gx - 1):
                pairs.append((g * yz + k, g * yz + (k ^ 1)))
            else:
                pairs.append((g * yz + k, (g + 1 if g % 2 else g - 1) * yz + k))
    return pairs


def is_even(axis):
    return lax.rem(lax.axis_index(axis), 2) == 0


def from_sides(mate, far, even, no_low, no_high):
    zero = jnp.zeros_like(mate)
    low = jnp.where(no_low, zero, jnp.where(even, far, mate))
    high = jnp.where(no_high, zero, jnp.where(even, mate, far))
    return low, high


def all_planes(turned, got_mate, got_far):
    g = lax.axis_index("gx")
    even, first, last = is_even("gx"), g == 0, g == lax.axis_size("gx") - 1
    sides = [from_sides(got_mate[x], got_far[x], even, first, last) for x in range(HALO)]
    return [low for low, _ in sides] + [turned[x] for x in range(turned.shape[0])] + [high for _, high in sides]


def edge_kernel(raw_far, raw_mate, turned, swap, _, send_a, send_b, got_far, got_mate):
    for x in range(HALO):
        got_far[x] = turn(swap[...], raw_far[x])
        got_mate[x] = turn(swap[...], raw_mate[x])
    edge = send_a.shape[1]
    even = is_even("yz")
    for x, t in enumerate(all_planes(turned, got_mate, got_far)):
        low, high = t[:edge], t[t.shape[0] - edge :]
        send_a[x] = jnp.where(even, high, low)
        send_b[x] = jnp.where(even, low, high)


def weights_kernel(volume, w1_hbm, w2_hbm, lower1, upper1, middle2, outer2, p_sel, swap, turned, vol, w1, w2, sems):
    pairs = ((w1_hbm, w1), (w2_hbm, w2), (volume, vol))
    loads = [pltpu.make_async_copy(a, b, sems.at[i]) for i, (a, b) in enumerate(pairs)]
    for load in loads:
        load.start()

    rows, columns = p_sel.shape
    z = rows // 4
    r, c = iota(p_sel.shape, 0), iota(p_sel.shape, 1)
    hit = (r // (2 * z) == (c // (z // 4)) % 2) & ((r // z) % 2 == c // (z // 2))
    hit = hit & ((r & (z - 1)) == 4 * (c & (z // 4 - 1)))
    p_sel[...] = jnp.where(hit, 1.0, 0.0).astype(BF)

    planes, chans, height, breadth = vol.shape
    dest = iota(swap.shape, 0)
    source = (dest & (chans - 1)) * height + dest // chans
    swap[...] = (iota(swap.shape, 1) == source).astype(F32).astype(BF)

    for load in loads:
        load.wait()
    for x in range(planes):
        turned[x] = turn(swap[...], vol[x])
    for w, bands in (
        (w1, ((lower1, lambda y: (0, 1, 2)), (upper1, lambda y: (3, 4, 5)))),
        (w2, ((middle2, lambda y: (2, 3)), (outer2, lambda y: (0, 1) if y < 2 else (4, 5)))),
    ):
        out_rows, width = w.shape[0], w.shape[1] // 9
        taps = w[...].astype(F32)
        zero = jnp.zeros((out_rows, width), F32)
        for band, window in bands:
            for y in range(4):
                pieces = []
                for a in range(3):
                    for row in window(y):
                        first = (3 * a + row - y) * width
                        pieces.append(taps[:, first : first + width] if 0 <= row - y < 3 else zero)
                band[out_rows * y : out_rows * (y + 1)] = jnp.concatenate(pieces, 1).astype(BF)


def put_taps(dest, t, chans):
    breadth = t.shape[1]
    lane = iota((1, breadth), 1)
    wide = t.astype(F32)
    before = jnp.where(lane == 0, 0.0, pltpu.roll(wide, 1, 1)).astype(BF)
    after = jnp.where(lane == breadth - 1, 0.0, pltpu.roll(wide, breadth - 1, 1)).astype(BF)
    for y in range(t.shape[0] // chans):
        for tap, value in enumerate((before, t, after)):
            row = (3 * y + tap) * chans
            dest[row : row + chans] = value[y * chans : (y + 1) * chans]


def three(taps, e, first, rows):
    return jnp.concatenate([taps[e + a, first : first + rows] for a in range(3)], 0)


def two_cells(taps, j, first, rows):
    return jnp.concatenate([three(taps, 2 * j, first, rows), three(taps, 2 * j + 1, first, rows)], 1)


def pool_first(acc, j, pairs, no_low, no_high):
    g = lax.axis_index("gx")
    breadth = acc.shape[1] // 2
    width = acc.shape[0] // 4
    r = relu(acc)
    s = r[:, :breadth] + r[:, breadth:]
    halves = []
    for y, drop in enumerate((no_low, no_high)):
        t = s[2 * y * width : (2 * y + 1) * width] + s[(2 * y + 1) * width : (2 * y + 2) * width]
        t = (t + pltpu.roll(t, breadth - 1, 1)) * 0.125
        if j < PLANES - 1:
            drop = drop | (g == 0)
        if j > pairs - PLANES:
            drop = drop | (g == lax.axis_size("gx") - 1)
        halves.append(t if drop is False else jnp.where(drop, 0.0, t))
    return pooled_taps(jnp.concatenate(halves, 0))


def pooled_taps(t):
    breadth = t.shape[1]
    lane = iota((1, breadth), 1)
    before = jnp.where(lane < 2, 0.0, pltpu.roll(t, 2, 1)).astype(BF)
    after = jnp.where(lane >= breadth - 2, 0.0, pltpu.roll(t, breadth - 2, 1)).astype(BF)
    chans = t.shape[0] // 2
    rows = [slice(y * chans, (y + 1) * chans) for y in range(2)]
    return jnp.concatenate([u[r] for r in rows for u in (before, t.astype(BF), after)], 0)


def second_taps(planes):
    return jnp.concatenate([jnp.concatenate(planes[x : x + 3], 0) for x in range(len(planes) - 2)], 1)


def inner_kernel(
    turned, got_mate, got_far, lower1, upper1, middle2, w3_hbm, partial1, partial2, picked, taps, w3, sem
):
    load = pltpu.make_async_copy(w3_hbm, w3, sem)
    load.start()
    chans = lower1.shape[1] // 27
    for e, t in enumerate(all_planes(turned, got_mate, got_far)):
        put_taps(taps.at[e], t, chans)
    pairs = partial1.shape[1]
    width = lower1.shape[0] // 4
    lower, upper = lower1[: 3 * width], upper1[width:]
    step = 3 * chans
    pooled = []
    zero = jnp.zeros((width, partial1.shape[3]), F32)
    for j in range(pairs):
        partial1[0, j, :width] = zero
        partial1[0, j, width:] = mat(upper, two_cells(taps, j, 0, 3 * step))
        partial1[1, j, : 3 * width] = mat(lower, two_cells(taps, j, 5 * step, 3 * step))
        partial1[1, j, 3 * width :] = zero
        a = mat(lower, two_cells(taps, j, step, 3 * step))
        b = mat(upper, two_cells(taps, j, 4 * step, 3 * step))
        acc = jnp.concatenate([a[:width], a[width:] + b[: 2 * width], b[2 * width :]], 0)
        pooled.append(pool_first(acc, j, pairs, False, False))
    partial2[...] = mat(middle2[...], second_taps(pooled))
    load.wait()
    out_rows = picked.shape[0] // 9
    own = (out_rows, w3.shape[1])
    first = lax.axis_index("yz") * out_rows
    pick = (iota(own, 1) == iota(own, 0) + first).astype(F32).astype(BF)
    own3 = lax.dot_general(pick, w3[...], (((1,), (1,)), ((), ())), preferred_element_type=F32)
    depth = picked.shape[1] // 3
    for tap in range(9):
        pieces = [own3[:, (9 * a + tap) * depth : (9 * a + tap + 1) * depth] for a in range(3)]
        picked[tap * out_rows : (tap + 1) * out_rows] = jnp.concatenate(pieces, 1)


def outer_kernel(got_a, got_b, partial1, partial2, lower1, upper1, outer2, p_sel, out, low_taps, high_taps):
    planes, edge, breadth = got_a.shape
    chans = edge // EDGE
    k = lax.axis_index("yz")
    even, first, last = is_even("yz"), k == 0, k == lax.axis_size("yz") - 1
    for e in range(planes):
        low, high = from_sides(got_a[e], got_b[e], even, first, last)
        put_taps(low_taps.at[e], low, chans)
        put_taps(high_taps.at[e], high, chans)
    pairs = partial1.shape[1]
    width = lower1.shape[0] // 4
    lower, upper = lower1[: 3 * width], upper1[width:]
    rows = 3 * edge
    below, above = [], []
    lows = [mat(lower, two_cells(low_taps, j, 0, rows)) for j in range(pairs)]
    highs = [mat(upper, two_cells(high_taps, j, 0, rows)) for j in range(pairs)]
    for j in range(pairs):
        p = partial1[0, j]
        below.append(pool_first(jnp.concatenate([p[: 3 * width] + lows[j], p[3 * width :]], 0), j, pairs, first, False))
        p = partial1[1, j]
        above.append(pool_first(jnp.concatenate([p[:width], p[width:] + highs[j]], 0), j, pairs, False, last))
    width = outer2.shape[0] // 4
    sums = [mat(outer2[2 * y * width : 2 * (y + 1) * width], second_taps(p)) for y, p in enumerate((below, above))]
    halves = []
    for y in range(2):
        r = relu(partial2[2 * y * width : 2 * (y + 1) * width] + sums[y])
        t = r[:width] + r[width:]
        t = [t[:, 2 * x * breadth : (2 * x + 1) * breadth] + t[:, (2 * x + 1) * breadth : 2 * (x + 1) * breadth] for x in range(PLANES)]
        halves.append([((u + pltpu.roll(u, breadth - 2, 1)) * 0.125).astype(BF) for u in t])
    out[...] = mat(jnp.concatenate(halves[0] + halves[1], 1), p_sel[...]).astype(BF)


def lay(tiles, rows):
    even = is_even("yz")
    half = tiles[0].shape[1] // 2
    lane = iota((1, 2 * half), 1)
    tiles = [tiles[i] for i in [0, 1, 2, 3]]
    low, high = [], []
    for m in range(len(tiles) // 2):
        a, b = tiles[2 * m][rows].astype(F32), tiles[2 * m + 1][rows].astype(F32)
        first, second = jnp.where(even, a, b), jnp.where(even, b, a)
        low.append(jnp.where(lane < half, first, pltpu.roll(second, half, 1)))
        high.append(jnp.where(lane < half, pltpu.roll(first, half, 1), second))
    return low, high


def put_plane(dest, blocks):
    wide = blocks[0].shape[1]
    k = lax.axis_index("yz")
    for m, block in enumerate(blocks):
        dest[: block.shape[0], pl.ds(pl.multiple_of((lax.div(k, 2) ^ m) * wide, wide), wide)] = block.astype(BF)


def lay_kernel(*refs):
    tiles, (mate, far) = refs[:-2], refs[-2:]
    low, high = lay(tiles, slice(None))
    even = is_even("gx")
    put_plane(mate, [jnp.where(even, b, a) for a, b in zip(low, high)])
    put_plane(far, [jnp.where(even, a, b) for a, b in zip(low, high)])
    depth = mate.shape[0]
    far[depth:] = jnp.zeros((far.shape[0] - depth, far.shape[1]), BF)


def shift_taps(products, z):
    rows, cells = products.shape[0] // 9, products.shape[1]
    lane = iota((1, cells), 1)
    depth = lane & (z - 1)
    total = None
    for b in range(3):
        one = [products[(3 * b + c) * rows : (3 * b + c + 1) * rows] for c in range(3)]
        t = one[1] + jnp.where(depth == 0, 0.0, pltpu.roll(one[0], 1, 1))
        t = t + jnp.where(depth == z - 1, 0.0, pltpu.roll(one[2], cells - 1, 1))
        if b == 0:
            t = jnp.where(lane < z, 0.0, pltpu.roll(t, z, 1))
        if b == 2:
            t = jnp.where(lane >= cells - z, 0.0, pltpu.roll(t, cells - z, 1))
        total = t if total is None else total + t
    return total


def middle_kernel(z, mate, far, w3, beside_mate, beside_far, w_mate, w_far):
    depth = mate.shape[0]
    even = is_even("gx")
    a, b = mate[...], far[:depth]
    both = jnp.concatenate([jnp.where(even, b, a), jnp.where(even, a, b)], 0)
    w = w3[...].astype(BF)
    first, second = w[:, depth:], w[:, : 2 * depth]
    beside_mate[...] = shift_taps(mat(jnp.where(even, second, first), both), z)
    beside_far[...] = shift_taps(mat(jnp.where(even, first, second), both), z)
    w_mate[...] = jnp.where(even, w[:, 2 * depth :], w[:, :depth])
    w_far[...] = jnp.where(even, w[:, :depth], w[:, 2 * depth :])


def is_end():
    g = lax.axis_index("gx")
    return (g == 0) | (g == lax.axis_size("gx") - 1)


def write_planes(beside_mate, beside_far, out, block, sem):
    even = is_even("gx")
    a, b = relu(beside_mate), relu(beside_far)
    rows, cells = a.shape
    pair = jnp.concatenate([jnp.where(even, b, a), jnp.where(even, a, b)], 1)
    block[...] = pair.astype(BF).reshape(rows, 2, cells)
    copy = pltpu.make_async_copy(block, out, sem)
    copy.start()
    copy.wait()


def near_kernel(z, beside_mate, beside_far, w_mate, got_mate, out, ready, block, sem):
    ready[...] = beside_mate[...] + shift_taps(mat(w_mate[...], got_mate[...]), z)

    @pl.when(is_end())
    def _():
        write_planes(ready[...], beside_far[...], out, block, sem)


def far_kernel(z, got_far, w_far, ready, beside_far, _, out, block, sem):
    @pl.when(jnp.logical_not(is_end()))
    def _():
        part = beside_far[...] + shift_taps(mat(w_far[...], got_far[: w_far.shape[1]]), z)
        write_planes(ready[...], part, out, block, sem)


def per_device(volume, weight_one, weight_two, weight_three):
    gx, yz = lax.axis_size("gx"), lax.axis_size("yz")
    planes, chans, height, breadth = volume.shape
    rows = chans * height
    edge = EDGE * chans
    c2, c3 = weight_one.shape[0], weight_two.shape[0]

    planes_shape = ((HALO, chans, height, breadth), BF)
    send_mate, send_far = call(
        planes_kernel,
        [planes_shape, planes_shape],
        volume,
        scratch=[pltpu.SemaphoreType.DMA((2,))],
        hbm=(0,),
    )
    near, away = gx_pairs(gx, yz, False), gx_pairs(gx, yz, True)
    raw_mate = lax.ppermute(send_mate, ("gx", "yz"), near)
    raw_far = lax.ppermute(send_far, ("gx", "yz"), away)
    k1, k2 = 27 * chans, 27 * c2
    lower1, upper1, middle2, outer2, p_sel, swap, turned = call(
        weights_kernel,
        [
            ((4 * c2, k1), BF),
            ((4 * c2, k1), BF),
            ((4 * c3, 2 * k2 // 3), BF),
            ((4 * c3, 2 * k2 // 3), BF),
            ((4 * breadth, breadth), BF),
            ((rows, rows), BF),
            ((planes, rows, breadth), BF),
        ],
        volume,
        weight_one,
        weight_two,
        scratch=[
            pltpu.VMEM(volume.shape, BF),
            pltpu.VMEM(weight_one.shape, BF),
            pltpu.VMEM(weight_two.shape, BF),
            pltpu.SemaphoreType.DMA((3,)),
        ],
        hbm=(0, 1, 2),
        flops=2 * 64 * 864 * 1728,
    )
    wide = planes + 2 * HALO
    halo = ((HALO, rows, breadth), BF)
    send_a, send_b, got_far, got_mate = call(
        edge_kernel,
        [((wide, edge, breadth), BF), ((wide, edge, breadth), BF), halo, halo],
        raw_far,
        raw_mate,
        turned,
        swap,
        p_sel,
    )
    got_b = lax.ppermute(send_b, ("gx", "yz"), yz_pairs(gx, yz, True))
    got_a = lax.ppermute(send_a, ("gx", "yz"), yz_pairs(gx, yz, False))
    pairs = 2 * PLANES + 2
    out_rows = weight_three.shape[0] // yz
    partial1, partial2, picked = call(
        inner_kernel,
        [
            ((2, pairs, 4 * c2, 2 * breadth), F32),
            ((4 * c3, 2 * PLANES * breadth), F32),
            ((9 * out_rows, 3 * c3), F32),
        ],
        turned,
        got_mate,
        got_far,
        lower1,
        upper1,
        middle2,
        weight_three.T,
        scratch=[
            pltpu.VMEM((wide, 3 * rows, breadth), BF),
            pltpu.VMEM(weight_three.shape[::-1], BF),
            pltpu.SemaphoreType.DMA,
        ],
        hbm=(6,),
        flops=2 * 300_000_000,
    )
    (tile,) = call(
        outer_kernel,
        [((c3, breadth), BF)],
        got_a,
        got_b,
        partial1,
        partial2,
        lower1,
        upper1,
        outer2,
        p_sel,
        scratch=[pltpu.VMEM((wide, 3 * edge, breadth), BF), pltpu.VMEM((wide, 3 * edge, breadth), BF)],
        flops=2 * 400_000_000,
    )
    tiles = [tile] + [lax.ppermute(tile, "yz", [(i, i ^ d) for i in range(yz)]) for d in range(1, yz)]
    cells = yz * (height // 4) * (breadth // 4)
    z = breadth // 4
    mate, far = call(lay_kernel, [((c3, cells), BF), ((c3 + 16, cells), BF)], tiles[0], *[tiles[d] for d in [1, 2, 3]])
    got_far = lax.ppermute(far, ("gx", "yz"), away)
    got_mate = lax.ppermute(mate, ("gx", "yz"), near)
    shape = (out_rows, 2, cells)
    plane, weights = ((out_rows, cells), F32), ((9 * out_rows, c3), BF)
    beside_mate, beside_far, w_mate, w_far = call(
        functools.partial(middle_kernel, z),
        [plane, plane, weights, weights],
        mate,
        far,
        picked,
        flops=2 * 32 * 1152 * 512,
    )
    block = [pltpu.VMEM(shape, BF), pltpu.SemaphoreType.DMA]
    out, ready = call(
        functools.partial(near_kernel, z),
        [(shape, BF), plane],
        beside_mate,
        beside_far,
        w_mate,
        got_mate,
        scratch=block,
        hbm_out=True,
        free=True,
    )
    (out,) = call(
        functools.partial(far_kernel, z),
        [(shape, BF)],
        got_far,
        w_far,
        ready,
        beside_far,
        out,
        scratch=block,
        hbm=(4,),
        hbm_out=True,
        aliases={4: 0},
        flops=2 * 32 * 576 * 256,
    )
    return out


def solution(mesh):
    placed = (P("gx", None, "yz", None), P(), P(), P())
    return jax.shard_map(
        per_device, mesh=mesh, in_specs=placed, out_specs=P("yz", "gx", None), check_vma=False
    )
```

```python
import functools

import jax
import jax.numpy as jnp
from jax import lax
from jax.experimental import pallas as pl
from jax.experimental.pallas import tpu as pltpu
from jax.sharding import PartitionSpec as P

BF = jnp.bfloat16
F32 = jnp.float32
PLANES = 2
HALO = 2 * PLANES - 1
EDGE = 3


def mat(a, b):
    return jnp.dot(a, b, preferred_element_type=F32)


def relu(a):
    return jnp.maximum(a, 0.0)


def iota(shape, dim):
    return lax.broadcasted_iota(jnp.int32, shape, dim)


def call(body, outs, *args, scratch=(), flops=0, free=False, hbm=(), hbm_out=False, aliases={}):
    moved = 0 if free else sum(a.size * a.dtype.itemsize for a in args)
    args = [pltpu.with_memory_space_constraint(a, pltpu.HBM) if i in hbm else a for i, a in enumerate(args)]
    return pl.pallas_call(
        body,
        out_shape=[jax.ShapeDtypeStruct(s, d) for s, d in outs],
        in_specs=[pl.BlockSpec(memory_space=pltpu.HBM if i in hbm else pltpu.VMEM) for i in range(len(args))],
        out_specs=[pl.BlockSpec(memory_space=pltpu.HBM if hbm_out and i == 0 else pltpu.VMEM) for i in range(len(outs))],
        scratch_shapes=list(scratch),
        input_output_aliases=aliases,
        compiler_params=pltpu.CompilerParams(vmem_limit_bytes=40 * 1024 * 1024),
        cost_estimate=pl.CostEstimate(flops=flops, bytes_accessed=moved, transcendentals=0),
    )(*args)


def planes_kernel(volume, send_mate, send_far, sems):
    planes = volume.shape[0]
    even = is_even("gx")
    copies = []
    for i, (out, first) in enumerate(
        ((send_far, jnp.where(even, 0, planes - HALO)), (send_mate, jnp.where(even, planes - HALO, 0)))
    ):
        copies.append(pltpu.make_async_copy(volume.at[pl.ds(first, HALO)], out, sems.at[i]))
    for copy in copies:
        copy.start()
    for copy in copies:
        copy.wait()


def turn(swap, plane):
    rows, breadth = swap.shape[0], plane.shape[-1]
    return mat(swap, plane.reshape(rows, breadth)).astype(BF)


def yz_pairs(gx, yz, second):
    pairs = []
    for g in range(gx):
        for k in range(yz):
            if not second:
                pairs.append((g * yz + k, g * yz + (k ^ 1)))
            elif k in (0, yz - 1):
                pairs.append((g * yz + k, (g ^ 1) * yz + k))
            else:
                pairs.append((g * yz + k, g * yz + (k + 1 if k % 2 else k - 1)))
    return pairs


def gx_pairs(gx, yz, far):
    pairs = []
    for g in range(gx):
        for k in range(yz):
            if not far:
                pairs.append((g * yz + k, (g ^ 1) * yz + k))
            elif g in (0, gx - 1):
                pairs.append((g * yz + k, g * yz + (k ^ 1)))
            else:
                pairs.append((g * yz + k, (g + 1 if g % 2 else g - 1) * yz + k))
    return pairs


def is_even(axis):
    return lax.rem(lax.axis_index(axis), 2) == 0


def from_sides(mate, far, even, no_low, no_high):
    zero = jnp.zeros_like(mate)
    low = jnp.where(no_low, zero, jnp.where(even, far, mate))
    high = jnp.where(no_high, zero, jnp.where(even, mate, far))
    return low, high


def all_planes(turned, got_mate, got_far):
    g = lax.axis_index("gx")
    even, first, last = is_even("gx"), g == 0, g == lax.axis_size("gx") - 1
    sides = [from_sides(got_mate[x], got_far[x], even, first, last) for x in range(HALO)]
    return [low for low, _ in sides] + [turned[x] for x in range(turned.shape[0])] + [high for _, high in sides]


def edge_kernel(raw_far, raw_mate, turned, swap, _, send_a, send_b, got_far, got_mate):
    for x in range(HALO):
        got_far[x] = turn(swap[...], raw_far[x])
        got_mate[x] = turn(swap[...], raw_mate[x])
    edge = send_a.shape[1]
    even = is_even("yz")
    for x, t in enumerate(all_planes(turned, got_mate, got_far)):
        low, high = t[:edge], t[t.shape[0] - edge :]
        send_a[x] = jnp.where(even, high, low)
        send_b[x] = jnp.where(even, low, high)


def weights_kernel(volume, w1_hbm, w2_hbm, lower1, upper1, middle2, outer2, p_sel, swap, turned, vol, w1, w2, sems):
    pairs = ((w1_hbm, w1), (w2_hbm, w2), (volume, vol))
    loads = [pltpu.make_async_copy(a, b, sems.at[i]) for i, (a, b) in enumerate(pairs)]
    for load in loads:
        load.start()

    rows, columns = p_sel.shape
    z = rows // 4
    r, c = iota(p_sel.shape, 0), iota(p_sel.shape, 1)
    hit = (r // (2 * z) == (c // (z // 4)) % 2) & ((r // z) % 2 == c // (z // 2))
    hit = hit & ((r & (z - 1)) == 4 * (c & (z // 4 - 1)))
    p_sel[...] = jnp.where(hit, 1.0, 0.0).astype(BF)

    planes, chans, height, breadth = vol.shape
    dest = iota(swap.shape, 0)
    source = (dest & (chans - 1)) * height + dest // chans
    swap[...] = (iota(swap.shape, 1) == source).astype(F32).astype(BF)

    for load in loads:
        load.wait()
    for x in range(planes):
        turned[x] = turn(swap[...], vol[x])
    for w, bands in (
        (w1, ((lower1, lambda y: (0, 1, 2)), (upper1, lambda y: (3, 4, 5)))),
        (w2, ((middle2, lambda y: (2, 3)), (outer2, lambda y: (0, 1) if y < 2 else (4, 5)))),
    ):
        out_rows, width = w.shape[0], w.shape[1] // 9
        taps = w[...].astype(F32)
        zero = jnp.zeros((out_rows, width), F32)
        for band, window in bands:
            for y in range(4):
                pieces = []
                for a in range(3):
                    for row in window(y):
                        first = (3 * a + row - y) * width
                        pieces.append(taps[:, first : first + width] if 0 <= row - y < 3 else zero)
                band[out_rows * y : out_rows * (y + 1)] = jnp.concatenate(pieces, 1).astype(BF)


def put_taps(dest, t, chans):
    breadth = t.shape[1]
    lane = iota((1, breadth), 1)
    wide = t.astype(F32)
    before = jnp.where(lane == 0, 0.0, pltpu.roll(wide, 1, 1)).astype(BF)
    after = jnp.where(lane == breadth - 1, 0.0, pltpu.roll(wide, breadth - 1, 1)).astype(BF)
    for y in range(t.shape[0] // chans):
        for tap, value in enumerate((before, t, after)):
            row = (3 * y + tap) * chans
            dest[row : row + chans] = value[y * chans : (y + 1) * chans]


def three(taps, e, first, rows):
    return jnp.concatenate([taps[e + a, first : first + rows] for a in range(3)], 0)


def two_cells(taps, j, first, rows):
    return jnp.concatenate([three(taps, 2 * j, first, rows), three(taps, 2 * j + 1, first, rows)], 1)


def pool_first(acc, j, pairs, no_low, no_high):
    g = lax.axis_index("gx")
    breadth = acc.shape[1] // 2
    width = acc.shape[0] // 4
    r = relu(acc)
    s = r[:, :breadth] + r[:, breadth:]
    halves = []
    for y, drop in enumerate((no_low, no_high)):
        t = s[2 * y * width : (2 * y + 1) * width] + s[(2 * y + 1) * width : (2 * y + 2) * width]
        t = (t + pltpu.roll(t, breadth - 1, 1)) * 0.125
        if j < PLANES - 1:
            drop = drop | (g == 0)
        if j > pairs - PLANES:
            drop = drop | (g == lax.axis_size("gx") - 1)
        halves.append(t if drop is False else jnp.where(drop, 0.0, t))
    return pooled_taps(jnp.concatenate(halves, 0))


def pooled_taps(t):
    breadth = t.shape[1]
    lane = iota((1, breadth), 1)
    before = jnp.where(lane < 2, 0.0, pltpu.roll(t, 2, 1)).astype(BF)
    after = jnp.where(lane >= breadth - 2, 0.0, pltpu.roll(t, breadth - 2, 1)).astype(BF)
    chans = t.shape[0] // 2
    rows = [slice(y * chans, (y + 1) * chans) for y in range(2)]
    return jnp.concatenate([u[r] for r in rows for u in (before, t.astype(BF), after)], 0)


def second_taps(planes):
    return jnp.concatenate([jnp.concatenate(planes[x : x + 3], 0) for x in range(len(planes) - 2)], 1)


def inner_kernel(
    turned, got_mate, got_far, lower1, upper1, middle2, w3_hbm, partial1, partial2, picked, taps, w3, sem
):
    load = pltpu.make_async_copy(w3_hbm, w3, sem)
    load.start()
    chans = lower1.shape[1] // 27
    for e, t in enumerate(all_planes(turned, got_mate, got_far)):
        put_taps(taps.at[e], t, chans)
    pairs = partial1.shape[1]
    width = lower1.shape[0] // 4
    lower, upper = lower1[: 3 * width], upper1[width:]
    step = 3 * chans
    pooled = []
    for j in range(pairs):
        partial1[0, j] = mat(upper, two_cells(taps, j, 0, 3 * step))
        partial1[1, j] = mat(lower, two_cells(taps, j, 5 * step, 3 * step))
        a = mat(lower, two_cells(taps, j, step, 3 * step))
        b = mat(upper, two_cells(taps, j, 4 * step, 3 * step))
        acc = jnp.concatenate([a[:width], a[width:] + b[: 2 * width], b[2 * width :]], 0)
        pooled.append(pool_first(acc, j, pairs, False, False))
    partial2[...] = mat(middle2[...], second_taps(pooled))
    load.wait()
    out_rows = picked.shape[0] // 9
    own = (out_rows, w3.shape[1])
    first = lax.axis_index("yz") * out_rows
    pick = (iota(own, 1) == iota(own, 0) + first).astype(F32).astype(BF)
    own3 = lax.dot_general(pick, w3[...], (((1,), (1,)), ((), ())), preferred_element_type=F32)
    depth = picked.shape[1] // 3
    for tap in range(9):
        pieces = [own3[:, (9 * a + tap) * depth : (9 * a + tap + 1) * depth] for a in range(3)]
        picked[tap * out_rows : (tap + 1) * out_rows] = jnp.concatenate(pieces, 1)


def outer_kernel(got_a, got_b, partial1, partial2, lower1, upper1, outer2, p_sel, out, low_taps, high_taps):
    planes, edge, breadth = got_a.shape
    chans = edge // EDGE
    k = lax.axis_index("yz")
    even, first, last = is_even("yz"), k == 0, k == lax.axis_size("yz") - 1
    for e in range(planes):
        low, high = from_sides(got_a[e], got_b[e], even, first, last)
        put_taps(low_taps.at[e], low, chans)
        put_taps(high_taps.at[e], high, chans)
    pairs = partial1.shape[1]
    width = lower1.shape[0] // 4
    lower, upper = lower1[: 3 * width], upper1[width:]
    rows = 3 * edge
    below, above = [], []
    lows = [mat(lower, two_cells(low_taps, j, 0, rows)) for j in range(pairs)]
    highs = [mat(upper, two_cells(high_taps, j, 0, rows)) for j in range(pairs)]
    for j in range(pairs):
        p = partial1[0, j]
        a = lows[j]
        a = jnp.concatenate([a[:width], p[: 2 * width] + a[width:], p[2 * width :]], 0)
        below.append(pool_first(a, j, pairs, first, False))
        p = partial1[1, j]
        b = highs[j]
        b = jnp.concatenate([p[:width], p[width:] + b[: 2 * width], b[2 * width :]], 0)
        above.append(pool_first(b, j, pairs, False, last))
    width = outer2.shape[0] // 4
    sums = [mat(outer2[2 * y * width : 2 * (y + 1) * width], second_taps(p)) for y, p in enumerate((below, above))]
    halves = []
    for y in range(2):
        r = relu(partial2[2 * y * width : 2 * (y + 1) * width] + sums[y])
        t = r[:width] + r[width:]
        t = [t[:, 2 * x * breadth : (2 * x + 1) * breadth] + t[:, (2 * x + 1) * breadth : 2 * (x + 1) * breadth] for x in range(PLANES)]
        halves.append([((u + pltpu.roll(u, breadth - 2, 1)) * 0.125).astype(BF) for u in t])
    out[...] = mat(jnp.concatenate(halves[0] + halves[1], 1), p_sel[...]).astype(BF)


def lay(tiles, rows):
    even = is_even("yz")
    half = tiles[0].shape[1] // 2
    lane = iota((1, 2 * half), 1)
    tiles = [tiles[i] for i in [0, 1, 2, 3]]
    low, high = [], []
    for m in range(len(tiles) // 2):
        a, b = tiles[2 * m][rows].astype(F32), tiles[2 * m + 1][rows].astype(F32)
        first, second = jnp.where(even, a, b), jnp.where(even, b, a)
        low.append(jnp.where(lane < half, first, pltpu.roll(second, half, 1)))
        high.append(jnp.where(lane < half, pltpu.roll(first, half, 1), second))
    return low, high


def put_plane(dest, blocks):
    wide = blocks[0].shape[1]
    k = lax.axis_index("yz")
    for m, block in enumerate(blocks):
        dest[: block.shape[0], pl.ds(pl.multiple_of((lax.div(k, 2) ^ m) * wide, wide), wide)] = block.astype(BF)


def lay_kernel(*refs):
    tiles, (mate, far) = refs[:-2], refs[-2:]
    low, high = lay(tiles, slice(None))
    even = is_even("gx")
    put_plane(mate, [jnp.where(even, b, a) for a, b in zip(low, high)])
    put_plane(far, [jnp.where(even, a, b) for a, b in zip(low, high)])
    depth = mate.shape[0]
    far[depth:] = jnp.zeros((far.shape[0] - depth, far.shape[1]), BF)


def shift_taps(products, z):
    rows, cells = products.shape[0] // 9, products.shape[1]
    lane = iota((1, cells), 1)
    depth = lane & (z - 1)
    total = None
    for b in range(3):
        one = [products[(3 * b + c) * rows : (3 * b + c + 1) * rows] for c in range(3)]
        t = one[1] + jnp.where(depth == 0, 0.0, pltpu.roll(one[0], 1, 1))
        t = t + jnp.where(depth == z - 1, 0.0, pltpu.roll(one[2], cells - 1, 1))
        if b == 0:
            t = jnp.where(lane < z, 0.0, pltpu.roll(t, z, 1))
        if b == 2:
            t = jnp.where(lane >= cells - z, 0.0, pltpu.roll(t, cells - z, 1))
        total = t if total is None else total + t
    return total


def middle_kernel(z, mate, far, w3, beside_mate, beside_far, w_mate, w_far):
    depth = mate.shape[0]
    even = is_even("gx")
    a, b = mate[...], far[:depth]
    both = jnp.concatenate([jnp.where(even, b, a), jnp.where(even, a, b)], 0)
    w = w3[...].astype(BF)
    first, second = w[:, depth:], w[:, : 2 * depth]
    beside_mate[...] = shift_taps(mat(jnp.where(even, second, first), both), z)
    beside_far[...] = shift_taps(mat(jnp.where(even, first, second), both), z)
    w_mate[...] = jnp.where(even, w[:, 2 * depth :], w[:, :depth])
    w_far[...] = jnp.where(even, w[:, :depth], w[:, 2 * depth :])


def is_end():
    g = lax.axis_index("gx")
    return (g == 0) | (g == lax.axis_size("gx") - 1)


def write_planes(beside_mate, beside_far, out, block, sem):
    even = is_even("gx")
    a, b = relu(beside_mate), relu(beside_far)
    rows, cells = a.shape
    pair = jnp.concatenate([jnp.where(even, b, a), jnp.where(even, a, b)], 1)
    block[...] = pair.astype(BF).reshape(rows, 2, cells)
    copy = pltpu.make_async_copy(block, out, sem)
    copy.start()
    copy.wait()


def near_kernel(z, beside_mate, beside_far, w_mate, got_mate, out, ready, block, sem):
    ready[...] = beside_mate[...] + shift_taps(mat(w_mate[...], got_mate[...]), z)

    @pl.when(is_end())
    def _():
        write_planes(ready[...], beside_far[...], out, block, sem)


def far_kernel(z, got_far, w_far, ready, beside_far, _, out, block, sem):
    @pl.when(jnp.logical_not(is_end()))
    def _():
        part = beside_far[...] + shift_taps(mat(w_far[...], got_far[: w_far.shape[1]]), z)
        write_planes(ready[...], part, out, block, sem)


def per_device(volume, weight_one, weight_two, weight_three):
    gx, yz = lax.axis_size("gx"), lax.axis_size("yz")
    planes, chans, height, breadth = volume.shape
    rows = chans * height
    edge = EDGE * chans
    c2, c3 = weight_one.shape[0], weight_two.shape[0]

    planes_shape = ((HALO, chans, height, breadth), BF)
    send_mate, send_far = call(
        planes_kernel,
        [planes_shape, planes_shape],
        volume,
        scratch=[pltpu.SemaphoreType.DMA((2,))],
        hbm=(0,),
    )
    near, away = gx_pairs(gx, yz, False), gx_pairs(gx, yz, True)
    raw_mate = lax.ppermute(send_mate, ("gx", "yz"), near)
    raw_far = lax.ppermute(send_far, ("gx", "yz"), away)
    k1, k2 = 27 * chans, 27 * c2
    lower1, upper1, middle2, outer2, p_sel, swap, turned = call(
        weights_kernel,
        [
            ((4 * c2, k1), BF),
            ((4 * c2, k1), BF),
            ((4 * c3, 2 * k2 // 3), BF),
            ((4 * c3, 2 * k2 // 3), BF),
            ((4 * breadth, breadth), BF),
            ((rows, rows), BF),
            ((planes, rows, breadth), BF),
        ],
        volume,
        weight_one,
        weight_two,
        scratch=[
            pltpu.VMEM(volume.shape, BF),
            pltpu.VMEM(weight_one.shape, BF),
            pltpu.VMEM(weight_two.shape, BF),
            pltpu.SemaphoreType.DMA((3,)),
        ],
        hbm=(0, 1, 2),
        flops=2 * 64 * 864 * 1728,
    )
    wide = planes + 2 * HALO
    halo = ((HALO, rows, breadth), BF)
    send_a, send_b, got_far, got_mate = call(
        edge_kernel,
        [((wide, edge, breadth), BF), ((wide, edge, breadth), BF), halo, halo],
        raw_far,
        raw_mate,
        turned,
        swap,
        p_sel,
    )
    got_b = lax.ppermute(send_b, ("gx", "yz"), yz_pairs(gx, yz, True))
    got_a = lax.ppermute(send_a, ("gx", "yz"), yz_pairs(gx, yz, False))
    pairs = 2 * PLANES + 2
    out_rows = weight_three.shape[0] // yz
    partial1, partial2, picked = call(
        inner_kernel,
        [
            ((2, pairs, 3 * c2, 2 * breadth), F32),
            ((4 * c3, 2 * PLANES * breadth), F32),
            ((9 * out_rows, 3 * c3), F32),
        ],
        turned,
        got_mate,
        got_far,
        lower1,
        upper1,
        middle2,
        weight_three.T,
        scratch=[
            pltpu.VMEM((wide, 3 * rows, breadth), BF),
            pltpu.VMEM(weight_three.shape[::-1], BF),
            pltpu.SemaphoreType.DMA,
        ],
        hbm=(6,),
        flops=2 * 300_000_000,
    )
    (tile,) = call(
        outer_kernel,
        [((c3, breadth), BF)],
        got_a,
        got_b,
        partial1,
        partial2,
        lower1,
        upper1,
        outer2,
        p_sel,
        scratch=[pltpu.VMEM((wide, 3 * edge, breadth), BF), pltpu.VMEM((wide, 3 * edge, breadth), BF)],
        flops=2 * 400_000_000,
    )
    tiles = [tile] + [lax.ppermute(tile, "yz", [(i, i ^ d) for i in range(yz)]) for d in range(1, yz)]
    cells = yz * (height // 4) * (breadth // 4)
    z = breadth // 4
    mate, far = call(lay_kernel, [((c3, cells), BF), ((c3 + 16, cells), BF)], tiles[0], *[tiles[d] for d in [1, 2, 3]])
    got_far = lax.ppermute(far, ("gx", "yz"), away)
    got_mate = lax.ppermute(mate, ("gx", "yz"), near)
    shape = (out_rows, 2, cells)
    plane, weights = ((out_rows, cells), F32), ((9 * out_rows, c3), BF)
    beside_mate, beside_far, w_mate, w_far = call(
        functools.partial(middle_kernel, z),
        [plane, plane, weights, weights],
        mate,
        far,
        picked,
        flops=2 * 32 * 1152 * 512,
    )
    block = [pltpu.VMEM(shape, BF), pltpu.SemaphoreType.DMA]
    out, ready = call(
        functools.partial(near_kernel, z),
        [(shape, BF), plane],
        beside_mate,
        beside_far,
        w_mate,
        got_mate,
        scratch=block,
        hbm_out=True,
        free=True,
    )
    (out,) = call(
        functools.partial(far_kernel, z),
        [(shape, BF)],
        got_far,
        w_far,
        ready,
        beside_far,
        out,
        scratch=block,
        hbm=(4,),
        hbm_out=True,
        aliases={4: 0},
        flops=2 * 32 * 576 * 256,
    )
    return out


def solution(mesh):
    placed = (P("gx", None, "yz", None), P(), P(), P())
    return jax.shard_map(
        per_device, mesh=mesh, in_specs=placed, out_specs=P("yz", "gx", None), check_vma=False
    )
```

```python
import functools

import jax
import jax.numpy as jnp
from jax import lax
from jax.experimental import pallas as pl
from jax.experimental.pallas import tpu as pltpu
from jax.sharding import PartitionSpec as P

BF = jnp.bfloat16
F32 = jnp.float32
PLANES = 2
HALO = 2 * PLANES - 1
EDGE = 3


def mat(a, b):
    return jnp.dot(a, b, preferred_element_type=F32)


def relu(a):
    return jnp.maximum(a, 0.0)


def iota(shape, dim):
    return lax.broadcasted_iota(jnp.int32, shape, dim)


def call(body, outs, *args, scratch=(), flops=0, free=False, hbm=(), hbm_out=False, aliases={}):
    moved = 0 if free else sum(a.size * a.dtype.itemsize for a in args)
    args = [pltpu.with_memory_space_constraint(a, pltpu.HBM) if i in hbm else a for i, a in enumerate(args)]
    return pl.pallas_call(
        body,
        out_shape=[jax.ShapeDtypeStruct(s, d) for s, d in outs],
        in_specs=[pl.BlockSpec(memory_space=pltpu.HBM if i in hbm else pltpu.VMEM) for i in range(len(args))],
        out_specs=[pl.BlockSpec(memory_space=pltpu.HBM if hbm_out and i == 0 else pltpu.VMEM) for i in range(len(outs))],
        scratch_shapes=list(scratch),
        input_output_aliases=aliases,
        compiler_params=pltpu.CompilerParams(vmem_limit_bytes=40 * 1024 * 1024),
        cost_estimate=pl.CostEstimate(flops=flops, bytes_accessed=moved, transcendentals=0),
    )(*args)


def planes_kernel(volume, send_mate, send_far, sems):
    planes = volume.shape[0]
    even = is_even("gx")
    copies = []
    for i, (out, first) in enumerate(
        ((send_far, jnp.where(even, 0, planes - HALO)), (send_mate, jnp.where(even, planes - HALO, 0)))
    ):
        copies.append(pltpu.make_async_copy(volume.at[pl.ds(first, HALO)], out, sems.at[i]))
    for copy in copies:
        copy.start()
    for copy in copies:
        copy.wait()


def turn(swap, plane):
    rows, breadth = swap.shape[0], plane.shape[-1]
    return mat(swap, plane.reshape(rows, breadth)).astype(BF)


def yz_pairs(gx, yz, second):
    pairs = []
    for g in range(gx):
        for k in range(yz):
            if not second:
                pairs.append((g * yz + k, g * yz + (k ^ 1)))
            elif k in (0, yz - 1):
                pairs.append((g * yz + k, (g ^ 1) * yz + k))
            else:
                pairs.append((g * yz + k, g * yz + (k + 1 if k % 2 else k - 1)))
    return pairs


def gx_pairs(gx, yz, far):
    pairs = []
    for g in range(gx):
        for k in range(yz):
            if not far:
                pairs.append((g * yz + k, (g ^ 1) * yz + k))
            elif g in (0, gx - 1):
                pairs.append((g * yz + k, g * yz + (k ^ 1)))
            else:
                pairs.append((g * yz + k, (g + 1 if g % 2 else g - 1) * yz + k))
    return pairs


def is_even(axis):
    return lax.rem(lax.axis_index(axis), 2) == 0


def from_sides(mate, far, even, no_low, no_high):
    zero = jnp.zeros_like(mate)
    low = jnp.where(no_low, zero, jnp.where(even, far, mate))
    high = jnp.where(no_high, zero, jnp.where(even, mate, far))
    return low, high


def all_planes(turned, got_mate, got_far):
    g = lax.axis_index("gx")
    even, first, last = is_even("gx"), g == 0, g == lax.axis_size("gx") - 1
    sides = [from_sides(got_mate[x], got_far[x], even, first, last) for x in range(HALO)]
    return [low for low, _ in sides] + [turned[x] for x in range(turned.shape[0])] + [high for _, high in sides]


def edge_kernel(raw_far, raw_mate, turned, swap, _, send_a, send_b, got_far, got_mate):
    rows, breadth = got_far.shape[1:]
    beside = [raw[x].reshape(rows, breadth) for raw in (raw_far, raw_mate) for x in range(HALO)]
    beside = mat(swap[...], jnp.concatenate(beside, 1)).astype(BF)
    for x in range(HALO):
        got_far[x] = beside[:, x * breadth : (x + 1) * breadth]
        got_mate[x] = beside[:, (HALO + x) * breadth : (HALO + x + 1) * breadth]
    edge = send_a.shape[1]
    even = is_even("yz")
    for x, t in enumerate(all_planes(turned, got_mate, got_far)):
        low, high = t[:edge], t[t.shape[0] - edge :]
        send_a[x] = jnp.where(even, high, low)
        send_b[x] = jnp.where(even, low, high)


def weights_kernel(volume, w1_hbm, w2_hbm, lower1, upper1, middle2, outer2, p_sel, swap, turned, vol, w1, w2, sems):
    pairs = ((w1_hbm, w1), (w2_hbm, w2), (volume, vol))
    loads = [pltpu.make_async_copy(a, b, sems.at[i]) for i, (a, b) in enumerate(pairs)]
    for load in loads:
        load.start()

    rows, columns = p_sel.shape
    z = rows // 4
    r, c = iota(p_sel.shape, 0), iota(p_sel.shape, 1)
    hit = (r // (2 * z) == (c // (z // 4)) % 2) & ((r // z) % 2 == c // (z // 2))
    hit = hit & ((r & (z - 1)) == 4 * (c & (z // 4 - 1)))
    p_sel[...] = jnp.where(hit, 1.0, 0.0).astype(BF)

    planes, chans, height, breadth = vol.shape
    dest = iota(swap.shape, 0)
    source = (dest & (chans - 1)) * height + dest // chans
    swap[...] = (iota(swap.shape, 1) == source).astype(F32).astype(BF)

    for load in loads:
        load.wait()
    for x in range(planes):
        turned[x] = turn(swap[...], vol[x])
    for w, bands in (
        (w1, ((lower1, lambda y: (0, 1, 2)), (upper1, lambda y: (3, 4, 5)))),
        (w2, ((middle2, lambda y: (2, 3)), (outer2, lambda y: (0, 1) if y < 2 else (4, 5)))),
    ):
        out_rows, width = w.shape[0], w.shape[1] // 9
        taps = w[...].astype(F32)
        zero = jnp.zeros((out_rows, width), F32)
        for band, window in bands:
            for y in range(4):
                pieces = []
                for a in range(3):
                    for row in window(y):
                        first = (3 * a + row - y) * width
                        pieces.append(taps[:, first : first + width] if 0 <= row - y < 3 else zero)
                band[out_rows * y : out_rows * (y + 1)] = jnp.concatenate(pieces, 1).astype(BF)


def put_taps(dest, t, chans):
    breadth = t.shape[1]
    lane = iota((1, breadth), 1)
    wide = t.astype(F32)
    before = jnp.where(lane == 0, 0.0, pltpu.roll(wide, 1, 1)).astype(BF)
    after = jnp.where(lane == breadth - 1, 0.0, pltpu.roll(wide, breadth - 1, 1)).astype(BF)
    for y in range(t.shape[0] // chans):
        for tap, value in enumerate((before, t, after)):
            row = (3 * y + tap) * chans
            dest[row : row + chans] = value[y * chans : (y + 1) * chans]


def three(taps, e, first, rows):
    return jnp.concatenate([taps[e + a, first : first + rows] for a in range(3)], 0)


def two_cells(taps, j, first, rows):
    return jnp.concatenate([three(taps, 2 * j, first, rows), three(taps, 2 * j + 1, first, rows)], 1)


def pool_first(acc, j, pairs, no_low, no_high):
    g = lax.axis_index("gx")
    breadth = acc.shape[1] // 2
    width = acc.shape[0] // 4
    r = relu(acc)
    s = r[:, :breadth] + r[:, breadth:]
    halves = []
    for y, drop in enumerate((no_low, no_high)):
        t = s[2 * y * width : (2 * y + 1) * width] + s[(2 * y + 1) * width : (2 * y + 2) * width]
        t = (t + pltpu.roll(t, breadth - 1, 1)) * 0.125
        if j < PLANES - 1:
            drop = drop | (g == 0)
        if j > pairs - PLANES:
            drop = drop | (g == lax.axis_size("gx") - 1)
        halves.append(t if drop is False else jnp.where(drop, 0.0, t))
    return pooled_taps(jnp.concatenate(halves, 0))


def pooled_taps(t):
    breadth = t.shape[1]
    lane = iota((1, breadth), 1)
    before = jnp.where(lane < 2, 0.0, pltpu.roll(t, 2, 1)).astype(BF)
    after = jnp.where(lane >= breadth - 2, 0.0, pltpu.roll(t, breadth - 2, 1)).astype(BF)
    chans = t.shape[0] // 2
    rows = [slice(y * chans, (y + 1) * chans) for y in range(2)]
    return jnp.concatenate([u[r] for r in rows for u in (before, t.astype(BF), after)], 0)


def second_taps(planes):
    return jnp.concatenate([jnp.concatenate(planes[x : x + 3], 0) for x in range(len(planes) - 2)], 1)


def inner_kernel(
    turned, got_mate, got_far, lower1, upper1, middle2, w3_hbm, partial1, partial2, picked, taps, w3, sem
):
    load = pltpu.make_async_copy(w3_hbm, w3, sem)
    load.start()
    chans = lower1.shape[1] // 27
    for e, t in enumerate(all_planes(turned, got_mate, got_far)):
        put_taps(taps.at[e], t, chans)
    pairs = partial1.shape[1]
    width = lower1.shape[0] // 4
    lower, upper = lower1[: 3 * width], upper1[width:]
    step = 3 * chans
    pooled = []
    zero = jnp.zeros((width, partial1.shape[3]), F32)
    for j in range(pairs):
        partial1[0, j, :width] = zero
        partial1[0, j, width:] = mat(upper, two_cells(taps, j, 0, 3 * step))
        partial1[1, j, : 3 * width] = mat(lower, two_cells(taps, j, 5 * step, 3 * step))
        partial1[1, j, 3 * width :] = zero
        a = mat(lower, two_cells(taps, j, step, 3 * step))
        b = mat(upper, two_cells(taps, j, 4 * step, 3 * step))
        acc = jnp.concatenate([a[:width], a[width:] + b[: 2 * width], b[2 * width :]], 0)
        pooled.append(pool_first(acc, j, pairs, False, False))
    partial2[...] = mat(middle2[...], second_taps(pooled))
    load.wait()
    out_rows = picked.shape[0] // 9
    own = (out_rows, w3.shape[1])
    first = lax.axis_index("yz") * out_rows
    pick = (iota(own, 1) == iota(own, 0) + first).astype(F32).astype(BF)
    own3 = lax.dot_general(pick, w3[...], (((1,), (1,)), ((), ())), preferred_element_type=F32)
    depth = picked.shape[1] // 3
    for tap in range(9):
        pieces = [own3[:, (9 * a + tap) * depth : (9 * a + tap + 1) * depth] for a in range(3)]
        picked[tap * out_rows : (tap + 1) * out_rows] = jnp.concatenate(pieces, 1)


def outer_kernel(got_a, got_b, partial1, partial2, lower1, upper1, outer2, p_sel, out, low_taps, high_taps):
    planes, edge, breadth = got_a.shape
    chans = edge // EDGE
    k = lax.axis_index("yz")
    even, first, last = is_even("yz"), k == 0, k == lax.axis_size("yz") - 1
    for e in range(planes):
        low, high = from_sides(got_a[e], got_b[e], even, first, last)
        put_taps(low_taps.at[e], low, chans)
        put_taps(high_taps.at[e], high, chans)
    pairs = partial1.shape[1]
    width = lower1.shape[0] // 4
    lower, upper = lower1[: 3 * width], upper1[width:]
    rows = 3 * edge
    below, above = [], []
    lows = [mat(lower, two_cells(low_taps, j, 0, rows)) for j in range(pairs)]
    highs = [mat(upper, two_cells(high_taps, j, 0, rows)) for j in range(pairs)]
    for j in range(pairs):
        p = partial1[0, j]
        below.append(pool_first(jnp.concatenate([p[: 3 * width] + lows[j], p[3 * width :]], 0), j, pairs, first, False))
        p = partial1[1, j]
        above.append(pool_first(jnp.concatenate([p[:width], p[width:] + highs[j]], 0), j, pairs, False, last))
    width = outer2.shape[0] // 4
    sums = [mat(outer2[2 * y * width : 2 * (y + 1) * width], second_taps(p)) for y, p in enumerate((below, above))]
    halves = []
    for y in range(2):
        r = relu(partial2[2 * y * width : 2 * (y + 1) * width] + sums[y])
        t = r[:width] + r[width:]
        t = [t[:, 2 * x * breadth : (2 * x + 1) * breadth] + t[:, (2 * x + 1) * breadth : 2 * (x + 1) * breadth] for x in range(PLANES)]
        halves.append([((u + pltpu.roll(u, breadth - 2, 1)) * 0.125).astype(BF) for u in t])
    out[...] = mat(jnp.concatenate(halves[0] + halves[1], 1), p_sel[...]).astype(BF)


def lay(tiles, rows):
    even = is_even("yz")
    half = tiles[0].shape[1] // 2
    lane = iota((1, 2 * half), 1)
    tiles = [tiles[i] for i in [0, 1, 2, 3]]
    low, high = [], []
    for m in range(len(tiles) // 2):
        a, b = tiles[2 * m][rows].astype(F32), tiles[2 * m + 1][rows].astype(F32)
        first, second = jnp.where(even, a, b), jnp.where(even, b, a)
        low.append(jnp.where(lane < half, first, pltpu.roll(second, half, 1)))
        high.append(jnp.where(lane < half, pltpu.roll(first, half, 1), second))
    return low, high


def put_plane(dest, blocks):
    wide = blocks[0].shape[1]
    k = lax.axis_index("yz")
    for m, block in enumerate(blocks):
        dest[: block.shape[0], pl.ds(pl.multiple_of((lax.div(k, 2) ^ m) * wide, wide), wide)] = block.astype(BF)


def lay_kernel(*refs):
    tiles, (mate, far) = refs[:-2], refs[-2:]
    low, high = lay(tiles, slice(None))
    even = is_even("gx")
    put_plane(mate, [jnp.where(even, b, a) for a, b in zip(low, high)])
    put_plane(far, [jnp.where(even, a, b) for a, b in zip(low, high)])
    depth = mate.shape[0]
    far[depth:] = jnp.zeros((far.shape[0] - depth, far.shape[1]), BF)


def shift_taps(products, z):
    rows, cells = products.shape[0] // 9, products.shape[1]
    lane = iota((1, cells), 1)
    depth = lane & (z - 1)
    total = None
    for b in range(3):
        one = [products[(3 * b + c) * rows : (3 * b + c + 1) * rows] for c in range(3)]
        t = one[1] + jnp.where(depth == 0, 0.0, pltpu.roll(one[0], 1, 1))
        t = t + jnp.where(depth == z - 1, 0.0, pltpu.roll(one[2], cells - 1, 1))
        if b == 0:
            t = jnp.where(lane < z, 0.0, pltpu.roll(t, z, 1))
        if b == 2:
            t = jnp.where(lane >= cells - z, 0.0, pltpu.roll(t, cells - z, 1))
        total = t if total is None else total + t
    return total


def middle_kernel(z, mate, far, w3, beside_mate, beside_far, w_mate, w_far):
    depth = mate.shape[0]
    even = is_even("gx")
    a, b = mate[...], far[:depth]
    both = jnp.concatenate([jnp.where(even, b, a), jnp.where(even, a, b)], 0)
    w = w3[...].astype(BF)
    first, second = w[:, depth:], w[:, : 2 * depth]
    beside_mate[...] = shift_taps(mat(jnp.where(even, second, first), both), z)
    beside_far[...] = shift_taps(mat(jnp.where(even, first, second), both), z)
    w_mate[...] = jnp.where(even, w[:, 2 * depth :], w[:, :depth])
    w_far[...] = jnp.where(even, w[:, :depth], w[:, 2 * depth :])


def is_end():
    g = lax.axis_index("gx")
    return (g == 0) | (g == lax.axis_size("gx") - 1)


def write_planes(beside_mate, beside_far, out, block, sem):
    even = is_even("gx")
    a, b = relu(beside_mate), relu(beside_far)
    rows, cells = a.shape
    pair = jnp.concatenate([jnp.where(even, b, a), jnp.where(even, a, b)], 1)
    block[...] = pair.astype(BF).reshape(rows, 2, cells)
    copy = pltpu.make_async_copy(block, out, sem)
    copy.start()
    copy.wait()


def near_kernel(z, beside_mate, beside_far, w_mate, got_mate, out, ready, block, sem):
    ready[...] = beside_mate[...] + shift_taps(mat(w_mate[...], got_mate[...]), z)

    @pl.when(is_end())
    def _():
        write_planes(ready[...], beside_far[...], out, block, sem)


def far_kernel(z, got_far, w_far, ready, beside_far, _, out, block, sem):
    @pl.when(jnp.logical_not(is_end()))
    def _():
        part = beside_far[...] + shift_taps(mat(w_far[...], got_far[: w_far.shape[1]]), z)
        write_planes(ready[...], part, out, block, sem)


def per_device(volume, weight_one, weight_two, weight_three):
    gx, yz = lax.axis_size("gx"), lax.axis_size("yz")
    planes, chans, height, breadth = volume.shape
    rows = chans * height
    edge = EDGE * chans
    c2, c3 = weight_one.shape[0], weight_two.shape[0]

    planes_shape = ((HALO, chans, height, breadth), BF)
    send_mate, send_far = call(
        planes_kernel,
        [planes_shape, planes_shape],
        volume,
        scratch=[pltpu.SemaphoreType.DMA((2,))],
        hbm=(0,),
    )
    near, away = gx_pairs(gx, yz, False), gx_pairs(gx, yz, True)
    raw_mate = lax.ppermute(send_mate, ("gx", "yz"), near)
    raw_far = lax.ppermute(send_far, ("gx", "yz"), away)
    k1, k2 = 27 * chans, 27 * c2
    lower1, upper1, middle2, outer2, p_sel, swap, turned = call(
        weights_kernel,
        [
            ((4 * c2, k1), BF),
            ((4 * c2, k1), BF),
            ((4 * c3, 2 * k2 // 3), BF),
            ((4 * c3, 2 * k2 // 3), BF),
            ((4 * breadth, breadth), BF),
            ((rows, rows), BF),
            ((planes, rows, breadth), BF),
        ],
        volume,
        weight_one,
        weight_two,
        scratch=[
            pltpu.VMEM(volume.shape, BF),
            pltpu.VMEM(weight_one.shape, BF),
            pltpu.VMEM(weight_two.shape, BF),
            pltpu.SemaphoreType.DMA((3,)),
        ],
        hbm=(0, 1, 2),
        flops=2 * 64 * 864 * 1728,
    )
    wide = planes + 2 * HALO
    halo = ((HALO, rows, breadth), BF)
    send_a, send_b, got_far, got_mate = call(
        edge_kernel,
        [((wide, edge, breadth), BF), ((wide, edge, breadth), BF), halo, halo],
        raw_far,
        raw_mate,
        turned,
        swap,
        p_sel,
    )
    got_b = lax.ppermute(send_b, ("gx", "yz"), yz_pairs(gx, yz, True))
    got_a = lax.ppermute(send_a, ("gx", "yz"), yz_pairs(gx, yz, False))
    pairs = 2 * PLANES + 2
    out_rows = weight_three.shape[0] // yz
    partial1, partial2, picked = call(
        inner_kernel,
        [
            ((2, pairs, 4 * c2, 2 * breadth), F32),
            ((4 * c3, 2 * PLANES * breadth), F32),
            ((9 * out_rows, 3 * c3), F32),
        ],
        turned,
        got_mate,
        got_far,
        lower1,
        upper1,
        middle2,
        weight_three.T,
        scratch=[
            pltpu.VMEM((wide, 3 * rows, breadth), BF),
            pltpu.VMEM(weight_three.shape[::-1], BF),
            pltpu.SemaphoreType.DMA,
        ],
        hbm=(6,),
        flops=2 * 300_000_000,
    )
    (tile,) = call(
        outer_kernel,
        [((c3, breadth), BF)],
        got_a,
        got_b,
        partial1,
        partial2,
        lower1,
        upper1,
        outer2,
        p_sel,
        scratch=[pltpu.VMEM((wide, 3 * edge, breadth), BF), pltpu.VMEM((wide, 3 * edge, breadth), BF)],
        flops=2 * 400_000_000,
    )
    tiles = [tile] + [lax.ppermute(tile, "yz", [(i, i ^ d) for i in range(yz)]) for d in range(1, yz)]
    cells = yz * (height // 4) * (breadth // 4)
    z = breadth // 4
    mate, far = call(lay_kernel, [((c3, cells), BF), ((c3 + 16, cells), BF)], tiles[0], *[tiles[d] for d in [1, 2, 3]])
    got_far = lax.ppermute(far, ("gx", "yz"), away)
    got_mate = lax.ppermute(mate, ("gx", "yz"), near)
    shape = (out_rows, 2, cells)
    plane, weights = ((out_rows, cells), F32), ((9 * out_rows, c3), BF)
    beside_mate, beside_far, w_mate, w_far = call(
        functools.partial(middle_kernel, z),
        [plane, plane, weights, weights],
        mate,
        far,
        picked,
        flops=2 * 32 * 1152 * 512,
    )
    block = [pltpu.VMEM(shape, BF), pltpu.SemaphoreType.DMA]
    out, ready = call(
        functools.partial(near_kernel, z),
        [(shape, BF), plane],
        beside_mate,
        beside_far,
        w_mate,
        got_mate,
        scratch=block,
        hbm_out=True,
        free=True,
    )
    (out,) = call(
        functools.partial(far_kernel, z),
        [(shape, BF)],
        got_far,
        w_far,
        ready,
        beside_far,
        out,
        scratch=block,
        hbm=(4,),
        hbm_out=True,
        aliases={4: 0},
        flops=2 * 32 * 576 * 256,
    )
    return out


def solution(mesh):
    placed = (P("gx", None, "yz", None), P(), P(), P())
    return jax.shard_map(
        per_device, mesh=mesh, in_specs=placed, out_specs=P("yz", "gx", None), check_vma=False
    )
```

```python
import functools

import jax
import jax.numpy as jnp
from jax import lax
from jax.experimental import pallas as pl
from jax.experimental.pallas import tpu as pltpu
from jax.sharding import PartitionSpec as P

BF = jnp.bfloat16
F32 = jnp.float32
PLANES = 2
HALO = 2 * PLANES - 1
EDGE = 3


def mat(a, b):
    return jnp.dot(a, b, preferred_element_type=F32)


def relu(a):
    return jnp.maximum(a, 0.0)


def iota(shape, dim):
    return lax.broadcasted_iota(jnp.int32, shape, dim)


def call(body, outs, *args, scratch=(), flops=0, free=False, hbm=(), hbm_out=False, aliases={}):
    moved = 0 if free else sum(a.size * a.dtype.itemsize for a in args)
    args = [pltpu.with_memory_space_constraint(a, pltpu.HBM) if i in hbm else a for i, a in enumerate(args)]
    return pl.pallas_call(
        body,
        out_shape=[jax.ShapeDtypeStruct(s, d) for s, d in outs],
        in_specs=[pl.BlockSpec(memory_space=pltpu.HBM if i in hbm else pltpu.VMEM) for i in range(len(args))],
        out_specs=[pl.BlockSpec(memory_space=pltpu.HBM if hbm_out and i == 0 else pltpu.VMEM) for i in range(len(outs))],
        scratch_shapes=list(scratch),
        input_output_aliases=aliases,
        compiler_params=pltpu.CompilerParams(vmem_limit_bytes=40 * 1024 * 1024),
        cost_estimate=pl.CostEstimate(flops=flops, bytes_accessed=moved, transcendentals=0),
    )(*args)


def planes_kernel(volume, send_mate, send_far, sems):
    planes = volume.shape[0]
    even = is_even("gx")
    copies = []
    for i, (out, first) in enumerate(
        ((send_far, jnp.where(even, 0, planes - HALO)), (send_mate, jnp.where(even, planes - HALO, 0)))
    ):
        copies.append(pltpu.make_async_copy(volume.at[pl.ds(first, HALO)], out, sems.at[i]))
    for copy in copies:
        copy.start()
    for copy in copies:
        copy.wait()


def turn(swap, plane):
    rows, breadth = swap.shape[0], plane.shape[-1]
    return mat(swap, plane.reshape(rows, breadth)).astype(BF)


def yz_pairs(gx, yz, second):
    pairs = []
    for g in range(gx):
        for k in range(yz):
            if not second:
                pairs.append((g * yz + k, g * yz + (k ^ 1)))
            elif k in (0, yz - 1):
                pairs.append((g * yz + k, (g ^ 1) * yz + k))
            else:
                pairs.append((g * yz + k, g * yz + (k + 1 if k % 2 else k - 1)))
    return pairs


def gx_pairs(gx, yz, far):
    pairs = []
    for g in range(gx):
        for k in range(yz):
            if not far:
                pairs.append((g * yz + k, (g ^ 1) * yz + k))
            elif g in (0, gx - 1):
                pairs.append((g * yz + k, g * yz + (k ^ 1)))
            else:
                pairs.append((g * yz + k, (g + 1 if g % 2 else g - 1) * yz + k))
    return pairs


def is_even(axis):
    return lax.rem(lax.axis_index(axis), 2) == 0


def from_sides(mate, far, even, no_low, no_high):
    zero = jnp.zeros_like(mate)
    low = jnp.where(no_low, zero, jnp.where(even, far, mate))
    high = jnp.where(no_high, zero, jnp.where(even, mate, far))
    return low, high


def all_planes(turned, got_mate, got_far):
    g = lax.axis_index("gx")
    even, first, last = is_even("gx"), g == 0, g == lax.axis_size("gx") - 1
    sides = [from_sides(got_mate[x], got_far[x], even, first, last) for x in range(HALO)]
    return [low for low, _ in sides] + [turned[x] for x in range(turned.shape[0])] + [high for _, high in sides]


def edge_kernel(raw_far, raw_mate, turned, swap, _, send_a, send_b, got_far, got_mate):
    rows, breadth = got_far.shape[1:]
    beside = [raw[x].reshape(rows, breadth) for raw in (raw_far, raw_mate) for x in range(HALO)]
    beside = mat(swap[...], jnp.concatenate(beside, 1)).astype(BF)
    for x in range(HALO):
        got_far[x] = beside[:, x * breadth : (x + 1) * breadth]
        got_mate[x] = beside[:, (HALO + x) * breadth : (HALO + x + 1) * breadth]
    edge = send_a.shape[1]
    even = is_even("yz")
    for x, t in enumerate(all_planes(turned, got_mate, got_far)):
        low, high = t[:edge], t[t.shape[0] - edge :]
        send_a[x] = jnp.where(even, high, low)
        send_b[x] = jnp.where(even, low, high)


def weights_kernel(volume, w1_hbm, w2_hbm, lower1, upper1, middle2, outer2, p_sel, swap, turned, vol, w1, w2, sems):
    pairs = ((w1_hbm, w1), (w2_hbm, w2), (volume, vol))
    loads = [pltpu.make_async_copy(a, b, sems.at[i]) for i, (a, b) in enumerate(pairs)]
    for load in loads:
        load.start()

    rows, columns = p_sel.shape
    z = rows // 4
    r, c = iota(p_sel.shape, 0), iota(p_sel.shape, 1)
    hit = (r // (2 * z) == (c // (z // 4)) % 2) & ((r // z) % 2 == c // (z // 2))
    hit = hit & ((r & (z - 1)) == 4 * (c & (z // 4 - 1)))
    p_sel[...] = jnp.where(hit, 1.0, 0.0).astype(BF)

    planes, chans, height, breadth = vol.shape
    dest = iota(swap.shape, 0)
    source = (dest & (chans - 1)) * height + dest // chans
    swap[...] = (iota(swap.shape, 1) == source).astype(F32).astype(BF)

    for load in loads:
        load.wait()
    for x in range(planes):
        turned[x] = turn(swap[...], vol[x])
    for w, bands in (
        (w1, ((lower1, lambda y: (0, 1, 2)), (upper1, lambda y: (3, 4, 5)))),
        (w2, ((middle2, lambda y: (2, 3)), (outer2, lambda y: (0, 1) if y < 2 else (4, 5)))),
    ):
        out_rows, width = w.shape[0], w.shape[1] // 9
        taps = w[...].astype(F32)
        zero = jnp.zeros((out_rows, width), F32)
        for band, window in bands:
            for y in range(4):
                pieces = []
                for a in range(3):
                    for row in window(y):
                        first = (3 * a + row - y) * width
                        pieces.append(taps[:, first : first + width] if 0 <= row - y < 3 else zero)
                band[out_rows * y : out_rows * (y + 1)] = jnp.concatenate(pieces, 1).astype(BF)


def put_taps(dest, t, chans):
    breadth = t.shape[1]
    lane = iota((1, breadth), 1)
    wide = t.astype(F32)
    before = jnp.where(lane == 0, 0.0, pltpu.roll(wide, 1, 1)).astype(BF)
    after = jnp.where(lane == breadth - 1, 0.0, pltpu.roll(wide, breadth - 1, 1)).astype(BF)
    for y in range(t.shape[0] // chans):
        for tap, value in enumerate((before, t, after)):
            row = (3 * y + tap) * chans
            dest[row : row + chans] = value[y * chans : (y + 1) * chans]


def three(taps, e, first, rows):
    return jnp.concatenate([taps[e + a, first : first + rows] for a in range(3)], 0)


def two_cells(taps, j, first, rows):
    return jnp.concatenate([three(taps, 2 * j, first, rows), three(taps, 2 * j + 1, first, rows)], 1)


def pool_first(acc, j, pairs, no_low, no_high):
    g = lax.axis_index("gx")
    breadth = acc.shape[1] // 2
    width = acc.shape[0] // 4
    r = relu(acc)
    s = r[:, :breadth] + r[:, breadth:]
    halves = []
    for y, drop in enumerate((no_low, no_high)):
        t = s[2 * y * width : (2 * y + 1) * width] + s[(2 * y + 1) * width : (2 * y + 2) * width]
        t = (t + pltpu.roll(t, breadth - 1, 1)) * 0.125
        if j < PLANES - 1:
            drop = drop | (g == 0)
        if j > pairs - PLANES:
            drop = drop | (g == lax.axis_size("gx") - 1)
        halves.append(t if drop is False else jnp.where(drop, 0.0, t))
    return pooled_taps(jnp.concatenate(halves, 0))


def pooled_taps(t):
    breadth = t.shape[1]
    lane = iota((1, breadth), 1)
    before = jnp.where(lane < 2, 0.0, pltpu.roll(t, 2, 1)).astype(BF)
    after = jnp.where(lane >= breadth - 2, 0.0, pltpu.roll(t, breadth - 2, 1)).astype(BF)
    chans = t.shape[0] // 2
    rows = [slice(y * chans, (y + 1) * chans) for y in range(2)]
    return jnp.concatenate([u[r] for r in rows for u in (before, t.astype(BF), after)], 0)


def second_taps(planes):
    return jnp.concatenate([jnp.concatenate(planes[x : x + 3], 0) for x in range(len(planes) - 2)], 1)


def inner_kernel(
    turned, got_mate, got_far, lower1, upper1, middle2, w3_hbm, partial1, partial2, picked, taps, w3, sem
):
    load = pltpu.make_async_copy(w3_hbm, w3, sem)
    load.start()
    chans = lower1.shape[1] // 27
    for e, t in enumerate(all_planes(turned, got_mate, got_far)):
        put_taps(taps.at[e], t, chans)
    pairs = partial1.shape[1]
    width = lower1.shape[0] // 4
    lower, upper = lower1[: 3 * width], upper1[width:]
    step = 3 * chans
    pooled = []
    for j in range(pairs):
        partial1[0, j] = mat(upper, two_cells(taps, j, 0, 3 * step))
        partial1[1, j] = mat(lower, two_cells(taps, j, 5 * step, 3 * step))
        a = mat(lower, two_cells(taps, j, step, 3 * step))
        b = mat(upper, two_cells(taps, j, 4 * step, 3 * step))
        acc = jnp.concatenate([a[:width], a[width:] + b[: 2 * width], b[2 * width :]], 0)
        pooled.append(pool_first(acc, j, pairs, False, False))
    partial2[...] = mat(middle2[...], second_taps(pooled))
    load.wait()
    out_rows = picked.shape[0] // 9
    own = (out_rows, w3.shape[1])
    first = lax.axis_index("yz") * out_rows
    pick = (iota(own, 1) == iota(own, 0) + first).astype(F32).astype(BF)
    own3 = lax.dot_general(pick, w3[...], (((1,), (1,)), ((), ())), preferred_element_type=F32)
    depth = picked.shape[1] // 3
    for tap in range(9):
        pieces = [own3[:, (9 * a + tap) * depth : (9 * a + tap + 1) * depth] for a in range(3)]
        picked[tap * out_rows : (tap + 1) * out_rows] = jnp.concatenate(pieces, 1)


def outer_kernel(got_a, got_b, partial1, partial2, lower1, upper1, outer2, p_sel, out, low_taps, high_taps):
    planes, edge, breadth = got_a.shape
    chans = edge // EDGE
    k = lax.axis_index("yz")
    even, first, last = is_even("yz"), k == 0, k == lax.axis_size("yz") - 1
    for e in range(planes):
        low, high = from_sides(got_a[e], got_b[e], even, first, last)
        put_taps(low_taps.at[e], low, chans)
        put_taps(high_taps.at[e], high, chans)
    pairs = partial1.shape[1]
    width = lower1.shape[0] // 4
    lower, upper = lower1[: 3 * width], upper1[width:]
    rows = 3 * edge
    below, above = [], []
    lows = [mat(lower, two_cells(low_taps, j, 0, rows)) for j in range(pairs)]
    highs = [mat(upper, two_cells(high_taps, j, 0, rows)) for j in range(pairs)]
    for j in range(pairs):
        p = partial1[0, j]
        a = lows[j]
        a = jnp.concatenate([a[:width], p[: 2 * width] + a[width:], p[2 * width :]], 0)
        below.append(pool_first(a, j, pairs, first, False))
        p = partial1[1, j]
        b = highs[j]
        b = jnp.concatenate([p[:width], p[width:] + b[: 2 * width], b[2 * width :]], 0)
        above.append(pool_first(b, j, pairs, False, last))
    width = outer2.shape[0] // 4
    sums = [mat(outer2[2 * y * width : 2 * (y + 1) * width], second_taps(p)) for y, p in enumerate((below, above))]
    halves = []
    for y in range(2):
        r = relu(partial2[2 * y * width : 2 * (y + 1) * width] + sums[y])
        t = r[:width] + r[width:]
        t = [t[:, 2 * x * breadth : (2 * x + 1) * breadth] + t[:, (2 * x + 1) * breadth : 2 * (x + 1) * breadth] for x in range(PLANES)]
        halves.append([((u + pltpu.roll(u, breadth - 2, 1)) * 0.125).astype(BF) for u in t])
    out[...] = mat(jnp.concatenate(halves[0] + halves[1], 1), p_sel[...]).astype(BF)


def lay(tiles, rows):
    even = is_even("yz")
    half = tiles[0].shape[1] // 2
    lane = iota((1, 2 * half), 1)
    tiles = [tiles[i] for i in [0, 1, 2, 3]]
    low, high = [], []
    for m in range(len(tiles) // 2):
        a, b = tiles[2 * m][rows].astype(F32), tiles[2 * m + 1][rows].astype(F32)
        first, second = jnp.where(even, a, b), jnp.where(even, b, a)
        low.append(jnp.where(lane < half, first, pltpu.roll(second, half, 1)))
        high.append(jnp.where(lane < half, pltpu.roll(first, half, 1), second))
    return low, high


def put_plane(dest, blocks):
    wide = blocks[0].shape[1]
    k = lax.axis_index("yz")
    for m, block in enumerate(blocks):
        dest[: block.shape[0], pl.ds(pl.multiple_of((lax.div(k, 2) ^ m) * wide, wide), wide)] = block.astype(BF)


def lay_kernel(*refs):
    tiles, (mate, far) = refs[:-2], refs[-2:]
    low, high = lay(tiles, slice(None))
    even = is_even("gx")
    put_plane(mate, [jnp.where(even, b, a) for a, b in zip(low, high)])
    put_plane(far, [jnp.where(even, a, b) for a, b in zip(low, high)])
    depth = mate.shape[0]
    far[depth:] = jnp.zeros((far.shape[0] - depth, far.shape[1]), BF)


def shift_taps(products, z):
    rows, cells = products.shape[0] // 9, products.shape[1]
    lane = iota((1, cells), 1)
    depth = lane & (z - 1)
    total = None
    for b in range(3):
        one = [products[(3 * b + c) * rows : (3 * b + c + 1) * rows] for c in range(3)]
        t = one[1] + jnp.where(depth == 0, 0.0, pltpu.roll(one[0], 1, 1))
        t = t + jnp.where(depth == z - 1, 0.0, pltpu.roll(one[2], cells - 1, 1))
        if b == 0:
            t = jnp.where(lane < z, 0.0, pltpu.roll(t, z, 1))
        if b == 2:
            t = jnp.where(lane >= cells - z, 0.0, pltpu.roll(t, cells - z, 1))
        total = t if total is None else total + t
    return total


def middle_kernel(z, mate, far, w3, beside_mate, beside_far, w_mate, w_far):
    depth = mate.shape[0]
    even = is_even("gx")
    a, b = mate[...], far[:depth]
    both = jnp.concatenate([jnp.where(even, b, a), jnp.where(even, a, b)], 0)
    w = w3[...].astype(BF)
    first, second = w[:, depth:], w[:, : 2 * depth]
    beside_mate[...] = shift_taps(mat(jnp.where(even, second, first), both), z)
    beside_far[...] = shift_taps(mat(jnp.where(even, first, second), both), z)
    w_mate[...] = jnp.where(even, w[:, 2 * depth :], w[:, :depth])
    w_far[...] = jnp.where(even, w[:, :depth], w[:, 2 * depth :])


def is_end():
    g = lax.axis_index("gx")
    return (g == 0) | (g == lax.axis_size("gx") - 1)


def write_planes(beside_mate, beside_far, out, block, sem):
    even = is_even("gx")
    a, b = relu(beside_mate), relu(beside_far)
    rows, cells = a.shape
    pair = jnp.concatenate([jnp.where(even, b, a), jnp.where(even, a, b)], 1)
    block[...] = pair.astype(BF).reshape(rows, 2, cells)
    copy = pltpu.make_async_copy(block, out, sem)
    copy.start()
    copy.wait()


def near_kernel(z, beside_mate, beside_far, w_mate, got_mate, out, ready, block, sem):
    ready[...] = beside_mate[...] + shift_taps(mat(w_mate[...], got_mate[...]), z)

    @pl.when(is_end())
    def _():
        write_planes(ready[...], beside_far[...], out, block, sem)


def far_kernel(z, got_far, w_far, ready, beside_far, _, out, block, sem):
    @pl.when(jnp.logical_not(is_end()))
    def _():
        part = beside_far[...] + shift_taps(mat(w_far[...], got_far[: w_far.shape[1]]), z)
        write_planes(ready[...], part, out, block, sem)


def per_device(volume, weight_one, weight_two, weight_three):
    gx, yz = lax.axis_size("gx"), lax.axis_size("yz")
    planes, chans, height, breadth = volume.shape
    rows = chans * height
    edge = EDGE * chans
    c2, c3 = weight_one.shape[0], weight_two.shape[0]

    planes_shape = ((HALO, chans, height, breadth), BF)
    send_mate, send_far = call(
        planes_kernel,
        [planes_shape, planes_shape],
        volume,
        scratch=[pltpu.SemaphoreType.DMA((2,))],
        hbm=(0,),
    )
    near, away = gx_pairs(gx, yz, False), gx_pairs(gx, yz, True)
    raw_mate = lax.ppermute(send_mate, ("gx", "yz"), near)
    raw_far = lax.ppermute(send_far, ("gx", "yz"), away)
    k1, k2 = 27 * chans, 27 * c2
    lower1, upper1, middle2, outer2, p_sel, swap, turned = call(
        weights_kernel,
        [
            ((4 * c2, k1), BF),
            ((4 * c2, k1), BF),
            ((4 * c3, 2 * k2 // 3), BF),
            ((4 * c3, 2 * k2 // 3), BF),
            ((4 * breadth, breadth), BF),
            ((rows, rows), BF),
            ((planes, rows, breadth), BF),
        ],
        volume,
        weight_one,
        weight_two,
        scratch=[
            pltpu.VMEM(volume.shape, BF),
            pltpu.VMEM(weight_one.shape, BF),
            pltpu.VMEM(weight_two.shape, BF),
            pltpu.SemaphoreType.DMA((3,)),
        ],
        hbm=(0, 1, 2),
        flops=2 * 64 * 864 * 1728,
    )
    wide = planes + 2 * HALO
    halo = ((HALO, rows, breadth), BF)
    send_a, send_b, got_far, got_mate = call(
        edge_kernel,
        [((wide, edge, breadth), BF), ((wide, edge, breadth), BF), halo, halo],
        raw_far,
        raw_mate,
        turned,
        swap,
        p_sel,
    )
    got_b = lax.ppermute(send_b, ("gx", "yz"), yz_pairs(gx, yz, True))
    got_a = lax.ppermute(send_a, ("gx", "yz"), yz_pairs(gx, yz, False))
    pairs = 2 * PLANES + 2
    out_rows = weight_three.shape[0] // yz
    partial1, partial2, picked = call(
        inner_kernel,
        [
            ((2, pairs, 3 * c2, 2 * breadth), F32),
            ((4 * c3, 2 * PLANES * breadth), F32),
            ((9 * out_rows, 3 * c3), F32),
        ],
        turned,
        got_mate,
        got_far,
        lower1,
        upper1,
        middle2,
        weight_three.T,
        scratch=[
            pltpu.VMEM((wide, 3 * rows, breadth), BF),
            pltpu.VMEM(weight_three.shape[::-1], BF),
            pltpu.SemaphoreType.DMA,
        ],
        hbm=(6,),
        flops=2 * 300_000_000,
    )
    (tile,) = call(
        outer_kernel,
        [((c3, breadth), BF)],
        got_a,
        got_b,
        partial1,
        partial2,
        lower1,
        upper1,
        outer2,
        p_sel,
        scratch=[pltpu.VMEM((wide, 3 * edge, breadth), BF), pltpu.VMEM((wide, 3 * edge, breadth), BF)],
        flops=2 * 400_000_000,
    )
    tiles = [tile] + [lax.ppermute(tile, "yz", [(i, i ^ d) for i in range(yz)]) for d in range(1, yz)]
    cells = yz * (height // 4) * (breadth // 4)
    z = breadth // 4
    mate, far = call(lay_kernel, [((c3, cells), BF), ((c3 + 16, cells), BF)], tiles[0], *[tiles[d] for d in [1, 2, 3]])
    got_far = lax.ppermute(far, ("gx", "yz"), away)
    got_mate = lax.ppermute(mate, ("gx", "yz"), near)
    shape = (out_rows, 2, cells)
    plane, weights = ((out_rows, cells), F32), ((9 * out_rows, c3), BF)
    beside_mate, beside_far, w_mate, w_far = call(
        functools.partial(middle_kernel, z),
        [plane, plane, weights, weights],
        mate,
        far,
        picked,
        flops=2 * 32 * 1152 * 512,
    )
    block = [pltpu.VMEM(shape, BF), pltpu.SemaphoreType.DMA]
    out, ready = call(
        functools.partial(near_kernel, z),
        [(shape, BF), plane],
        beside_mate,
        beside_far,
        w_mate,
        got_mate,
        scratch=block,
        hbm_out=True,
        free=True,
    )
    (out,) = call(
        functools.partial(far_kernel, z),
        [(shape, BF)],
        got_far,
        w_far,
        ready,
        beside_far,
        out,
        scratch=block,
        hbm=(4,),
        hbm_out=True,
        aliases={4: 0},
        flops=2 * 32 * 576 * 256,
    )
    return out


def solution(mesh):
    placed = (P("gx", None, "yz", None), P(), P(), P())
    return jax.shard_map(
        per_device, mesh=mesh, in_specs=placed, out_specs=P("yz", "gx", None), check_vma=False
    )
```
